32 devices in a mesh: member: 4 (over y, x), section: 2 (over core), dp: 4 (over z).
Axes of the slice: x: 2, y: 2, z: 4, core: 2. Of those that a mesh axis runs over, the one named last changes fastest.
Arguments:
- tokens: int32 [16, 2, 512], P(('member', 'dp')), parts along dimension 0, may hold values from 0 to 50303
- margins: int32 [16], P(('member', 'dp')), parts along dimension 0, may hold values from 1 to 6, as said below
- tie_flags: int32 [16], P(('member', 'dp')), parts along dimension 0, may hold values 0 or 1
- embedding: float32 [3072, 50304], P(('member', 'section', 'dp')), parts along dimension 0, may hold values from -1.2 to 1.2
- embed_moment: float32 [3072, 50304], P(('member', 'section', 'dp')), parts along dimension 0, may hold values from -3.02732e-05 to 3.02732e-05
- embed_second: float32 [3072, 50304], P(('member', 'section', 'dp')), parts along dimension 0, may hold values from 4.7338158e-12 to 1.8935263e-11
- layer_blocks: float32 [8, 48, 384, 384], P(('member', 'section'), 'dp'), parts along dimension 0, may hold values from -0.21875 to 0.21875
- left_stats: float32 [8, 48, 384, 384], P(('member', 'section'), 'dp'), parts along dimension 0, may hold values from 0 to 1.56809423e-06, as said below
- right_stats: float32 [8, 48, 384, 384], P(('member', 'section'), 'dp'), parts along dimension 0, may hold values from 0 to 1.56809423e-06, as said below
- left_root: float32 [8, 48, 384, 384], P(('member', 'section'), 'dp'), parts along dimension 0, may hold values from -40.211745 to 60.31762, as said below
- right_root: float32 [8, 48, 384, 384], P(('member', 'section'), 'dp'), parts along dimension 0, may hold values from -40.211745 to 60.31762, as said below
- layer_vectors: float32 [8, 9984], P(('member', 'section'), 'dp'), parts along dimension 0, may hold values from -0.35 to 1.9
- vector_moment: float32 [8, 9984], P(('member', 'section'), 'dp'), parts along dimension 0, may hold values from -0.00030273202 to 0.00030273202
- vector_second: float32 [8, 9984], P(('member', 'section'), 'dp'), parts along dimension 0, may hold values from 4.7338156e-10 to 1.8935262e-09
- closing_vectors: float32 [9216], P(('member', 'section', 'dp')), parts along dimension 0, may hold values from -1.46969385 to 2
- final_moment: float32 [9216], P(('member', 'section', 'dp')), parts along dimension 0, may hold values from -0.00030273202 to 0.00030273202
- final_second: float32 [9216], P(('member', 'section', 'dp')), parts along dimension 0, may hold values from 4.7338156e-10 to 1.8935262e-09
Outputs:
- loss_sum: float32 [4], P('member'), parts along dimension 0
- grad_norm: float32 [4], P('member'), parts along dimension 0
- block_grads: float32 [8, 48, 384, 384], P(('member', 'section'), 'dp'), parts along dimension 0
- new_blocks: float32 [8, 48, 384, 384], P(('member', 'section'), 'dp'), parts along dimension 0
- new_left: float32 [8, 48, 384, 384], P(('member', 'section'), 'dp'), parts along dimension 0
- new_right: float32 [8, 48, 384, 384], P(('member', 'section'), 'dp'), parts along dimension 0
- vector_moments: float32 [8, 9984], P(('member', 'section'), 'dp'), parts along dimension 0
- vector_seconds: float32 [8, 9984], P(('member', 'section'), 'dp'), parts along dimension 0
- new_vectors: float32 [8, 9984], P(('member', 'section'), 'dp'), parts along dimension 0
- final_moments: float32 [9216], P(('member', 'section', 'dp')), parts along dimension 0
- final_seconds: float32 [9216], P(('member', 'section', 'dp')), parts along dimension 0
- new_final: float32 [9216], P(('member', 'section', 'dp')), parts along dimension 0
- embed_moments: float32 [3072, 50304], P(('member', 'section', 'dp')), parts along dimension 0
- embed_seconds: float32 [3072, 50304], P(('member', 'section', 'dp')), parts along dimension 0
- new_embedding: float32 [3072, 50304], P(('member', 'section', 'dp')), parts along dimension 0
The draws below stay inside these ranges and needn't reach their ends.
There are 4 independent parts, one for each index of `member`. The reference program is written for one: setup_inputs(seed, part) draws one part's arguments, and reference() takes and returns one part's arrays. A program takes and returns all parts, laid end to end along the dimension named above; each array names one. Nothing has to cross between parts.
Inputs may be any that keep to these rules, and one draw needn't show every extreme that they name: margins never fall by more than 1 from one pair to the next. `left_stats`: diagonal, positive on the diagonal. `right_stats`: diagonal, positive on the diagonal. `left_root`: symmetric. `right_root`: symmetric.
All inputs are finite; a program needn't handle non-finite values. No bound on the sum of `tie_flags` on one device may be relied on, other than what follows from the above.
Results may differ from the reference program's by a relative error of at most 0.011.
The reference program's roundings to bfloat16 on the way count: a program that leaves them out, or rounds other values in their place, can miss the bound.
Values may be sent and summed in bfloat16 or wider, within the bound.
No kernel may reach another device: no remote copies, remote signals or barrier semaphores. Data moves between devices by JAX's collectives and lax.ppermute only.
A program may use at most 512 MiB of HBM per device.

```python
import math
import jax
import jax.numpy as jnp
import numpy as np
from jax import lax

D = 768
HEADS = 12
HEAD = 64
ROT = 16
FF = 3072
VOCAB = 50304
LENGTH = 512
BLOCK = 384
STEP = 10
PAIRS = 4
NBLOCKS = 48
VEC = 9984
PARAMS = 52811520


def draw_margins(key, part):
    key = jax.random.fold_in(key, 11)
    index = jnp.arange(PAIRS)
    extra = jax.random.randint(key, (PAIRS,), 0, 2)
    extra = jnp.where(index == 0, 0, jnp.where(index == PAIRS - 1, 1, extra))
    return (1 + 6 * index // PAIRS + extra).astype(jnp.int32)


def draw_layer_vectors(key, part):
    key = jax.random.fold_in(key, 12)
    first, second = jax.random.split(key)
    index = jnp.arange(VEC)
    column = (index % D).astype(jnp.float32)
    rising = 0.5 + column / D
    spread = jnp.exp(jax.random.uniform(first, (2, VEC), minval=-0.22, maxval=0.22))
    noise = jax.random.uniform(second, (2, VEC), minval=-0.35, maxval=0.35)
    is_gain = (index < D) | (index >= 2 * D) & (index < 3 * D)
    return jnp.where(is_gain[None, :], rising[None, :] * spread, noise).astype(jnp.float32)


def draw_closing_vectors(key, part):
    key = jax.random.fold_in(key, 13)
    first, second, third = jax.random.split(key, 3)
    gain = jnp.exp(jax.random.uniform(first, (D,), minval=-0.69, maxval=0.69))
    shift = jax.random.uniform(second, (D,), minval=-0.35, maxval=0.35)
    reach = 1.7 * math.sqrt(LENGTH / D)
    head = jax.random.uniform(third, (D,), minval=-reach, maxval=reach)
    return jnp.concatenate([gain, shift, head]).astype(jnp.float32)


def stats_level():
    return 0.0526 * BLOCK / PARAMS


def identity_matrix():
    return (jnp.arange(BLOCK)[:, None] == jnp.arange(BLOCK)[None, :]).astype(jnp.float32)


def diagonal_stats(key):
    factor = jnp.exp(jax.random.uniform(key, (2, NBLOCKS, BLOCK), minval=0.0, maxval=math.log(4.0)))
    return (stats_level() * factor[..., None] * identity_matrix()).astype(jnp.float32)


def root_matrix(key):
    level = stats_level() ** (-0.25)
    first, second = jax.random.split(key)
    diagonal = level * jnp.exp(jax.random.uniform(first, (2, NBLOCKS, BLOCK), minval=-0.35, maxval=0.35))
    beside = jax.random.uniform(second, (2, NBLOCKS, BLOCK, BLOCK), minval=-1.0, maxval=1.0) * (0.5 * level / math.sqrt(BLOCK))
    beside = 0.5 * (beside + jnp.swapaxes(beside, -1, -2))
    eye_matrix = identity_matrix()
    return (beside * (1.0 - eye_matrix) + diagonal[..., None] * eye_matrix).astype(jnp.float32)


def draw_left_stats(key, part):
    key = jax.random.fold_in(key, 21)
    return diagonal_stats(key)


def draw_right_stats(key, part):
    key = jax.random.fold_in(key, 22)
    return diagonal_stats(key)


def draw_left_root(key, part):
    key = jax.random.fold_in(key, 23)
    return root_matrix(key)


def draw_right_root(key, part):
    key = jax.random.fold_in(key, 24)
    return root_matrix(key)


def with_ends(entries, key, smallest, top_value):
    extent = entries.shape
    index_at = [jax.random.randint(jax.random.fold_in(key, axis), (), 0, extent[axis]) for axis in range(len(extent))]
    entries = entries.at[tuple(index_at)].set(smallest)
    longest = extent.index(max(extent))
    index_at[longest] = (index_at[longest] + 1) % extent[longest]
    return entries.at[tuple(index_at)].set(top_value)


def block_levels(own_key, extent, shards, smallest, top_value):
    def one(position, blocks):
        draws = jax.random.uniform(jax.random.fold_in(jax.random.fold_in(own_key, 6), position), (blocks,), jnp.float32, smallest / len(shards), top_value / len(shards))
        return jnp.repeat(jnp.exp(draws), extent[position] // blocks).reshape((-1,) + (1,) * (len(extent) - position - 1))

    level = one(*shards[0])
    for cut in shards[1:]:
        level = level * one(*cut)
    return level


def rank_table(number_of, skew):
    weights = [(1 << 20) // math.isqrt(rank ** skew) + 1 for rank in range(1, number_of + 1)]
    deviation = 1 + sum(weights) // (1 << 30)
    return np.cumsum(np.array([max(1, weight // deviation) for weight in weights]))


def skewed_ids(own_key, dims, count, lean):
    listing = rank_table(count, lean)
    ticket = jax.random.randint(jax.random.fold_in(own_key, 1), dims, 0, int(listing[count - 1]))
    grade = jnp.searchsorted(jnp.asarray(listing, jnp.int32), ticket, side="right")
    return jax.random.permutation(jax.random.fold_in(own_key, 2), count)[grade].astype(jnp.int32)


def gaussian(own_key, dims, scale, limit, cuts=(), kind=jnp.bfloat16):
    level = block_levels(own_key, dims, cuts, -0.22, 0.18) if cuts else 1.0
    drawn = jax.random.normal(own_key, dims, jnp.float32) * scale * level
    return jnp.minimum(jnp.maximum(drawn, -limit), limit).astype(kind)


def setup_inputs(seed: int = 0, part: int = 0) -> dict:
    seeds = jax.random.split(jax.random.key(seed), 18)
    part_splits = jax.random.split(jax.random.fold_in(seeds[17], part), 18)
    return {
        "tokens": with_ends(skewed_ids(part_splits[0], (PAIRS, 2, LENGTH), VOCAB, 2), jax.random.fold_in(part_splits[0], 3), 0, VOCAB - 1).astype(jnp.int32),
        "margins": draw_margins(jax.random.fold_in(jax.random.fold_in(seeds[17], part), 71), part),
        "tie_flags": with_ends((jax.random.randint(part_splits[2], (PAIRS,), 0, 4) < 1).astype(jnp.int32), jax.random.fold_in(part_splits[2], 1), 0, 1),
        "embedding": gaussian(part_splits[3], (D, VOCAB), 0.2, 1.2, ((0, 8),), jnp.float32),
        "embed_moment": gaussian(part_splits[4], (D, VOCAB), (0.055 * PARAMS ** -0.5), 3.027320053661242e-05, ((0, 8),), jnp.float32),
        "embed_second": jnp.clip(jnp.exp(math.log(1.8935263079722375e-11) - 1.3862944 * jax.random.uniform(part_splits[5], (D, VOCAB), jnp.float32) ** block_levels(part_splits[5], (D, VOCAB), ((0, 8),), -0.2, 0.2)), 4.733815769930594e-12, 1.8935263079722375e-11),
        "layer_blocks": gaussian(part_splits[6], (2, NBLOCKS, BLOCK, BLOCK), D ** -0.5, 0.21875, ((0, 2), (1, 4)), jnp.float32),
        "left_stats": draw_left_stats(jax.random.fold_in(jax.random.fold_in(seeds[17], part), 71), part),
        "right_stats": draw_right_stats(jax.random.fold_in(jax.random.fold_in(seeds[17], part), 71), part),
        "left_root": draw_left_root(jax.random.fold_in(jax.random.fold_in(seeds[17], part), 71), part),
        "right_root": draw_right_root(jax.random.fold_in(jax.random.fold_in(seeds[17], part), 71), part),
        "layer_vectors": draw_layer_vectors(jax.random.fold_in(jax.random.fold_in(seeds[17], part), 71), part),
        "vector_moment": gaussian(part_splits[12], (2, VEC), (0.55 * PARAMS ** -0.5), 0.00030273202, ((0, 2), (1, 4)), jnp.float32),
        "vector_second": jnp.clip(jnp.exp(math.log(1.8935262247055107e-09) - 1.3862944 * jax.random.uniform(part_splits[13], (2, VEC), jnp.float32) ** block_levels(part_splits[13], (2, VEC), ((0, 2), (1, 4)), -0.2, 0.2)), 4.733815561763777e-10, 1.8935262247055107e-09),
        "closing_vectors": draw_closing_vectors(jax.random.fold_in(jax.random.fold_in(seeds[17], part), 71), part),
        "final_moment": gaussian(part_splits[15], (3 * D,), (0.55 * PARAMS ** -0.5), 0.00030273202, ((0, 8),), jnp.float32),
        "final_second": jnp.clip(jnp.exp(math.log(1.8935262247055107e-09) - 1.3862944 * jax.random.uniform(part_splits[16], (3 * D,), jnp.float32) ** block_levels(part_splits[16], (3 * D,), ((0, 8),), -0.2, 0.2)), 4.733815561763777e-10, 1.8935262247055107e-09),
    }


highest = lax.Precision.HIGHEST
norm_eps = 1e-05
beta_first = 0.9
beta_second = 0.999
adam_eps = 1e-08
clip_limit = 1.0
embed_rate = 0.2
embed_decay = 0.01
vector_rate = 0.5
shampoo_rate = 0.1
stats_decay = 0.95
rope_base = 10000.0

@jax.custom_vjp
def low(v):
    return lax.optimization_barrier(v.astype(jnp.bfloat16)).astype(jnp.float32)

@jax.custom_vjp
def low_back(v):
    return v

def low_keep(v):
    return (low(v), None)

def low_pass(kept, grad):
    return (grad,)

def back_keep(v):
    return (v, None)

def back_low(kept, grad):
    return (low(grad),)
low.defvjp(low_keep, low_pass)
low_back.defvjp(back_keep, back_low)

def layer_norm(values, gain, shift):
    centred = values - lax.optimization_barrier(jnp.mean(values, axis=-1, keepdims=True))
    spread = lax.optimization_barrier(jnp.mean(centred * centred, axis=-1, keepdims=True))
    return centred * lax.rsqrt(spread + norm_eps) * gain + shift

def rope_tables(positions):
    half_rot = ROT // 2
    lanes = jnp.arange(HEAD)
    index = jnp.where(lanes < half_rot, lanes, lanes - half_rot).astype(jnp.float32)
    inverse_matrix = rope_base ** (-2.0 * index / ROT)
    angles = positions[:, None].astype(jnp.float32) * inverse_matrix[None, :]
    inside = lanes < ROT
    cosine = jnp.where(inside, jnp.cos(angles), 1.0)
    sine = jnp.where(inside, jnp.sin(angles), 0.0)
    return (cosine[:, None, :], sine[:, None, :])

def rotate(values, cosine, sine):
    half_rot = ROT // 2
    turned = jnp.concatenate([-values[..., half_rot:ROT], values[..., :half_rot], values[..., ROT:]], axis=-1)
    return values * cosine + turned * sine

def assemble(blocks):
    tiles_d = D // BLOCK
    tiles_f = FF // BLOCK

    def build(start, row_tiles, col_tiles):
        piece = blocks[start:start + row_tiles * col_tiles].reshape(row_tiles, col_tiles, BLOCK, BLOCK)
        return piece.transpose(0, 2, 1, 3).reshape(row_tiles * BLOCK, col_tiles * BLOCK)
    first = tiles_d * 3 * tiles_d
    second = first + tiles_d * tiles_d
    third = second + tiles_d * tiles_f
    return (build(0, tiles_d, 3 * tiles_d), build(first, tiles_d, tiles_d), build(second, tiles_d, tiles_f), build(third, tiles_f, tiles_d))

def split_vectors(vectors):
    widths = [D, D, D, D, 3 * D, D, FF, D]
    parts = []
    start = 0
    for count in widths:
        parts.append(vectors[start:start + count])
        start = start + count
    return parts

def layer(inputs, mats, vectors):
    qkv_w, out_w, up_w, down_w = mats
    gain_one, shift_one, gain_two, shift_two, qkv_bias, out_bias, up_bias, down_bias = split_vectors(vectors)
    positions = jnp.arange(LENGTH)
    cosine, sine = rope_tables(positions)
    scale_factor = 1.0 / math.sqrt(HEAD)
    normed = low(layer_norm(inputs, gain_one, shift_one))
    projected = low_back(jnp.dot(normed, qkv_w, precision=highest) + qkv_bias)
    queries = low(rotate(projected[:, :D].reshape(LENGTH, HEADS, HEAD), cosine, sine))
    keys = low(rotate(projected[:, D:2 * D].reshape(LENGTH, HEADS, HEAD), cosine, sine))
    values = low(projected[:, 2 * D:].reshape(LENGTH, HEADS, HEAD))
    scores = low_back(jnp.einsum('qhd,khd->hqk', queries, keys, precision=highest) * scale_factor)
    allowed = positions[None, :] <= positions[:, None]
    scores = jnp.where(allowed[None], scores, -1e+30)
    peak = lax.optimization_barrier(jnp.max(scores, axis=-1, keepdims=True))
    expo = jnp.exp(scores - peak)
    probs = low(expo / lax.optimization_barrier(jnp.sum(expo, axis=-1, keepdims=True)))
    attended = low(low_back(jnp.einsum('hqk,khd->qhd', probs, values, precision=highest))).reshape(LENGTH, D)
    attn_out = jnp.dot(attended, out_w, precision=highest) + out_bias
    second = low(layer_norm(inputs, gain_two, shift_two))
    pre_act = low_back(jnp.dot(second, up_w, precision=highest) + up_bias)
    activated = low(jax.nn.gelu(pre_act, approximate=False))
    branch = jnp.dot(activated, down_w, precision=highest) + down_bias
    return inputs + low_back(attn_out + branch)

def sequence_reward(token_row, table, mats_all, vectors_all, final_all):
    hidden_state = jnp.take(table, token_row, axis=1).T
    hidden_state = layer(hidden_state, mats_all[0], vectors_all[0])
    hidden_state = low(low_back(hidden_state))
    hidden_state = layer(hidden_state, mats_all[1], vectors_all[1])
    normed = low(layer_norm(hidden_state, final_all[:D], final_all[D:2 * D]))
    return jnp.mean(jnp.dot(normed, final_all[2 * D:], precision=highest))

def total_loss(table, blocks, vectors, final_all, tokens, margins, tie_flags):
    table = low(table)
    blocks = low(blocks)
    vectors = low(vectors)
    final_all = low(final_all)
    mats_all = [assemble(blocks[0]), assemble(blocks[1])]

    def one_row(token_row):
        return sequence_reward(token_row, table, mats_all, vectors, final_all)
    rewards = lax.map(jax.checkpoint(one_row), tokens.reshape(-1, LENGTH)).reshape(-1, 2)
    gap = rewards[:, 0] - rewards[:, 1]
    half_margin = 0.5 * margins.astype(jnp.float32)
    tie = tie_flags.astype(jnp.float32)
    losses = (1.0 - tie) * jax.nn.softplus(half_margin - gap) + tie * 0.5 * (jax.nn.softplus(gap) + jax.nn.softplus(-gap))
    return jnp.sum(losses)

def adam_step(weight, moment, second, grad, rate, decay):
    moment_new = beta_first * moment + (1.0 - beta_first) * grad
    second_new = beta_second * second + (1.0 - beta_second) * grad * grad
    corrected = moment_new / (1.0 - beta_first ** STEP)
    scaled = jnp.sqrt(second_new / (1.0 - beta_second ** STEP)) + adam_eps
    return (moment_new, second_new, weight - rate * (corrected / scaled + decay * weight))

def reference(tokens, margins, tie_flags, embedding, embed_moment, embed_second, layer_blocks, left_stats, right_stats, left_root, right_root, layer_vectors, vector_moment, vector_second, closing_vectors, final_moment, final_second):

    def loss_of(table, blocks, vectors, final_all):
        return total_loss(table, blocks, vectors, final_all, tokens, margins, tie_flags)
    loss_value, back = jax.vjp(loss_of, embedding, layer_blocks, layer_vectors, closing_vectors)
    embed_grad, block_grad, vector_grad, final_grad = back(jnp.ones((), jnp.float32))
    squares = jnp.sum(embed_grad * embed_grad) + jnp.sum(block_grad * block_grad) + jnp.sum(vector_grad * vector_grad) + jnp.sum(final_grad * final_grad)
    norm_value = jnp.sqrt(squares)
    factor = clip_limit / jnp.maximum(norm_value, clip_limit)
    embed_grad = embed_grad * factor
    block_grad = block_grad * factor
    vector_grad = vector_grad * factor
    final_grad = final_grad * factor
    new_left = stats_decay * left_stats + (1.0 - stats_decay) * jnp.einsum('...ij,...kj->...ik', block_grad, block_grad, precision=highest)
    new_right = stats_decay * right_stats + (1.0 - stats_decay) * jnp.einsum('...ji,...jk->...ik', block_grad, block_grad, precision=highest)
    inner = jnp.einsum('...ij,...jk->...ik', block_grad, right_root, precision=highest)
    direction = jnp.einsum('...ij,...jk->...ik', left_root, inner, precision=highest)
    new_blocks = layer_blocks - shampoo_rate * direction
    vector_m, vector_v, vector_w = adam_step(layer_vectors, vector_moment, vector_second, vector_grad, vector_rate, 0.0)
    final_m, final_v, final_w = adam_step(closing_vectors, final_moment, final_second, final_grad, vector_rate, 0.0)
    embed_m, embed_v, embed_w = adam_step(embedding, embed_moment, embed_second, embed_grad, embed_rate, embed_decay)
    return (loss_value.reshape(1), norm_value.reshape(1), block_grad, new_blocks, new_left, new_right, vector_m, vector_v, vector_w, final_m, final_v, final_w, embed_m, embed_v, embed_w)
```

```python
import functools
import math

import jax
import jax.numpy as jnp
from jax import lax
from jax.experimental import pallas as pl
from jax.experimental.pallas import tpu as pltpu
from jax.sharding import PartitionSpec as P

D = 768
HEADS = 12
HEAD = 64
ROT = 16
FF = 3072
STEP = 10
TILE = 384
PAIR = 2 * HEAD
QROWS = 256
CHUNK = 768

norm_eps = 1e-05
beta_first = 0.9
beta_second = 0.999
adam_eps = 1e-08
clip_limit = 1.0
embed_rate = 0.2
embed_decay = 0.01
vector_rate = 0.5
shampoo_rate = 0.1
stats_decay = 0.95
rope_base = 10000.0

f32 = jnp.float32
bf16 = jnp.bfloat16
VMEM_LIMIT = 60 * 2**20

COL_A, COL_O, COL_B, COL_H = 0, D, 2 * D, 3 * D
COL_QKV = 3 * D + FF
COL_GP = COL_QKV + 3 * D
COL_X = COL_GP + FF
KEPT = COL_X + D
COL_DP, COL_G, COL_DH = 0, 3 * D, 4 * D
GRADS = 4 * D + FF

V_G1, V_C1, V_G2, V_C2, V_QKV, V_O = 0, D, 2 * D, 3 * D, 4 * D, 7 * D
V_B1, V_B2, V_END = 8 * D, 8 * D + FF, 9 * D + FF


def block_places():
    places = []
    for matrix, (rows, cols) in enumerate(((D, 3 * D), (D, D), (D, FF), (FF, D))):
        for row in range(rows // TILE):
            for col in range(cols // TILE):
                places.append((matrix, row, col))
    return places


PLACES = block_places()


def nt(a, b):
    return lax.dot_general(a, b, (((1,), (1,)), ((), ())), preferred_element_type=f32)


def tn(a, b):
    return lax.dot_general(a, b, (((0,), (0,)), ((), ())), preferred_element_type=f32)


def nn(a, b):
    return lax.dot_general(a, b, (((1,), (0,)), ((), ())), preferred_element_type=f32)


def normalized(x):
    mean = jnp.mean(x, axis=-1, keepdims=True)
    centred = x - mean
    spread = jnp.mean(centred * centred, axis=-1, keepdims=True)
    scale = lax.rsqrt(spread + norm_eps)
    return centred * scale, scale


def norm_back(grad, gain, hat, scale):
    inner = grad * gain
    first = jnp.mean(inner, axis=-1, keepdims=True)
    second = jnp.mean(inner * hat, axis=-1, keepdims=True)
    return scale * (inner - first - hat * second)


def gelu_both(h):
    expo = jnp.exp(-0.5 * h * h)
    t = 1.0 / (1.0 + (0.3275911 * math.sqrt(0.5)) * jnp.abs(h))
    poly = 0.5 * 1.061405429
    for coef in (-1.453152027, 1.421413741, -0.284496736, 0.254829592):
        poly = poly * t + 0.5 * coef
    tail = poly * t * expo
    cdf = jnp.where(h >= 0.0, 1.0 - tail, tail)
    return h * cdf, cdf + h * expo * (1.0 / math.sqrt(2.0 * math.pi))


def head_masks(value):
    lane = lax.broadcasted_iota(jnp.int32, (1, PAIR), 1)
    return [
        jnp.where(lane < HEAD, value, 0.0).astype(bf16),
        jnp.where(lane < HEAD, 0.0, value).astype(bf16),
    ]


def weight_copies(shards, mats, sems):
    per = shards[0].shape[0]
    copies = []
    for index, (matrix, row, col) in enumerate(PLACES):
        copies.append(
            (
                matrix,
                pltpu.make_async_copy(
                    shards[index // per].at[index % per],
                    mats[matrix].at[pl.ds(row * TILE, TILE), pl.ds(col * TILE, TILE)],
                    sems.at[index],
                ),
            )
        )
    return copies


def wait_for(copies, matrix):
    for which, copy in copies:
        if which == matrix:
            copy.wait()


def forward_kernel(shard_count, first, *refs):
    slot_ref, x_ref, vec_ref, fin_ref, cos_ref, sa_ref, sb_ref = refs[:7]
    shards = refs[7 : 7 + shard_count]
    rest = refs[7 + shard_count + (0 if first else 3) :]
    xb_ref, red_ref, kept_out, xo_out, lse_out = rest[:5]
    wqkv, wo, w1, w2, kept, xo, lse, wsem, osem = rest[5:]
    mats = (wqkv, wo, w1, w2)
    length = x_ref.shape[0]
    slot = slot_ref[0]
    copies = weight_copies(shards, mats, wsem)
    for _, copy in copies:
        copy.start()

    stores = []

    def store(index, start, width):
        copy = pltpu.make_async_copy(
            kept.at[:, pl.ds(start, width)],
            kept_out.at[slot, :, pl.ds(start, width)],
            osem.at[index],
        )
        copy.start()
        stores.append(copy)

    hat, _ = normalized(x_ref[...].astype(f32))
    kept[:, COL_X : COL_X + D] = x_ref[...]
    kept[:, COL_A : COL_A + D] = (hat * vec_ref[:, V_G1 : V_G1 + D] + vec_ref[:, V_C1 : V_C1 + D]).astype(bf16)
    kept[:, COL_B : COL_B + D] = (hat * vec_ref[:, V_G2 : V_G2 + D] + vec_ref[:, V_C2 : V_C2 + D]).astype(bf16)
    wait_for(copies, 0)
    for part in range(3):
        at = part * D
        proj = nn(kept[:, COL_A : COL_A + D], wqkv[:, at : at + D])
        proj = proj + vec_ref[:, V_QKV + at : V_QKV + at + D]
        if part == 2:
            kept[:, COL_QKV + at : COL_QKV + at + D] = proj.astype(bf16)
        else:
            for p in range(D // PAIR):
                u = proj[:, p * PAIR : (p + 1) * PAIR]
                turned = (
                    u * cos_ref[...]
                    + pltpu.roll(u, PAIR - ROT // 2, 1) * sa_ref[...]
                    + pltpu.roll(u, ROT // 2, 1) * sb_ref[...]
                )
                kept[:, COL_QKV + at + p * PAIR : COL_QKV + at + (p + 1) * PAIR] = turned.astype(bf16)
    store(0, COL_QKV, 3 * D)
    store(1, COL_X, D)

    scales = head_masks(1.0 / math.sqrt(HEAD))
    lane = lax.broadcasted_iota(jnp.int32, (1, PAIR), 1)
    lse[...] = jnp.zeros_like(lse)
    q_at = lax.broadcasted_iota(jnp.int32, (QROWS, QROWS), 0)
    k_at = lax.broadcasted_iota(jnp.int32, (QROWS, QROWS), 1)

    def attend(p, carry):
        lanes = pl.multiple_of(p * PAIR, PAIR)
        for tile in range(length // QROWS):
            rows = pl.ds(tile * QROWS, QROWS)
            keys = (tile + 1) * QROWS
            q = kept[rows, pl.ds(COL_QKV + lanes, PAIR)]
            k = kept[pl.ds(0, keys), pl.ds(COL_QKV + D + lanes, PAIR)]
            v = kept[pl.ds(0, keys), pl.ds(COL_QKV + 2 * D + lanes, PAIR)]
            outs = []
            for side in range(2):
                s = nt(q * scales[side], k)
                near = jnp.where(k_at <= q_at, s[:, keys - QROWS :], -1e30)
                s = jnp.concatenate([s[:, : keys - QROWS], near], axis=1) if tile else near
                peak = jnp.max(s, axis=1, keepdims=True)
                expo = jnp.exp(s - peak)
                total = jnp.sum(expo, axis=1, keepdims=True)
                soft = (expo * (1.0 / total)).astype(bf16)
                outs.append(nn(soft, v))
                log_total = peak + jnp.log(total)
                lse[rows, :] = jnp.where(lane == 2 * p + side, log_total, lse[rows, :])
            mixed = jnp.where(lane < HEAD, outs[0], outs[1])
            kept[rows, pl.ds(COL_O + lanes, PAIR)] = mixed.astype(bf16)
        return carry

    lax.fori_loop(0, HEADS // 2, attend, 0)
    wait_for(copies, 1)
    out = x_ref[...].astype(f32) + (nn(kept[:, COL_O : COL_O + D], wo[...]) + vec_ref[:, V_O : V_O + D])
    store(2, COL_A, 3 * D)
    wait_for(copies, 2)
    wait_for(copies, 3)
    branch = jnp.zeros((length, D), f32) + vec_ref[:, V_B2 : V_B2 + D]
    for c in range(0, FF, CHUNK):
        h = nn(kept[:, COL_B : COL_B + D], w1[:, c : c + CHUNK]) + vec_ref[:, V_B1 + c : V_B1 + c + CHUNK]
        act, slope = gelu_both(h)
        kept[:, COL_H + c : COL_H + c + CHUNK] = act.astype(bf16)
        kept[:, COL_GP + c : COL_GP + c + CHUNK] = slope.astype(bf16)
        branch = branch + nn(kept[:, COL_H + c : COL_H + c + CHUNK], w2[c : c + CHUNK, :])
    store(3, COL_H, FF)
    store(4, COL_GP, FF)
    out = out + branch
    xo[...] = out
    xb_ref[...] = out.astype(bf16)
    tails = [
        pltpu.make_async_copy(xo, xo_out.at[slot], osem.at[5]),
        pltpu.make_async_copy(lse, lse_out.at[slot], osem.at[6]),
    ]
    for copy in tails:
        copy.start()
    hat, _ = normalized(out)
    final = (hat * fin_ref[:, :D] + fin_ref[:, D : 2 * D]).astype(bf16)
    red_ref[0:1, :] = jnp.sum(hat, axis=0, keepdims=True)
    red_ref[1:2, :] = jnp.sum(final.astype(f32), axis=0, keepdims=True)
    red_ref[2:8, :] = jnp.zeros((6, D), f32)
    for copy in stores + tails:
        copy.wait()


def forward(slot, x, vec, fin, tables, shards, state, slots):
    length = x.shape[0]
    count = len(shards)
    first = state is None
    whole = pl.BlockSpec(memory_space=pltpu.VMEM)
    anywhere = pl.BlockSpec(memory_space=pl.ANY)
    kept_shape = (
        jax.ShapeDtypeStruct((slots, length, KEPT), bf16),
        jax.ShapeDtypeStruct((slots, length, D), f32),
        jax.ShapeDtypeStruct((slots, length, PAIR), f32),
    )
    operands = [slot, x, vec, fin, *tables, *shards] + ([] if first else list(state))
    return pl.pallas_call(
        functools.partial(forward_kernel, count, first),
        out_shape=(
            jax.ShapeDtypeStruct((length, D), bf16),
            jax.ShapeDtypeStruct((8, D), f32),
            *kept_shape,
        ),
        in_specs=[pl.BlockSpec(memory_space=pltpu.SMEM)]
        + [whole] * 6
        + [anywhere] * (len(operands) - 7),
        out_specs=(whole, whole, anywhere, anywhere, anywhere),
        input_output_aliases={} if first else {7 + count + i: 2 + i for i in range(3)},
        scratch_shapes=[
            pltpu.VMEM((D, 3 * D), bf16),
            pltpu.VMEM((D, D), bf16),
            pltpu.VMEM((D, FF), bf16),
            pltpu.VMEM((FF, D), bf16),
            pltpu.VMEM((length, KEPT), bf16),
            pltpu.VMEM((length, D), f32),
            pltpu.VMEM((length, PAIR), f32),
            pltpu.SemaphoreType.DMA((len(PLACES),)),
            pltpu.SemaphoreType.DMA((7,)),
        ],
        compiler_params=pltpu.CompilerParams(vmem_limit_bytes=VMEM_LIMIT),
        cost_estimate=pl.CostEstimate(flops=10 * 10**9, bytes_accessed=30 * 10**6, transcendentals=5 * 10**6),
        name="layer_forward",
    )(*operands)


def backward_kernel(shard_count, *refs):
    slot_ref, flag_ref, recv_ref, vec_ref, fin_ref, cos_ref, sa_ref, sb_ref = refs[:8]
    shards = refs[8 : 8 + shard_count]
    kept_in, xo_in, lse_in = refs[8 + shard_count : 11 + shard_count]
    rest = refs[11 + shard_count :]
    dx_ref, vg_ref, kept_out = rest[:3]
    wqkv, wo, w1, w2, qkv, gp, x, xo, lse, grads, dmix, dq, dk, dv, wsem, isem, osem = rest[3:]
    mats = (wqkv, wo, w1, w2)
    length = recv_ref.shape[0]
    slot = slot_ref[0]
    copies = weight_copies(shards, mats, wsem)
    loads = [
        pltpu.make_async_copy(xo_in.at[slot], xo, isem.at[0]),
        pltpu.make_async_copy(kept_in.at[slot, :, pl.ds(COL_GP, FF)], gp, isem.at[1]),
        pltpu.make_async_copy(kept_in.at[slot, :, pl.ds(COL_X, D)], x, isem.at[2]),
        pltpu.make_async_copy(kept_in.at[slot, :, pl.ds(COL_QKV, 3 * D)], qkv, isem.at[3]),
        pltpu.make_async_copy(lse_in.at[slot], lse, isem.at[4]),
    ]
    loads[0].start()
    for which, copy in copies:
        if which == 3:
            copy.start()
    loads[1].start()
    loads[2].start()
    for which, copy in copies:
        if which == 2:
            copy.start()
    loads[3].start()
    loads[4].start()
    for which, copy in copies:
        if which < 2:
            copy.start()

    loads[0].wait()
    hat, scale = normalized(xo[...])
    weight = fin_ref[:, 2 * D : 3 * D] * fin_ref[:, :D]
    top = flag_ref[0] * norm_back(1.0, weight, hat, scale)
    use_top = flag_ref[1] > 0.5
    xo[...] = jnp.where(use_top, top, recv_ref[...].astype(f32))
    grads[:, COL_G : COL_G + D] = xo[...].astype(bf16)
    bias = jnp.sum(grads[:, COL_G : COL_G + D].astype(f32), axis=0, keepdims=True)
    vg_ref[:, V_O : V_O + D] = bias
    vg_ref[:, V_B2 : V_B2 + D] = bias

    wait_for(copies, 3)
    loads[1].wait()
    loads[2].wait()
    wait_for(copies, 2)
    second = jnp.zeros((length, D), f32)
    for c in range(0, FF, CHUNK):
        act = nt(grads[:, COL_G : COL_G + D], w2[c : c + CHUNK, :])
        pre = (act * gp[:, c : c + CHUNK].astype(f32)).astype(bf16)
        grads[:, COL_DH + c : COL_DH + c + CHUNK] = pre
        vg_ref[:, V_B1 + c : V_B1 + c + CHUNK] = jnp.sum(pre.astype(f32), axis=0, keepdims=True)
        second = second + nt(pre, w1[:, c : c + CHUNK])
    hat, scale = normalized(x[...].astype(f32))
    vg_ref[:, V_G2 : V_G2 + D] = jnp.sum(second * hat, axis=0, keepdims=True)
    vg_ref[:, V_C2 : V_C2 + D] = jnp.sum(second, axis=0, keepdims=True)
    xo[...] = xo[...] + norm_back(second, vec_ref[:, V_G2 : V_G2 + D], hat, scale)
    stores = [
        pltpu.make_async_copy(
            grads.at[:, pl.ds(COL_G, D)], kept_out.at[slot, :, pl.ds(COL_X, D)], osem.at[0]
        ),
        pltpu.make_async_copy(
            grads.at[:, pl.ds(COL_DH, FF)], kept_out.at[slot, :, pl.ds(COL_GP, FF)], osem.at[1]
        ),
    ]
    stores[0].start()
    stores[1].start()

    wait_for(copies, 1)
    dmix[...] = nt(grads[:, COL_G : COL_G + D], wo[...]).astype(bf16)
    loads[3].wait()
    loads[4].wait()
    lse_rows = jnp.transpose(lse[...])
    lse[0:PAIR, :] = lse_rows[:, 0:PAIR]
    for part in range(1, length // PAIR):
        lse[part * PAIR : (part + 1) * PAIR, :] = lse_rows[:, part * PAIR : (part + 1) * PAIR]
    scales = head_masks(1.0 / math.sqrt(HEAD))
    ones = head_masks(1.0)
    k_at = lax.broadcasted_iota(jnp.int32, (QROWS, QROWS), 0)
    q_at = lax.broadcasted_iota(jnp.int32, (QROWS, QROWS), 1)

    def attend(p, carry):
        lanes = pl.multiple_of(p * PAIR, PAIR)
        for tile in range(length // QROWS):
            rows = pl.ds(tile * QROWS, QROWS)
            keys = (tile + 1) * QROWS
            q = qkv[rows, pl.ds(lanes, PAIR)]
            k = qkv[pl.ds(0, keys), pl.ds(D + lanes, PAIR)]
            v = qkv[pl.ds(0, keys), pl.ds(2 * D + lanes, PAIR)]
            dm = dmix[rows, pl.ds(lanes, PAIR)]
            dq_sum = dk_sum = dv_sum = None
            for side in range(2):
                qs = q * scales[side]
                ks = k * scales[side]
                dms = dm * ones[side]
                s = nt(k, qs)
                row = jnp.concatenate(
                    [
                        lse[pl.ds(part * PAIR + 2 * p + side, 1), :]
                        for part in range(tile * QROWS // PAIR, (tile + 1) * QROWS // PAIR)
                    ],
                    axis=1,
                )
                soft = jnp.exp(s - row)
                near = jnp.where(k_at <= q_at, soft[keys - QROWS :, :], 0.0)
                soft = jnp.concatenate([soft[: keys - QROWS, :], near], axis=0) if tile else near
                dsoft = nt(v, dms)
                centre = jnp.sum(soft * dsoft, axis=0, keepdims=True)
                ds = (soft * (dsoft - centre)).astype(bf16)
                one_dv = nn(soft.astype(bf16), dms)
                one_dk = nn(ds, qs)
                one_dq = tn(ds, ks)
                if side:
                    dq_sum, dk_sum, dv_sum = dq_sum + one_dq, dk_sum + one_dk, dv_sum + one_dv
                else:
                    dq_sum, dk_sum, dv_sum = one_dq, one_dk, one_dv
            dq[rows, :] = dq_sum
            if tile:
                old = pl.ds(0, tile * QROWS)
                new = pl.ds(tile * QROWS, QROWS)
                dk[old, :] = dk[old, :] + dk_sum[: tile * QROWS]
                dk[new, :] = dk_sum[tile * QROWS :]
                dv[old, :] = dv[old, :] + dv_sum[: tile * QROWS]
                dv[new, :] = dv_sum[tile * QROWS :]
            else:
                dk[rows, :] = dk_sum
                dv[rows, :] = dv_sum
        for part, ref in ((0, dq), (1, dk)):
            g = ref[...]
            turned = (
                g * cos_ref[...]
                - pltpu.roll(g, PAIR - ROT // 2, 1) * sa_ref[...]
                - pltpu.roll(g, ROT // 2, 1) * sb_ref[...]
            )
            grads[:, pl.ds(COL_DP + part * D + lanes, PAIR)] = turned.astype(bf16)
        grads[:, pl.ds(COL_DP + 2 * D + lanes, PAIR)] = dv[...].astype(bf16)
        return carry

    lax.fori_loop(0, HEADS // 2, attend, 0)
    stores.append(
        pltpu.make_async_copy(
            grads.at[:, pl.ds(COL_DP, 3 * D)], kept_out.at[slot, :, pl.ds(COL_QKV, 3 * D)], osem.at[2]
        )
    )
    stores[2].start()
    vg_ref[:, V_QKV : V_QKV + 3 * D] = jnp.sum(
        grads[:, COL_DP : COL_DP + 3 * D].astype(f32), axis=0, keepdims=True
    )
    wait_for(copies, 0)
    one = nt(grads[:, COL_DP : COL_DP + 3 * D], wqkv[...])
    hat, scale = normalized(x[...].astype(f32))
    vg_ref[:, V_G1 : V_G1 + D] = jnp.sum(one * hat, axis=0, keepdims=True)
    vg_ref[:, V_C1 : V_C1 + D] = jnp.sum(one, axis=0, keepdims=True)
    total = xo[...] + norm_back(one, vec_ref[:, V_G1 : V_G1 + D], hat, scale)
    dx_ref[...] = total.astype(bf16)
    for copy in stores:
        copy.wait()


def backward(slot, flags, recv, vec, fin, tables, shards, state):
    length = recv.shape[0]
    count = len(shards)
    whole = pl.BlockSpec(memory_space=pltpu.VMEM)
    anywhere = pl.BlockSpec(memory_space=pl.ANY)
    small = pl.BlockSpec(memory_space=pltpu.SMEM)
    operands = [slot, flags, recv, vec, fin, *tables, *shards, *state]
    return pl.pallas_call(
        functools.partial(backward_kernel, count),
        out_shape=(
            jax.ShapeDtypeStruct((length, D), bf16),
            jax.ShapeDtypeStruct((1, V_END), f32),
            jax.ShapeDtypeStruct(state[0].shape, bf16),
        ),
        in_specs=[small, small] + [whole] * 6 + [anywhere] * (len(operands) - 8),
        out_specs=(whole, whole, anywhere),
        input_output_aliases={8 + count: 2},
        scratch_shapes=[
            pltpu.VMEM((D, 3 * D), bf16),
            pltpu.VMEM((D, D), bf16),
            pltpu.VMEM((D, FF), bf16),
            pltpu.VMEM((FF, D), bf16),
            pltpu.VMEM((length, 3 * D), bf16),
            pltpu.VMEM((length, FF), bf16),
            pltpu.VMEM((length, D), bf16),
            pltpu.VMEM((length, D), f32),
            pltpu.VMEM((length, PAIR), f32),
            pltpu.VMEM((length, GRADS), bf16),
            pltpu.VMEM((length, D), bf16),
            pltpu.VMEM((length, PAIR), f32),
            pltpu.VMEM((length, PAIR), f32),
            pltpu.VMEM((length, PAIR), f32),
            pltpu.SemaphoreType.DMA((len(PLACES),)),
            pltpu.SemaphoreType.DMA((5,)),
            pltpu.SemaphoreType.DMA((3,)),
        ],
        compiler_params=pltpu.CompilerParams(vmem_limit_bytes=VMEM_LIMIT),
        cost_estimate=pl.CostEstimate(flops=20 * 10**9, bytes_accessed=40 * 10**6, transcendentals=5 * 10**6),
        name="layer_backward",
    )(*operands)


def product_kernel(left_at, right_at, x_ref, y_ref, out_ref):
    units, rows, width = x_ref.shape
    x = x_ref[...].reshape(units * rows, width)
    y = y_ref[...].reshape(units * rows, width)
    out_ref[0] = tn(x, y)


def products(left_at, right_at, kept, units):
    count = left_at.shape[0]
    length = kept.shape[1]
    return pl.pallas_call(
        product_kernel,
        out_shape=jax.ShapeDtypeStruct((count, TILE, TILE), f32),
        grid_spec=pltpu.PrefetchScalarGridSpec(
            num_scalar_prefetch=2,
            grid=(count,),
            in_specs=[
                pl.BlockSpec((units, length, TILE), lambda i, a, b: (0, 0, a[i])),
                pl.BlockSpec((units, length, TILE), lambda i, a, b: (0, 0, b[i])),
            ],
            out_specs=pl.BlockSpec((1, TILE, TILE), lambda i, a, b: (i, 0, 0)),
        ),
        compiler_params=pltpu.CompilerParams(vmem_limit_bytes=VMEM_LIMIT),
        cost_estimate=pl.CostEstimate(
            flops=2 * count * TILE * TILE * units * length,
            bytes_accessed=count * TILE * (4 * units * length + 4 * TILE),
            transcendentals=0,
        ),
        name="weight_products",
    )(left_at, right_at, kept, kept)


def split(value):
    high = value.astype(bf16)
    return high, (value - high.astype(f32)).astype(bf16)


def shampoo_kernel(factor_ref, g_ref, w_ref, ls_ref, rs_ref, lr_ref, rr_ref, bg_ref, nw_ref, nl_ref, nr_ref):
    factor = factor_ref[0]
    g = g_ref[0]
    bg_ref[0] = g.astype(f32) * factor
    level = (1.0 - stats_decay) * factor * factor
    nl_ref[0] = stats_decay * ls_ref[0] + level * nt(g, g)
    nr_ref[0] = stats_decay * rs_ref[0] + level * tn(g, g)
    right_high, right_low = split(rr_ref[0])
    inner = nn(g, right_high) + nn(g, right_low)
    inner_high, inner_low = split(inner)
    left_high, left_low = split(lr_ref[0])
    direction = nn(left_high, inner_high) + (nn(left_high, inner_low) + nn(left_low, inner_high))
    nw_ref[0] = w_ref[0] - (shampoo_rate * factor) * direction


def shampoo(factor, grad, weights, left_stats, right_stats, left_root, right_root):
    count = grad.shape[0]
    block = pl.BlockSpec((1, TILE, TILE), lambda i: (i, 0, 0))
    shape = jax.ShapeDtypeStruct((count, TILE, TILE), f32)
    return pl.pallas_call(
        shampoo_kernel,
        out_shape=(shape,) * 4,
        grid=(count,),
        in_specs=[pl.BlockSpec(memory_space=pltpu.SMEM)] + [block] * 6,
        out_specs=(block,) * 4,
        compiler_params=pltpu.CompilerParams(vmem_limit_bytes=VMEM_LIMIT),
        cost_estimate=pl.CostEstimate(
            flops=14 * count * TILE**3, bytes_accessed=38 * count * TILE * TILE, transcendentals=0
        ),
        name="shampoo",
    )(factor, grad, weights, left_stats, right_stats, left_root, right_root)


def rope_columns(length):
    half_rot = ROT // 2
    lanes = jnp.arange(PAIR) % HEAD
    index = jnp.where(lanes < half_rot, lanes, lanes - half_rot).astype(f32)
    inverse = rope_base ** (-2.0 * index / ROT)
    angles = jnp.arange(length)[:, None].astype(f32) * inverse[None, :]
    cosine = jnp.where(lanes < ROT, jnp.cos(angles), 1.0)
    sine = jnp.where(lanes < ROT, jnp.sin(angles), 0.0)
    first = jnp.where(lanes < half_rot, -sine, 0.0)
    second = jnp.where(lanes < half_rot, 0.0, sine)
    return cosine, first, second


def adam_step(weight, moment, second, grad, rate, decay):
    moment_new = beta_first * moment + (1.0 - beta_first) * grad
    second_new = beta_second * second + (1.0 - beta_second) * grad * grad
    corrected = moment_new / (1.0 - beta_first**STEP)
    scaled = jnp.sqrt(second_new / (1.0 - beta_second**STEP)) + adam_eps
    return (moment_new, second_new, weight - rate * (corrected / scaled + decay * weight))


def rounded(values):
    return lax.reduce_precision(values, 8, 7)


def chosen(flags, values):
    total = values[-1]
    for flag, value in zip(flags[:-1], values[:-1]):
        total = jnp.where(flag, value, total)
    return total


def ordered(section, mine, other, axis):
    return jnp.concatenate(
        [jnp.where(section == 0, mine, other), jnp.where(section == 0, other, mine)], axis=axis
    )


def swapped(value):
    return lax.ppermute(value, "section", [(0, 1), (1, 0)])


def local(
    tokens,
    margins,
    tie_flags,
    embedding,
    embed_moment,
    embed_second,
    layer_blocks,
    left_stats,
    right_stats,
    left_root,
    right_root,
    layer_vectors,
    vector_moment,
    vector_second,
    closing_vectors,
    final_moment,
    final_second,
):
    both = ("section", "dp")
    count = lax.axis_size("dp")
    section = lax.axis_index("section")
    place = lax.axis_index("dp")
    low, high = count // 2 - 1, count // 2
    is_high = place >= high
    length = tokens.shape[2]
    units = tokens.shape[0] * count
    own_blocks = layer_blocks.shape[1]
    own_vector = layer_vectors.shape[1]
    own_final = closing_vectors.shape[0]
    features, vocab = embedding.shape

    own = layer_blocks[0].astype(bf16)
    shards = [None] * count
    order_low = list(range(count - 1, low, -1)) + list(range(low + 1))
    order_high = [count - 1 - k for k in order_low]
    for k in order_low:
        direct = lax.ppermute(own, both, [(k, low), (count + k, count + high)])
        relayed = lax.ppermute(direct, both, [(low, count + low), (count + high, high)])
        shards[k] = jnp.where((section == 1) == is_high, direct, relayed)

    pack = jnp.concatenate(
        [
            tokens.reshape(-1).astype(f32),
            margins.astype(f32),
            tie_flags.astype(f32),
            rounded(layer_vectors[0]),
            rounded(closing_vectors),
        ]
    )
    packs = lax.all_gather(pack, both, axis=0, tiled=False).reshape(2, count, -1)
    at = tokens.size
    ids = packs[0, :, :at].astype(jnp.int32).reshape(-1)
    pair_margins = packs[0, :, at : at + margins.size].reshape(-1)
    at = at + margins.size
    pair_ties = packs[0, :, at : at + margins.size].reshape(-1)
    at = at + margins.size
    layer_all = packs[:, :, at : at + own_vector].reshape(2, -1)
    vec = jnp.where(is_high, layer_all[1], layer_all[0])[None]
    fin = packs[:, :, at + own_vector :].reshape(1, -1)
    tables = rope_columns(length)

    looked = jnp.take(embedding.astype(bf16), ids, axis=1)
    half = jnp.concatenate([lax.ppermute(looked, "dp", [(k, low)]) for k in range(count)], axis=0)
    span = units * length
    mine = lax.dynamic_slice_in_dim(half, section * span, span, 1)
    other = swapped(lax.dynamic_slice_in_dim(half, (1 - section) * span, span, 1))
    embedded = ordered(section, mine, other, 0).reshape(D, units, length).transpose(1, 2, 0)

    slots = units + 1
    state = None
    arrived = []
    sums = []
    for tick in range(units + 2):
        slot = jnp.where(is_high, tick - 2 if tick >= 2 else units, min(tick, units))
        inputs = embedded[min(tick, units - 1)]
        if tick >= 2:
            inputs = jnp.where(is_high, arrived[tick - 2], inputs)
        result, tail, *state = forward(
            slot.astype(jnp.int32).reshape(1), inputs, vec, fin, tables, [*shards], state, slots
        )
        if tick < units:
            arrived.append(lax.ppermute(result, "dp", [(low, high)]))
        if tick >= 2:
            sums.append(tail[:2])
    sums = jnp.stack(sums)
    sum_hat, sum_final = sums[:, 0], sums[:, 1]
    final_gain, head = fin[0, :D], fin[0, 2 * D :]
    rewards = (jnp.sum(sum_final * head, axis=1) / length).reshape(-1, 2)
    pairs = units // 2
    gap = rewards[:, 0] - rewards[:, 1]
    half_margin = 0.5 * lax.dynamic_slice_in_dim(pair_margins, section * pairs, pairs, 0)
    tie = lax.dynamic_slice_in_dim(pair_ties, section * pairs, pairs, 0)
    pair_loss = (1.0 - tie) * jax.nn.softplus(half_margin - gap) + tie * 0.5 * (
        jax.nn.softplus(gap) + jax.nn.softplus(-gap)
    )
    gap_grad = -(1.0 - tie) * jax.nn.sigmoid(half_margin - gap) + tie * 0.5 * (
        jax.nn.sigmoid(gap) - jax.nn.sigmoid(-gap)
    )
    reward_grad = (jnp.stack([gap_grad, -gap_grad], axis=1) / length).reshape(-1)
    final_local = jnp.concatenate(
        [
            head * jnp.sum(reward_grad[:, None] * sum_hat, axis=0),
            head * (length * jnp.sum(reward_grad)),
            jnp.sum(reward_grad[:, None] * sum_final, axis=0),
        ]
    )

    arrived = []
    vector_sum = jnp.zeros((1, V_END), f32)
    embed_grads = []
    for tick in range(units + 2):
        slot = jnp.where(is_high, min(tick, units), tick - 2 if tick >= 2 else units)
        flags = jnp.stack([reward_grad[min(tick, units - 1)], is_high.astype(f32)])
        received = arrived[tick - 2] if tick >= 2 else jnp.zeros((length, D), bf16)
        grad_in, vector_part, state[0] = backward(
            slot.astype(jnp.int32).reshape(1), flags, received, vec, fin, tables, [*shards], state
        )
        if tick < units:
            arrived.append(lax.ppermute(grad_in, "dp", [(high, low)]))
        live = jnp.where(is_high, tick < units, tick >= 2)
        vector_sum = vector_sum + jnp.where(live, vector_part, 0.0)
        if tick >= 2:
            embed_grads.append(grad_in)

    embed_grads = jnp.stack(embed_grads).reshape(span, D).T
    half_width = D // 2
    mine = lax.dynamic_slice_in_dim(embed_grads, section * half_width, half_width, 0)
    other = swapped(lax.dynamic_slice_in_dim(embed_grads, (1 - section) * half_width, half_width, 0))
    half = ordered(section, mine, other, 1)
    token_grads = chosen(
        [place == k for k in range(count)],
        [
            lax.ppermute(half[k * features : (k + 1) * features], "dp", [(low, k)])
            for k in range(count)
        ],
    )

    left_at = jnp.array([(0, 2, 4, 6)[m] + row for m, row, _ in PLACES], jnp.int32)
    right_at = jnp.array([(14, 28, 20, 28)[m] + col for m, _, col in PLACES], jnp.int32)
    part = (own_blocks + 1) // 2
    rest = own_blocks - part
    kept = state[0]

    def part_of(start):
        return products(
            lax.dynamic_slice_in_dim(left_at, start, part, 0),
            lax.dynamic_slice_in_dim(right_at, start, part, 0),
            kept,
            units,
        )

    pieces = []
    for step in range(count):
        base = jnp.where(is_high, order_high[step], order_low[step]) * own_blocks
        sent = swapped(part_of(base + (1 - section) * rest))
        total = (part_of(base + section * rest) + sent).astype(bf16)
        route = [
            (core * count + source, core * count + target)
            for core in range(2)
            for source, target in ((low, order_low[step]), (high, order_high[step]))
        ]
        pieces.append(lax.ppermute(total, both, route))
    piece_low = chosen([place == k for k in order_low], pieces)
    piece_high = chosen([place == k for k in order_high], pieces)
    mine = jnp.where(section == 0, piece_low, piece_high)
    other = swapped(jnp.where(section == 0, piece_high, piece_low))
    grad_blocks = jnp.concatenate(
        [
            jnp.where(section == 0, mine, other),
            jnp.where(section == 0, other, mine)[2 * part - own_blocks :],
        ],
        axis=0,
    )

    zero = jnp.zeros((V_END,), f32)
    live_low, live_high = place == low, place == high
    vector_pack = jnp.concatenate(
        [
            jnp.where(live_low, vector_sum[0], zero),
            jnp.where(live_high, vector_sum[0], zero),
            jnp.where(live_high, final_local, 0.0),
            jnp.where(live_high, jnp.sum(pair_loss), 0.0).reshape(1),
        ]
    )
    vector_all = lax.psum(vector_pack, both)
    loss_total = vector_all[-1:]
    owned_vector = lax.dynamic_slice_in_dim(
        vector_all, section * V_END + place * own_vector, own_vector, 0
    )[None]
    owned_final = lax.dynamic_slice_in_dim(
        vector_all, 2 * V_END + (section * count + place) * own_final, own_final, 0
    )

    table_grad = jax.ops.segment_sum(token_grads.T.astype(f32), ids, num_segments=vocab).T
    block_values = grad_blocks.astype(f32)
    squares = (
        jnp.sum(block_values * block_values)
        + jnp.sum(owned_vector * owned_vector)
        + jnp.sum(owned_final * owned_final)
        + jnp.sum(table_grad * table_grad)
    )
    norm_value = jnp.sqrt(lax.psum(squares, both))
    factor = clip_limit / jnp.maximum(norm_value, clip_limit)

    block_grad, new_blocks, new_left, new_right = (
        out[None]
        for out in shampoo(
            factor.reshape(1),
            grad_blocks,
            layer_blocks[0],
            left_stats[0],
            right_stats[0],
            left_root[0],
            right_root[0],
        )
    )
    vector_m, vector_v, vector_w = adam_step(
        layer_vectors, vector_moment, vector_second, owned_vector * factor, vector_rate, 0.0
    )
    final_m, final_v, final_w = adam_step(
        closing_vectors, final_moment, final_second, owned_final * factor, vector_rate, 0.0
    )
    embed_m, embed_v, embed_w = adam_step(
        embedding, embed_moment, embed_second, table_grad * factor, embed_rate, embed_decay
    )
    return (
        loss_total,
        norm_value.reshape(1),
        block_grad,
        new_blocks,
        new_left,
        new_right,
        vector_m,
        vector_v,
        vector_w,
        final_m,
        final_v,
        final_w,
        embed_m,
        embed_v,
        embed_w,
    )


def solution(mesh):
    return jax.shard_map(
        local,
        mesh=mesh,
        in_specs=(
            P(("member", "dp"), None, None),
            P(("member", "dp")),
            P(("member", "dp")),
            P(("member", "section", "dp"), None),
            P(("member", "section", "dp"), None),
            P(("member", "section", "dp"), None),
            P(("member", "section"), "dp", None, None),
            P(("member", "section"), "dp", None, None),
            P(("member", "section"), "dp", None, None),
            P(("member", "section"), "dp", None, None),
            P(("member", "section"), "dp", None, None),
            P(("member", "section"), "dp"),
            P(("member", "section"), "dp"),
            P(("member", "section"), "dp"),
            P(("member", "section", "dp")),
            P(("member", "section", "dp")),
            P(("member", "section", "dp")),
        ),
        out_specs=(
            P("member"),
            P("member"),
            P(("member", "section"), "dp", None, None),
            P(("member", "section"), "dp", None, None),
            P(("member", "section"), "dp", None, None),
            P(("member", "section"), "dp", None, None),
            P(("member", "section"), "dp"),
            P(("member", "section"), "dp"),
            P(("member", "section"), "dp"),
            P(("member", "section", "dp")),
            P(("member", "section", "dp")),
            P(("member", "section", "dp")),
            P(("member", "section", "dp"), None),
            P(("member", "section", "dp"), None),
            P(("member", "section", "dp"), None),
        ),
        check_vma=False,
    )
```

```python
import functools
import math

import jax
import jax.numpy as jnp
from jax import lax
from jax.experimental import pallas as pl
from jax.experimental.pallas import tpu as pltpu
from jax.sharding import PartitionSpec as P

D = 768
HEADS = 12
HEAD = 64
ROT = 16
FF = 3072
STEP = 10
TILE = 384
PAIR = 2 * HEAD
QROWS = 256
CHUNK = 768
LSE_ROWS = 16

norm_eps = 1e-05
beta_first = 0.9
beta_second = 0.999
adam_eps = 1e-08
clip_limit = 1.0
embed_rate = 0.2
embed_decay = 0.01
vector_rate = 0.5
shampoo_rate = 0.1
stats_decay = 0.95
rope_base = 10000.0

f32 = jnp.float32
bf16 = jnp.bfloat16
VMEM_LIMIT = 60 * 2**20
LIGHT = pl.CostEstimate(flops=1, bytes_accessed=1, transcendentals=0)

COL_A, COL_O, COL_B, COL_H = 0, D, 2 * D, 3 * D
COL_QKV = 3 * D + FF
COL_GP = COL_QKV + 3 * D
COL_X = COL_GP + FF
KEPT = COL_X + D
COL_DP, COL_G, COL_DH = 0, 3 * D, 4 * D
GRADS = 4 * D + FF

V_G1, V_C1, V_G2, V_C2, V_QKV, V_O = 0, D, 2 * D, 3 * D, 4 * D, 7 * D
V_B1, V_B2, V_END = 8 * D, 8 * D + FF, 9 * D + FF


def block_places():
    places = []
    for matrix, (rows, cols) in enumerate(((D, 3 * D), (D, D), (D, FF), (FF, D))):
        for row in range(rows // TILE):
            for col in range(cols // TILE):
                places.append((matrix, row, col))
    return places


PLACES = block_places()


def nt(a, b):
    return lax.dot_general(a, b, (((1,), (1,)), ((), ())), preferred_element_type=f32)


def tn(a, b):
    return lax.dot_general(a, b, (((0,), (0,)), ((), ())), preferred_element_type=f32)


def nn(a, b):
    return lax.dot_general(a, b, (((1,), (0,)), ((), ())), preferred_element_type=f32)


def normalized(x):
    mean = jnp.mean(x, axis=-1, keepdims=True)
    centred = x - mean
    spread = jnp.mean(centred * centred, axis=-1, keepdims=True)
    scale = lax.rsqrt(spread + norm_eps)
    return centred * scale, scale


def norm_back(grad, gain, hat, scale):
    inner = grad * gain
    first = jnp.mean(inner, axis=-1, keepdims=True)
    second = jnp.mean(inner * hat, axis=-1, keepdims=True)
    return scale * (inner - first - hat * second)


def gelu_both(h):
    expo = jnp.exp(-0.5 * h * h)
    t = 1.0 / (1.0 + (0.3275911 * math.sqrt(0.5)) * jnp.abs(h))
    poly = 0.5 * 1.061405429
    for coef in (-1.453152027, 1.421413741, -0.284496736, 0.254829592):
        poly = poly * t + 0.5 * coef
    tail = poly * t * expo
    cdf = jnp.where(h >= 0.0, 1.0 - tail, tail)
    return h * cdf, cdf + h * expo * (1.0 / math.sqrt(2.0 * math.pi))


def head_masks(value):
    lane = lax.broadcasted_iota(jnp.int32, (1, PAIR), 1)
    return [
        jnp.where(lane < HEAD, value, 0.0).astype(bf16),
        jnp.where(lane < HEAD, 0.0, value).astype(bf16),
    ]


def arrivals(count):
    low = count // 2 - 1
    order = list(range(count - 1, low, -1)) + list(range(low))
    return [order[i : i + 2] for i in range(0, count - 1, 2)]


def shard_sources(count, is_high, direct):
    rounds = arrivals(count)
    own = count // 2 - 1
    sources = [None] * count
    for index, pair in enumerate(rounds):
        for side, shard in enumerate(pair):
            sources[shard] = index + (0 if direct == (side == 0) else len(rounds))
    sources[own] = 2 * len(rounds) + (0 if direct else 1)
    return sources[::-1] if is_high else sources


class Weights:
    def __init__(self, role, arrays, mats, sems):
        self.role = role
        count = len(PLACES) // arrays[0].shape[0]
        per = arrays[0].shape[0]
        self.copies = []
        for is_high in (False, True):
            for direct in (False, True):
                sources = shard_sources(count, is_high, direct)
                self.copies.append(
                    [
                        pltpu.make_async_copy(
                            arrays[sources[index // per]].at[index % per],
                            mats[matrix].at[pl.ds(row * TILE, TILE), pl.ds(col * TILE, TILE)],
                            sems.at[index],
                        )
                        for index, (matrix, row, col) in enumerate(PLACES)
                    ]
                )

    def start(self, *matrices):
        for role, copies in enumerate(self.copies):

            @pl.when(self.role == role)
            def _(copies=copies):
                for matrix in matrices:
                    for place, copy in zip(PLACES, copies):
                        if place[0] == matrix:
                            copy.start()

    def wait(self, matrix):
        for place, copy in zip(PLACES, self.copies[0]):
            if place[0] == matrix:
                copy.wait()


def forward_kernel(tick, unit, part_count, shard_count, first, handed, *refs):
    meta_ref, order_ref, vec_ref, fin_ref, cos_ref, sa_ref, sb_ref = refs[:7]
    if handed:
        recv_ref, *refs = refs[7:]
    else:
        refs = refs[7:]
    parts, refs = refs[:part_count], refs[part_count:]
    shards = refs[:shard_count]
    rest = refs[shard_count + (0 if first else 3) :]
    xb_ref, red_ref, kept_out, xo_out, lse_out = rest[:5]
    wqkv, wo, w1, w2, kept, xo, lse, looked, wsem, isem, osem = rest[5:]
    mats = (wqkv, wo, w1, w2)
    length = xb_ref.shape[0]
    slot = meta_ref[1 + tick]
    weights = Weights(meta_ref[0], shards, mats, wsem)
    width = looked.shape[2]

    def assemble():
        copies = [
            pltpu.make_async_copy(part.at[pl.ds(unit * length, length)], looked.at[k], isem.at[k])
            for k, part in enumerate(parts)
        ]
        for copy in copies:
            copy.start()
        for copy in copies:
            copy.wait()
        found = jnp.zeros((length, D), f32)
        for k in range(part_count):
            found = found + nn(looked[k], order_ref[k * width : (k + 1) * width, :])
        kept[:, COL_X : COL_X + D] = found.astype(bf16)

    weights.start(0)
    if handed:
        is_high = meta_ref[0] >= 2

        @pl.when(is_high)
        def _():
            copy = pltpu.make_async_copy(recv_ref, kept.at[:, pl.ds(COL_X, D)], isem.at[0])
            copy.start()
            copy.wait()

        pl.when(jnp.logical_not(is_high))(assemble)
    else:
        assemble()
    inputs = kept[:, COL_X : COL_X + D]
    stores = []

    def store(index, start, width):
        copy = pltpu.make_async_copy(
            kept.at[:, pl.ds(start, width)],
            kept_out.at[slot, :, pl.ds(start, width)],
            osem.at[index],
        )
        copy.start()
        stores.append(copy)

    hat, _ = normalized(inputs.astype(f32))
    kept[:, COL_A : COL_A + D] = (hat * vec_ref[:, V_G1 : V_G1 + D] + vec_ref[:, V_C1 : V_C1 + D]).astype(bf16)
    kept[:, COL_B : COL_B + D] = (hat * vec_ref[:, V_G2 : V_G2 + D] + vec_ref[:, V_C2 : V_C2 + D]).astype(bf16)
    weights.wait(0)
    weights.start(1, 2, 3)
    for part in range(3):
        at = part * D
        proj = nn(kept[:, COL_A : COL_A + D], wqkv[:, at : at + D])
        proj = proj + vec_ref[:, V_QKV + at : V_QKV + at + D]
        if part == 2:
            kept[:, COL_QKV + at : COL_QKV + at + D] = proj.astype(bf16)
        else:
            for p in range(D // PAIR):
                u = proj[:, p * PAIR : (p + 1) * PAIR]
                turned = (
                    u * cos_ref[...]
                    + pltpu.roll(u, PAIR - ROT // 2, 1) * sa_ref[...]
                    + pltpu.roll(u, ROT // 2, 1) * sb_ref[...]
                )
                kept[:, COL_QKV + at + p * PAIR : COL_QKV + at + (p + 1) * PAIR] = turned.astype(bf16)
    store(0, COL_QKV, 3 * D)
    store(1, COL_X, D)
    lse[HEADS:LSE_ROWS, :] = jnp.zeros((LSE_ROWS - HEADS, length), f32)

    scales = head_masks(1.0 / math.sqrt(HEAD))
    lane = lax.broadcasted_iota(jnp.int32, (1, PAIR), 1)
    k_at = lax.broadcasted_iota(jnp.int32, (QROWS, QROWS), 0)
    q_at = lax.broadcasted_iota(jnp.int32, (QROWS, QROWS), 1)

    def attend(p, carry):
        lanes = pl.multiple_of(p * PAIR, PAIR)
        for tile in range(length // QROWS):
            rows = pl.ds(tile * QROWS, QROWS)
            keys = (tile + 1) * QROWS
            q = kept[rows, pl.ds(COL_QKV + lanes, PAIR)]
            k = kept[pl.ds(0, keys), pl.ds(COL_QKV + D + lanes, PAIR)]
            v = kept[pl.ds(0, keys), pl.ds(COL_QKV + 2 * D + lanes, PAIR)]
            outs = []
            for side in range(2):
                s = nt(k, q * scales[side])
                near = jnp.where(k_at <= q_at, s[keys - QROWS :, :], -1e30)
                s = jnp.concatenate([s[: keys - QROWS, :], near], axis=0) if tile else near
                peak = jnp.max(s, axis=0, keepdims=True)
                expo = jnp.exp(s - peak)
                total = jnp.sum(expo, axis=0, keepdims=True)
                soft = (expo * (1.0 / total)).astype(bf16)
                outs.append(tn(soft, v))
                lse[pl.ds(2 * p + side, 1), rows] = peak + jnp.log(total)
            mixed = jnp.where(lane < HEAD, outs[0], outs[1])
            kept[rows, pl.ds(COL_O + lanes, PAIR)] = mixed.astype(bf16)
        return carry

    lax.fori_loop(0, HEADS // 2, attend, 0)
    weights.wait(1)
    out = kept[:, COL_X : COL_X + D].astype(f32) + (nn(kept[:, COL_O : COL_O + D], wo[...]) + vec_ref[:, V_O : V_O + D])
    store(2, COL_A, 3 * D)
    weights.wait(2)
    weights.wait(3)
    branch = jnp.zeros((length, D), f32) + vec_ref[:, V_B2 : V_B2 + D]
    for c in range(0, FF, CHUNK):
        h = nn(kept[:, COL_B : COL_B + D], w1[:, c : c + CHUNK]) + vec_ref[:, V_B1 + c : V_B1 + c + CHUNK]
        act, slope = gelu_both(h)
        kept[:, COL_H + c : COL_H + c + CHUNK] = act.astype(bf16)
        kept[:, COL_GP + c : COL_GP + c + CHUNK] = slope.astype(bf16)
        branch = branch + nn(kept[:, COL_H + c : COL_H + c + CHUNK], w2[c : c + CHUNK, :])
        store(5 + 2 * (c // CHUNK), COL_H + c, CHUNK)
        store(6 + 2 * (c // CHUNK), COL_GP + c, CHUNK)
    out = out + branch
    xo[...] = out
    xb_ref[...] = out.astype(bf16)
    tails = [
        pltpu.make_async_copy(xo, xo_out.at[slot], osem.at[3]),
        pltpu.make_async_copy(lse, lse_out.at[slot], osem.at[4]),
    ]
    for copy in tails:
        copy.start()
    hat, _ = normalized(out)
    final = (hat * fin_ref[:, :D] + fin_ref[:, D : 2 * D]).astype(bf16)
    red_ref[0:1, :] = jnp.sum(hat, axis=0, keepdims=True)
    red_ref[1:2, :] = jnp.sum(final.astype(f32), axis=0, keepdims=True)
    red_ref[2:8, :] = jnp.zeros((6, D), f32)
    for copy in stores + tails:
        copy.wait()


def forward(tick, meta, order, parts, unit, recv, vec, fin, tables, shards, state, slots):
    length = tables[0].shape[0]
    count = len(shards)
    first, handed = state is None, recv is not None
    whole = pl.BlockSpec(memory_space=pltpu.VMEM)
    anywhere = pl.BlockSpec(memory_space=pl.ANY)
    kept_shape = (
        jax.ShapeDtypeStruct((slots, length, KEPT), bf16),
        jax.ShapeDtypeStruct((slots, length, D), f32),
        jax.ShapeDtypeStruct((slots, LSE_ROWS, length), f32),
    )
    operands = [meta, order, vec, fin, *tables]
    if handed:
        operands.append(recv)
    operands += parts
    before = len(operands)
    operands = operands + [*shards] + ([] if first else list(state))
    return pl.pallas_call(
        functools.partial(forward_kernel, tick, unit, len(parts), count, first, handed),
        out_shape=(
            jax.ShapeDtypeStruct((length, D), bf16),
            jax.ShapeDtypeStruct((8, D), f32),
            *kept_shape,
        ),
        in_specs=[pl.BlockSpec(memory_space=pltpu.SMEM)]
        + [whole] * 6
        + [anywhere] * (len(operands) - 7),
        out_specs=(whole, whole, anywhere, anywhere, anywhere),
        input_output_aliases={} if first else {before + count + i: 2 + i for i in range(3)},
        scratch_shapes=[
            pltpu.VMEM((D, 3 * D), bf16),
            pltpu.VMEM((D, D), bf16),
            pltpu.VMEM((D, FF), bf16),
            pltpu.VMEM((FF, D), bf16),
            pltpu.VMEM((length, KEPT), bf16),
            pltpu.VMEM((length, D), f32),
            pltpu.VMEM((LSE_ROWS, length), f32),
            pltpu.VMEM((len(parts), length, parts[0].shape[1]), bf16),
            pltpu.SemaphoreType.DMA((len(PLACES),)),
            pltpu.SemaphoreType.DMA((len(parts),)),
            pltpu.SemaphoreType.DMA((5 + 2 * (FF // CHUNK),)),
        ],
        compiler_params=pltpu.CompilerParams(vmem_limit_bytes=VMEM_LIMIT),
        cost_estimate=pl.CostEstimate(flops=10 * 10**9, bytes_accessed=30 * 10**6, transcendentals=5 * 10**6),
        name="layer_forward",
    )(*operands)


def backward_kernel(tick, units, shard_count, handed, back_in, back_out, *refs):
    meta_ref, flag_ref, order_ref, vec_ref, fin_ref, cos_ref, sa_ref, sb_ref = refs[:8]
    if handed:
        recv_ref, *refs = refs[8:]
    else:
        refs = refs[8:]
    shards = refs[:shard_count]
    kept_in, xo_in, lse_in = refs[shard_count : 3 + shard_count]
    rest = refs[3 + shard_count + back_in :]
    dx_ref, vg_ref, kept_out = rest[:3]
    backs, rest = rest[3 : 3 + back_out], rest[3 + back_out :]
    wqkv, wo, w1, w2, qkv, gp, x, xo, lse, grads, dmix, dq, dk, dv, turned, wsem, isem, osem, bsem = rest
    mats = (wqkv, wo, w1, w2)
    length = cos_ref.shape[0]
    slot = meta_ref[1 + units + 2 + tick]
    weights = Weights(meta_ref[0], shards, mats, wsem)
    loads = [
        pltpu.make_async_copy(xo_in.at[slot], xo, isem.at[0]),
        pltpu.make_async_copy(kept_in.at[slot, :, pl.ds(COL_GP, FF)], gp, isem.at[1]),
        pltpu.make_async_copy(kept_in.at[slot, :, pl.ds(COL_X, D)], x, isem.at[2]),
        pltpu.make_async_copy(kept_in.at[slot, :, pl.ds(COL_QKV, 3 * D)], qkv, isem.at[3]),
        pltpu.make_async_copy(lse_in.at[slot], lse, isem.at[4]),
    ]
    loads[0].start()
    weights.start(1)
    loads[3].start()
    loads[4].start()
    loads[0].wait()
    hat, scale = normalized(xo[...])
    headed = fin_ref[:, 2 * D : 3 * D] * fin_ref[:, :D]
    top = flag_ref[min(tick, units - 1)] * norm_back(1.0, headed, hat, scale)
    if handed:
        top = jnp.where(meta_ref[0] >= 2, top, recv_ref[...].astype(f32))
    xo[...] = top
    grads[:, COL_G : COL_G + D] = xo[...].astype(bf16)
    bias = jnp.sum(grads[:, COL_G : COL_G + D].astype(f32), axis=0, keepdims=True)
    vg_ref[:, V_O : V_O + D] = bias
    vg_ref[:, V_B2 : V_B2 + D] = bias

    weights.wait(1)
    dmix[...] = nt(grads[:, COL_G : COL_G + D], wo[...]).astype(bf16)
    loads[3].wait()
    loads[4].wait()
    weights.start(3)
    loads[1].start()
    weights.start(2)
    loads[2].start()
    weights.start(0)
    scales = head_masks(1.0 / math.sqrt(HEAD))
    ones = head_masks(1.0)
    k_at = lax.broadcasted_iota(jnp.int32, (QROWS, QROWS), 0)
    q_at = lax.broadcasted_iota(jnp.int32, (QROWS, QROWS), 1)

    def attend(p, carry):
        lanes = pl.multiple_of(p * PAIR, PAIR)
        for tile in range(length // QROWS):
            rows = pl.ds(tile * QROWS, QROWS)
            keys = (tile + 1) * QROWS
            q = qkv[rows, pl.ds(lanes, PAIR)]
            k = qkv[pl.ds(0, keys), pl.ds(D + lanes, PAIR)]
            v = qkv[pl.ds(0, keys), pl.ds(2 * D + lanes, PAIR)]
            dm = dmix[rows, pl.ds(lanes, PAIR)]
            dq_sum = dk_sum = dv_sum = None
            for side in range(2):
                qs = q * scales[side]
                ks = k * scales[side]
                dms = dm * ones[side]
                s = nt(k, qs)
                soft = jnp.exp(s - lse[pl.ds(2 * p + side, 1), rows])
                near = jnp.where(k_at <= q_at, soft[keys - QROWS :, :], 0.0)
                soft = jnp.concatenate([soft[: keys - QROWS, :], near], axis=0) if tile else near
                dsoft = nt(v, dms)
                centre = jnp.sum(soft * dsoft, axis=0, keepdims=True)
                ds = (soft * (dsoft - centre)).astype(bf16)
                one_dv = nn(soft.astype(bf16), dms)
                one_dk = nn(ds, qs)
                one_dq = tn(ds, ks)
                if side:
                    dq_sum, dk_sum, dv_sum = dq_sum + one_dq, dk_sum + one_dk, dv_sum + one_dv
                else:
                    dq_sum, dk_sum, dv_sum = one_dq, one_dk, one_dv
            dq[rows, :] = dq_sum
            if tile:
                old = pl.ds(0, tile * QROWS)
                new = pl.ds(tile * QROWS, QROWS)
                dk[old, :] = dk[old, :] + dk_sum[: tile * QROWS]
                dk[new, :] = dk_sum[tile * QROWS :]
                dv[old, :] = dv[old, :] + dv_sum[: tile * QROWS]
                dv[new, :] = dv_sum[tile * QROWS :]
            else:
                dk[rows, :] = dk_sum
                dv[rows, :] = dv_sum
        for part, ref in ((0, dq), (1, dk)):
            g = ref[...]
            turned = (
                g * cos_ref[...]
                - pltpu.roll(g, PAIR - ROT // 2, 1) * sa_ref[...]
                - pltpu.roll(g, ROT // 2, 1) * sb_ref[...]
            )
            grads[:, pl.ds(COL_DP + part * D + lanes, PAIR)] = turned.astype(bf16)
        grads[:, pl.ds(COL_DP + 2 * D + lanes, PAIR)] = dv[...].astype(bf16)
        return carry

    lax.fori_loop(0, HEADS // 2, attend, 0)
    stores = [
        pltpu.make_async_copy(
            grads.at[:, pl.ds(COL_DP, 3 * D)], kept_out.at[slot, :, pl.ds(COL_QKV, 3 * D)], osem.at[2]
        )
    ]
    stores[0].start()
    weights.wait(3)
    loads[1].wait()
    loads[2].wait()
    weights.wait(2)
    second = jnp.zeros((length, D), f32)
    for c in range(0, FF, CHUNK):
        act = nt(grads[:, COL_G : COL_G + D], w2[c : c + CHUNK, :])
        pre = (act * gp[:, c : c + CHUNK].astype(f32)).astype(bf16)
        grads[:, COL_DH + c : COL_DH + c + CHUNK] = pre
        vg_ref[:, V_B1 + c : V_B1 + c + CHUNK] = jnp.sum(pre.astype(f32), axis=0, keepdims=True)
        second = second + nt(pre, w1[:, c : c + CHUNK])
    hat, scale = normalized(x[...].astype(f32))
    vg_ref[:, V_G2 : V_G2 + D] = jnp.sum(second * hat, axis=0, keepdims=True)
    vg_ref[:, V_C2 : V_C2 + D] = jnp.sum(second, axis=0, keepdims=True)
    xo[...] = xo[...] + norm_back(second, vec_ref[:, V_G2 : V_G2 + D], hat, scale)
    stores += [
        pltpu.make_async_copy(
            grads.at[:, pl.ds(COL_G, D)], kept_out.at[slot, :, pl.ds(COL_X, D)], osem.at[0]
        ),
        pltpu.make_async_copy(
            grads.at[:, pl.ds(COL_DH, FF)], kept_out.at[slot, :, pl.ds(COL_GP, FF)], osem.at[1]
        ),
    ]
    stores[1].start()
    stores[2].start()

    vg_ref[:, V_QKV : V_QKV + 3 * D] = jnp.sum(
        grads[:, COL_DP : COL_DP + 3 * D].astype(f32), axis=0, keepdims=True
    )
    weights.wait(0)
    one = nt(grads[:, COL_DP : COL_DP + 3 * D], wqkv[...])
    hat, scale = normalized(x[...].astype(f32))
    vg_ref[:, V_G1 : V_G1 + D] = jnp.sum(one * hat, axis=0, keepdims=True)
    vg_ref[:, V_C1 : V_C1 + D] = jnp.sum(one, axis=0, keepdims=True)
    total = xo[...] + norm_back(one, vec_ref[:, V_G1 : V_G1 + D], hat, scale)
    dx_ref[...] = total.astype(bf16)
    if back_out:
        turned[...] = nt(order_ref[...], dx_ref[...]).astype(bf16)
        start = (tick - 2) * length if tick <= units else 0
        width = backs[0].shape[0]
        for k, back in enumerate(backs):
            copy = pltpu.make_async_copy(
                turned.at[pl.ds(k * width, width)], back.at[:, pl.ds(start, length)], bsem.at[k]
            )
            copy.start()
            stores.append(copy)
    for copy in stores:
        copy.wait()


def backward(tick, units, meta, flags, order, recv, vec, fin, tables, shards, state, backs):
    length = tables[0].shape[0]
    count = len(shards)
    handed = recv is not None
    chips = len(PLACES) // shards[0].shape[0]
    spans = 0 if tick < 2 else (units - 1 if tick <= units else 1)
    back_shapes = [jax.ShapeDtypeStruct((D // chips, spans * length), bf16)] * (chips if spans else 0)
    whole = pl.BlockSpec(memory_space=pltpu.VMEM)
    anywhere = pl.BlockSpec(memory_space=pl.ANY)
    small = pl.BlockSpec(memory_space=pltpu.SMEM)
    operands = [meta, flags, order, vec, fin, *tables]
    if handed:
        operands.append(recv)
    dense = len(operands)
    operands = operands + [*shards, *state, *backs]
    aliases = {dense + count: 2} | {dense + count + 3 + i: 3 + i for i in range(len(backs))}
    return pl.pallas_call(
        functools.partial(backward_kernel, tick, units, count, handed, len(backs), len(back_shapes)),
        out_shape=(
            jax.ShapeDtypeStruct((length, D), bf16),
            jax.ShapeDtypeStruct((1, V_END), f32),
            jax.ShapeDtypeStruct(state[0].shape, bf16),
            *back_shapes,
        ),
        in_specs=[small, small] + [whole] * (dense - 2) + [anywhere] * (len(operands) - dense),
        out_specs=(whole, whole, anywhere) + (anywhere,) * len(back_shapes),
        input_output_aliases=aliases,
        scratch_shapes=[
            pltpu.VMEM((D, 3 * D), bf16),
            pltpu.VMEM((D, D), bf16),
            pltpu.VMEM((D, FF), bf16),
            pltpu.VMEM((FF, D), bf16),
            pltpu.VMEM((length, 3 * D), bf16),
            pltpu.VMEM((length, FF), bf16),
            pltpu.VMEM((length, D), bf16),
            pltpu.VMEM((length, D), f32),
            pltpu.VMEM((LSE_ROWS, length), f32),
            pltpu.VMEM((length, GRADS), bf16),
            pltpu.VMEM((length, D), bf16),
            pltpu.VMEM((length, PAIR), f32),
            pltpu.VMEM((length, PAIR), f32),
            pltpu.VMEM((length, PAIR), f32),
            pltpu.VMEM((D, length), bf16),
            pltpu.SemaphoreType.DMA((len(PLACES),)),
            pltpu.SemaphoreType.DMA((5,)),
            pltpu.SemaphoreType.DMA((3,)),
            pltpu.SemaphoreType.DMA((chips,)),
        ],
        compiler_params=pltpu.CompilerParams(vmem_limit_bytes=VMEM_LIMIT),
        cost_estimate=pl.CostEstimate(flops=20 * 10**9, bytes_accessed=40 * 10**6, transcendentals=5 * 10**6),
        name="layer_backward",
    )(*operands)


def product_kernel(left_at, right_at, count_ref, x_ref, y_ref, *refs):
    sent_ref = refs[0] if len(refs) == 4 else None
    out_ref, square_ref, turned = refs[-3:] if sent_ref is not None else (refs[0], None, refs[1])
    units, rows, width = x_ref.shape
    step = pl.program_id(0)
    before = left_at[jnp.maximum(step - 1, 0)]

    @pl.when(jnp.logical_or(step == 0, left_at[step] != before))
    def _():
        for unit in range(units):
            turned[:, unit * rows : (unit + 1) * rows] = jnp.transpose(x_ref[unit])

    found = nn(turned[...], y_ref[...].reshape(units * rows, -1))
    if sent_ref is None:
        for i in range(out_ref.shape[0]):
            out_ref[i] = found[:, i * TILE : (i + 1) * TILE]
        return

    @pl.when(step == 0)
    def _():
        square_ref[...] = jnp.zeros_like(square_ref)

    for i in range(out_ref.shape[0]):
        whole = found[:, i * TILE : (i + 1) * TILE] + sent_ref[i]
        out_ref[i] = whole.astype(bf16)
        weight = count_ref[step * out_ref.shape[0] + i].astype(f32)
        square_ref[...] += weight * jnp.sum(whole * whole, axis=0, keepdims=True)


def products(left_at, right_at, counted, kept, units, each, sent=None):
    steps = left_at.shape[0]
    length = kept.shape[1]
    block = pl.BlockSpec((each, TILE, TILE), lambda i, a, b, c: (i, 0, 0))
    shape = (steps * each, TILE, TILE)
    if sent is None:
        out_shape, out_specs, more = jax.ShapeDtypeStruct(shape, f32), block, []
    else:
        out_shape = (jax.ShapeDtypeStruct(shape, bf16), jax.ShapeDtypeStruct((1, TILE), f32))
        out_specs, more = (block, pl.BlockSpec((1, TILE), lambda i, a, b, c: (0, 0))), [sent]
    return pl.pallas_call(
        product_kernel,
        out_shape=out_shape,
        grid_spec=pltpu.PrefetchScalarGridSpec(
            num_scalar_prefetch=3,
            grid=(steps,),
            in_specs=[
                pl.BlockSpec((units, length, TILE), lambda i, a, b, c: (0, 0, a[i])),
                pl.BlockSpec((units, length, each * TILE), lambda i, a, b, c: (0, 0, b[i])),
            ]
            + [block] * len(more),
            out_specs=out_specs,
            scratch_shapes=[pltpu.VMEM((TILE, units * length), bf16)],
        ),
        compiler_params=pltpu.CompilerParams(vmem_limit_bytes=VMEM_LIMIT),
        cost_estimate=LIGHT,
        name="weight_products",
    )(left_at, right_at, counted, kept, kept, *more)


def lookup_kernel(ids_ref, embedding_ref, first_ref, rest_ref, table, wide):
    step = pl.program_id(0)
    features = embedding_ref.shape[0]
    lanes = table.shape[1]
    tiles = embedding_ref.shape[1] // lanes
    tokens = wide.shape[0]

    def turn(i):
        tile = embedding_ref[:, pl.ds(pl.multiple_of(i * lanes, lanes), lanes)]
        table[pl.ds(pl.multiple_of((step * tiles + i) * lanes, lanes), lanes), :features] = jnp.transpose(tile)

    def several(i, carry):
        for j in range(8):
            turn(i * 8 + j)
        return carry

    lax.fori_loop(0, tiles // 8, several, 0)
    for i in range(tiles // 8 * 8, tiles):
        turn(i)

    @pl.when(step == pl.num_programs(0) - 1)
    def _():
        def fetch(i, carry):
            for j in range(16):
                wide[pl.ds(i * 16 + j, 1), :] = table[pl.ds(ids_ref[i * 16 + j], 1), :]
            return carry

        lax.fori_loop(0, tokens // 16, fetch, 0)
        first = first_ref.shape[0]
        first_ref[...] = wide[:first, :features].astype(bf16)
        rest_ref[...] = wide[first:, :features].astype(bf16)


def lookup(ids, embedding, first):
    features, vocab = embedding.shape
    tokens = ids.shape[0]
    lanes = 128
    steps = 3 if vocab % (3 * lanes) == 0 else 1
    whole = lambda i: (0, 0)
    return pl.pallas_call(
        lookup_kernel,
        out_shape=(
            jax.ShapeDtypeStruct((first, features), bf16),
            jax.ShapeDtypeStruct((tokens - first, features), bf16),
        ),
        grid=(steps,),
        in_specs=[
            pl.BlockSpec(memory_space=pltpu.SMEM),
            pl.BlockSpec((features, vocab // steps), lambda i: (0, i)),
        ],
        out_specs=(
            pl.BlockSpec((first, features), whole),
            pl.BlockSpec((tokens - first, features), whole),
        ),
        scratch_shapes=[pltpu.VMEM((vocab, lanes), f32), pltpu.VMEM((tokens, lanes), f32)],
        compiler_params=pltpu.CompilerParams(vmem_limit_bytes=VMEM_LIMIT),
        cost_estimate=LIGHT,
        name="table_lookup",
    )(ids, embedding)


def table_kernel(ids_ref, *refs):
    parts = refs[:-5]
    out_ref, square_ref, table, wide, total = refs[-5:]
    step = pl.program_id(0)
    features = out_ref.shape[0]
    tokens = wide.shape[0]
    vocab, lanes = table.shape
    tiles = out_ref.shape[1] // lanes

    @pl.when(step == 0)
    def _():
        def clear(i, carry):
            table[pl.ds(pl.multiple_of(i * 3 * lanes, lanes), 3 * lanes), :] = jnp.zeros((3 * lanes, lanes), f32)
            return carry

        lax.fori_loop(0, vocab // (3 * lanes), clear, 0)
        total[...] = jnp.zeros_like(total)
        if features < lanes:
            wide[:, features:] = jnp.zeros((tokens, lanes - features), f32)
        start = 0
        for part in parts:

            def upright(i, carry, part=part, start=start):
                tile = part[:, pl.ds(pl.multiple_of(i * lanes, lanes), lanes)].astype(f32)
                wide[pl.ds(pl.multiple_of(start + i * lanes, lanes), lanes), :features] = jnp.transpose(tile)
                return carry

            lax.fori_loop(0, part.shape[1] // lanes, upright, 0)
            start += part.shape[1]

        def add(i, carry):
            for j in range(16):
                row = pl.ds(ids_ref[i * 16 + j], 1)
                table[row, :] = table[row, :] + wide[pl.ds(i * 16 + j, 1), :]
            return carry

        lax.fori_loop(0, tokens // 16, add, 0)

    def turn(i):
        tile = table[pl.ds(pl.multiple_of((step * tiles + i) * lanes, lanes), lanes), :]
        total[...] += tile * tile
        out_ref[:, pl.ds(pl.multiple_of(i * lanes, lanes), lanes)] = jnp.transpose(tile)[:features]

    def several(i, carry):
        for j in range(8):
            turn(i * 8 + j)
        return carry

    lax.fori_loop(0, tiles // 8, several, 0)
    for i in range(tiles // 8 * 8, tiles):
        turn(i)

    @pl.when(step == pl.num_programs(0) - 1)
    def _():
        square_ref[...] = jnp.sum(total[...], axis=0, keepdims=True)


def table_gradient(ids, parts, vocab):
    tokens, features = ids.shape[0], parts[0].shape[0]
    lanes = 128
    steps = 3 if vocab % (3 * lanes) == 0 else 1
    return pl.pallas_call(
        table_kernel,
        out_shape=(jax.ShapeDtypeStruct((features, vocab), f32), jax.ShapeDtypeStruct((1, lanes), f32)),
        grid=(steps,),
        in_specs=[
            pl.BlockSpec(memory_space=pltpu.SMEM),
        ]
        + [pl.BlockSpec(part.shape, lambda i: (0, 0), pipeline_mode=pl.Buffered(1)) for part in parts],
        out_specs=(
            pl.BlockSpec((features, vocab // steps), lambda i: (0, i)),
            pl.BlockSpec((1, lanes), lambda i: (0, 0)),
        ),
        scratch_shapes=[
            pltpu.VMEM((vocab, lanes), f32),
            pltpu.VMEM((tokens, lanes), f32),
            pltpu.VMEM((lanes, lanes), f32),
        ],
        compiler_params=pltpu.CompilerParams(vmem_limit_bytes=VMEM_LIMIT),
        cost_estimate=LIGHT,
        name="table_gradient",
    )(ids, *parts)


def split(value):
    high = value.astype(bf16)
    return high, (value - high.astype(f32)).astype(bf16)


def shampoo_kernel(factor_ref, g_ref, w_ref, ls_ref, rs_ref, lr_ref, rr_ref, bg_ref, nw_ref, nl_ref, nr_ref):
    factor = factor_ref[0]
    level = (1.0 - stats_decay) * factor * factor
    for i in range(g_ref.shape[0]):
        g = g_ref[i]
        bg_ref[i] = g.astype(f32) * factor
        nl_ref[i] = stats_decay * ls_ref[i] + level * nt(g, g)
        nr_ref[i] = stats_decay * rs_ref[i] + level * tn(g, g)
        right_high, right_low = split(rr_ref[i])
        inner = nn(g, right_high) + nn(g, right_low)
        inner_high, inner_low = split(inner)
        left_high, left_low = split(lr_ref[i])
        direction = nn(left_high, inner_high) + (nn(left_high, inner_low) + nn(left_low, inner_high))
        nw_ref[i] = w_ref[i] - (shampoo_rate * factor) * direction


def shampoo(factor, grad, weights, left_stats, right_stats, left_root, right_root):
    count = grad.shape[0]
    each = max(i for i in (1, 2, 3) if count % i == 0)
    block = pl.BlockSpec((each, TILE, TILE), lambda i: (i, 0, 0))
    shape = jax.ShapeDtypeStruct((count, TILE, TILE), f32)
    return pl.pallas_call(
        shampoo_kernel,
        out_shape=(shape,) * 4,
        grid=(count // each,),
        in_specs=[pl.BlockSpec(memory_space=pltpu.SMEM)] + [block] * 6,
        out_specs=(block,) * 4,
        compiler_params=pltpu.CompilerParams(vmem_limit_bytes=VMEM_LIMIT),
        cost_estimate=LIGHT,
        name="shampoo",
    )(factor, grad, weights, left_stats, right_stats, left_root, right_root)


def rope_columns(length):
    half_rot = ROT // 2
    lanes = jnp.arange(PAIR) % HEAD
    index = jnp.where(lanes < half_rot, lanes, lanes - half_rot).astype(f32)
    inverse = rope_base ** (-2.0 * index / ROT)
    angles = jnp.arange(length)[:, None].astype(f32) * inverse[None, :]
    cosine = jnp.where(lanes < ROT, jnp.cos(angles), 1.0)
    sine = jnp.where(lanes < ROT, jnp.sin(angles), 0.0)
    first = jnp.where(lanes < half_rot, -sine, 0.0)
    second = jnp.where(lanes < half_rot, 0.0, sine)
    return cosine, first, second


def adam_step(weight, moment, second, grad, rate, decay):
    moment_new = beta_first * moment + (1.0 - beta_first) * grad
    second_new = beta_second * second + (1.0 - beta_second) * grad * grad
    corrected = moment_new / (1.0 - beta_first**STEP)
    scaled = jnp.sqrt(second_new / (1.0 - beta_second**STEP)) + adam_eps
    return (moment_new, second_new, weight - rate * (corrected / scaled + decay * weight))


def rounded(values):
    return lax.reduce_precision(values, 8, 7)


def chosen(flags, values):
    total = values[-1]
    for flag, value in zip(flags[:-1], values[:-1]):
        total = jnp.where(flag, value, total)
    return total


def ordered(section, mine, other, axis):
    return jnp.concatenate(
        [jnp.where(section == 0, mine, other), jnp.where(section == 0, other, mine)], axis=axis
    )


def swapped(value):
    return lax.ppermute(value, "section", [(0, 1), (1, 0)])


def local(
    tokens,
    margins,
    tie_flags,
    embedding,
    embed_moment,
    embed_second,
    layer_blocks,
    left_stats,
    right_stats,
    left_root,
    right_root,
    layer_vectors,
    vector_moment,
    vector_second,
    closing_vectors,
    final_moment,
    final_second,
):
    both = ("section", "dp")
    count = lax.axis_size("dp")
    section = lax.axis_index("section")
    place = lax.axis_index("dp")
    low, high = count // 2 - 1, count // 2
    is_high = place >= high
    order_low = list(range(count - 1, low, -1)) + list(range(low + 1))
    order_high = [count - 1 - k for k in order_low]
    length = tokens.shape[2]
    units = tokens.shape[0] * count
    own_blocks = layer_blocks.shape[1]
    own_vector = layer_vectors.shape[1]
    own_final = closing_vectors.shape[0]
    features, vocab = embedding.shape

    own_closing = rounded(closing_vectors)
    pack = jnp.concatenate(
        [
            tokens.reshape(-1).astype(f32),
            margins.astype(f32),
            tie_flags.astype(f32),
            rounded(layer_vectors[0]),
            own_closing,
        ]
    )
    passed = [pack] + [
        lax.ppermute(pack, "dp", [(i, (i + d) % count) for i in range(count)]) for d in range(1, count)
    ]
    packs = jnp.stack(passed)

    own, packs = lax.optimization_barrier((layer_blocks[0].astype(bf16), packs))
    rounds = arrivals(count)
    received = []
    for pair in rounds:
        route = []
        for side, shard in enumerate(pair):
            route.append((shard, side * count + low))
            route.append((count + count - 1 - shard, (1 - side) * count + high))
        received.append(lax.ppermute(own, both, route))

    packs = packs[(place - jnp.arange(count)) % count]
    at = tokens.size
    ids = packs[:, :at].astype(jnp.int32).reshape(2, units, length)
    pair_margins = packs[:, at : at + margins.size].reshape(-1)
    at = at + margins.size
    pair_ties = packs[:, at : at + margins.size].reshape(-1)
    at = at + margins.size
    other_packs = swapped(packs[:, at:])
    layer_packs = jnp.where((section == 1) == is_high, packs[:, at:], other_packs)
    vec = layer_packs[:, :own_vector].reshape(1, -1)
    fin = ordered(section, packs[:, at + own_vector :], other_packs[:, own_vector:], 0).reshape(1, -1)
    tables = rope_columns(length)

    ids_here = jnp.where(section == 0, ids, ids[::-1])
    looked = lookup(
        jnp.concatenate([ids_here[:, :1].reshape(-1), ids_here[:, 1:].reshape(-1)]), embedding, 2 * length
    )

    def joined(rows):
        half = rows.shape[0] // 2
        return ordered(section, rows[:half], swapped(rows[half:]), 1)

    def sent_on(rows):
        return [rows if k == low else lax.ppermute(rows, "dp", [(k, low)]) for k in range(count)]

    looked = [joined(rows) for rows in looked]
    first = sent_on(looked[0])
    slot_at = jnp.arange(D)
    chip, within = slot_at // (2 * features), slot_at % (2 * features)
    feature_at = within // features * (D // 2) + chip * features + within % features
    order = (feature_at[:, None] == jnp.arange(D)[None, :]).astype(bf16)
    first, later, received, vec, fin, tables, order = lax.optimization_barrier(
        (first, looked[1], received, vec, fin, tables, order)
    )
    relays = [
        lax.ppermute(
            array, both, [(low, count + low), (count + low, low), (high, count + high), (count + high, high)]
        )
        for array in [own, *received]
    ]
    later, relays[-1] = lax.optimization_barrier((later, relays[-1]))
    later = sent_on(later)
    shards = [*received, *relays[1:], own, relays[0]]
    role = is_high * 2 + ((section == 1) == is_high) * 1

    slots = units + 1
    early = [*range(units), units, units]
    late = [units, units, *range(units)]
    meta = jnp.where(is_high, jnp.array([0, *late, *early]), jnp.array([0, *early, *late])).at[0].set(role)
    meta = meta.astype(jnp.int32)
    state = None
    arrived = []
    sums = []
    for tick in range(units + 2):
        unit = min(tick, units - 1)
        result, tail, *state = forward(
            tick,
            meta,
            order,
            later if unit else first,
            max(unit - 1, 0),
            arrived[tick - 2] if tick >= 2 else None,
            vec,
            fin,
            tables,
            shards,
            state,
            slots,
        )
        if tick < units:
            arrived.append(lax.ppermute(result, "dp", [(low, high)]))
        if tick >= 2:
            sums.append(tail[:2])
    sums = jnp.stack(sums)
    sum_hat, sum_final = sums[:, 0], sums[:, 1]
    final_gain, head = fin[0, :D], fin[0, 2 * D :]
    rewards = (jnp.sum(sum_final * head, axis=1) / length).reshape(-1, 2)
    pairs = units // 2
    gap = rewards[:, 0] - rewards[:, 1]
    half_margin = 0.5 * lax.dynamic_slice_in_dim(pair_margins, section * pairs, pairs, 0)
    tie = lax.dynamic_slice_in_dim(pair_ties, section * pairs, pairs, 0)
    pair_loss = (1.0 - tie) * jax.nn.softplus(half_margin - gap) + tie * 0.5 * (
        jax.nn.softplus(gap) + jax.nn.softplus(-gap)
    )
    gap_grad = -(1.0 - tie) * jax.nn.sigmoid(half_margin - gap) + tie * 0.5 * (
        jax.nn.sigmoid(gap) - jax.nn.sigmoid(-gap)
    )
    reward_grad = (jnp.stack([gap_grad, -gap_grad], axis=1) / length).reshape(-1)
    final_local = jnp.concatenate(
        [
            head * jnp.sum(reward_grad[:, None] * sum_hat, axis=0),
            head * (length * jnp.sum(reward_grad)),
            jnp.sum(reward_grad[:, None] * sum_final, axis=0),
        ]
    )

    def returned(parts):
        return chosen(
            [place == k for k in range(count)],
            [part if k == low else lax.ppermute(part, "dp", [(low, k)]) for k, part in enumerate(parts)],
        )

    def own_features(both_cores):
        mine, other = both_cores[:features], both_cores[features:]
        return [jnp.where(section == 0, mine, other), swapped(jnp.where(section == 0, other, mine))]

    arrived = []
    vector_sum = jnp.zeros((1, V_END), f32)
    backs = []
    token_grads = []
    for tick in range(units + 2):
        if tick == units + 1:
            token_grads.append(returned(backs))
            backs = []
        grad_in, vector_part, state[0], *backs = backward(
            tick,
            units,
            meta,
            reward_grad,
            order,
            arrived[tick - 2] if tick >= 2 else None,
            vec,
            fin,
            tables,
            shards,
            state,
            backs,
        )
        if tick < units:
            arrived.append(lax.ppermute(grad_in, "dp", [(high, low)]))
        live = jnp.where(is_high, tick < units, tick >= 2)
        vector_sum = vector_sum + jnp.where(live, vector_part, 0.0)
    token_grads.append(returned(backs))

    vector_pack = jnp.concatenate([vector_sum[0], jnp.where(place == high, final_local, 0.0)])
    vector_pack = vector_pack + swapped(vector_pack)
    own_rows = own_vector + own_final
    extra = -(-2 * own_rows // (16 * TILE)) * 16

    def vector_rows(k):
        values = jnp.concatenate(
            [
                lax.dynamic_slice_in_dim(vector_pack, k * own_vector, own_vector, 0),
                lax.dynamic_slice_in_dim(vector_pack, V_END + (section * count + k) * own_final, own_final, 0),
            ]
        )
        top = rounded(values)
        halves = jnp.concatenate([top.astype(bf16), (values - top).astype(bf16)])
        return jnp.pad(halves, (0, extra * TILE - 2 * own_rows)).reshape(extra, TILE)

    left_at = jnp.array([(0, 2, 4, 6)[m] + row for m, row, _ in PLACES], jnp.int32)
    right_at = jnp.array([(14, 28, 20, 28)[m] + col for m, _, col in PLACES], jnp.int32)
    part = (own_blocks + 1) // 2
    rest = own_blocks - part
    kept = state[0]
    each = 2 if own_blocks % 4 == 0 else 1

    def tiles_of(shards, half):
        places = jnp.concatenate([shard * own_blocks + half * rest + jnp.arange(0, part, each) for shard in shards])
        return left_at[places], right_at[places] // each

    live = (place == low) | (place == high)
    token_grads[0], left_at = lax.optimization_barrier((token_grads[0], left_at))
    squares = jnp.where(live & (section == 0), jnp.sum(vector_pack * vector_pack), 0.0)
    counted = jnp.where((jnp.arange(part) < part - rest) & (section == 1), 0, 1).astype(jnp.int32)
    group = max(count // 2, 1)
    counted = jnp.concatenate([counted] * group)
    sent, keeping, groups = [], [], []
    for start in range(0, count, group):
        steps = range(start, start + group)
        groups.append([jnp.where(is_high, order_high[step], order_low[step]) for step in steps])
        keeping.append(tiles_of(groups[-1], section))
        sums = products(*tiles_of(groups[-1], 1 - section), counted, kept, units, each)
        left_at, sums = lax.optimization_barrier((left_at, sums))
        sent.append(swapped(sums))
    pieces = []
    for start, shards_here, tiles, others in zip(range(0, count, group), groups, keeping, sent):
        if pieces:
            tiles, pieces = lax.optimization_barrier((tiles, pieces))
        total, block_squares = products(*tiles, counted, kept, units, each, others)
        squares = squares + jnp.where(live, jnp.sum(block_squares), 0.0)
        total = total.reshape(group, part * TILE, TILE)
        pieces += [
            jnp.concatenate([total[i], vector_rows(shard)], axis=0) for i, shard in enumerate(shards_here)
        ]
    for step in range(count - 1):
        route = [
            (core * count + source, core * count + target)
            for core in range(2)
            for source, target in ((low, order_low[step]), (high, order_high[step]))
        ]
        pieces[step] = lax.ppermute(pieces[step], both, route)
    token_grads[1], pieces[-1] = lax.optimization_barrier((token_grads[1], pieces[-1]))
    ids_ordered = jnp.concatenate(
        [ids_here[0, :-1], ids_here[1, :-1], ids_here[0, -1:], ids_here[1, -1:]], axis=0
    ).reshape(-1)
    table_grad, table_squares = table_gradient(
        ids_ordered, own_features(token_grads[0]) + own_features(token_grads[1]), vocab
    )

    loss = jnp.where(place == high, jnp.sum(pair_loss), 0.0)
    square_total, loss_total = lax.psum((squares + jnp.sum(table_squares), loss), both)
    norm_value = jnp.sqrt(square_total)
    factor = clip_limit / jnp.maximum(norm_value, clip_limit)
    embed_m, embed_v, embed_w = adam_step(
        embedding, embed_moment, embed_second, table_grad * factor, embed_rate, embed_decay
    )
    pieces, embed_w = lax.optimization_barrier((pieces, embed_w))
    piece_low = chosen([place == k for k in order_low], pieces)
    piece_high = chosen([place == k for k in order_high], pieces)
    mine = jnp.where(section == 0, piece_low, piece_high)
    other = swapped(jnp.where(section == 0, piece_high, piece_low)[: part * TILE])
    block_part, other = (value.reshape(part, TILE, TILE) for value in (mine[: part * TILE], other))
    grad_blocks = jnp.concatenate(
        [
            jnp.where(section == 0, block_part, other),
            jnp.where(section == 0, other, block_part)[2 * part - own_blocks :],
        ],
        axis=0,
    )

    def vectors_of(piece, start, width):
        rows = piece[part * TILE :].reshape(-1)
        return rows[start : start + width].astype(f32) + rows[own_rows + start : own_rows + start + width].astype(f32)

    owned_vector = vectors_of(mine, 0, own_vector)[None]
    owned_final = vectors_of(piece_high, own_vector, own_final)

    block_grad, new_blocks, new_left, new_right = (
        out[None]
        for out in shampoo(
            factor.reshape(1),
            grad_blocks,
            layer_blocks[0],
            left_stats[0],
            right_stats[0],
            left_root[0],
            right_root[0],
        )
    )
    vector_m, vector_v, vector_w = adam_step(
        layer_vectors, vector_moment, vector_second, owned_vector * factor, vector_rate, 0.0
    )
    final_m, final_v, final_w = adam_step(
        closing_vectors, final_moment, final_second, owned_final * factor, vector_rate, 0.0
    )
    return (
        loss_total.reshape(1),
        norm_value.reshape(1),
        block_grad,
        new_blocks,
        new_left,
        new_right,
        vector_m,
        vector_v,
        vector_w,
        final_m,
        final_v,
        final_w,
        embed_m,
        embed_v,
        embed_w,
    )


def solution(mesh):
    return jax.shard_map(
        local,
        mesh=mesh,
        in_specs=(
            P(("member", "dp"), None, None),
            P(("member", "dp")),
            P(("member", "dp")),
            P(("member", "section", "dp"), None),
            P(("member", "section", "dp"), None),
            P(("member", "section", "dp"), None),
            P(("member", "section"), "dp", None, None),
            P(("member", "section"), "dp", None, None),
            P(("member", "section"), "dp", None, None),
            P(("member", "section"), "dp", None, None),
            P(("member", "section"), "dp", None, None),
            P(("member", "section"), "dp"),
            P(("member", "section"), "dp"),
            P(("member", "section"), "dp"),
            P(("member", "section", "dp")),
            P(("member", "section", "dp")),
            P(("member", "section", "dp")),
        ),
        out_specs=(
            P("member"),
            P("member"),
            P(("member", "section"), "dp", None, None),
            P(("member", "section"), "dp", None, None),
            P(("member", "section"), "dp", None, None),
            P(("member", "section"), "dp", None, None),
            P(("member", "section"), "dp"),
            P(("member", "section"), "dp"),
            P(("member", "section"), "dp"),
            P(("member", "section", "dp")),
            P(("member", "section", "dp")),
            P(("member", "section", "dp")),
            P(("member", "section", "dp"), None),
            P(("member", "section", "dp"), None),
            P(("member", "section", "dp"), None),
        ),
        check_vma=False,
    )
```

```python
import functools
import math

import jax
import jax.numpy as jnp
from jax import lax
from jax.experimental import pallas as pl
from jax.experimental.pallas import tpu as pltpu
from jax.sharding import PartitionSpec as P

D = 768
HEADS = 12
HEAD = 64
ROT = 16
FF = 3072
STEP = 10
TILE = 384
PAIR = 2 * HEAD
QROWS = 256
CHUNK = 768
LSE_ROWS = 16

norm_eps = 1e-05
beta_first = 0.9
beta_second = 0.999
adam_eps = 1e-08
clip_limit = 1.0
embed_rate = 0.2
embed_decay = 0.01
vector_rate = 0.5
shampoo_rate = 0.1
stats_decay = 0.95
rope_base = 10000.0

f32 = jnp.float32
bf16 = jnp.bfloat16
VMEM_LIMIT = 60 * 2**20
LIGHT = pl.CostEstimate(flops=1, bytes_accessed=1, transcendentals=0)

COL_A, COL_O, COL_B, COL_H = 0, D, 2 * D, 3 * D
COL_QKV = 3 * D + FF
COL_GP = COL_QKV + 3 * D
COL_X = COL_GP + FF
KEPT = COL_X + D
COL_DP, COL_G, COL_DH = 0, 3 * D, 4 * D
GRADS = 4 * D + FF

V_G1, V_C1, V_G2, V_C2, V_QKV, V_O = 0, D, 2 * D, 3 * D, 4 * D, 7 * D
V_B1, V_B2, V_END = 8 * D, 8 * D + FF, 9 * D + FF


def block_places():
    places = []
    for matrix, (rows, cols) in enumerate(((D, 3 * D), (D, D), (D, FF), (FF, D))):
        for row in range(rows // TILE):
            for col in range(cols // TILE):
                places.append((matrix, row, col))
    return places


PLACES = block_places()


def nt(a, b):
    return lax.dot_general(a, b, (((1,), (1,)), ((), ())), preferred_element_type=f32)


def tn(a, b):
    return lax.dot_general(a, b, (((0,), (0,)), ((), ())), preferred_element_type=f32)


def nn(a, b):
    return lax.dot_general(a, b, (((1,), (0,)), ((), ())), preferred_element_type=f32)


def normalized(x):
    mean = jnp.mean(x, axis=-1, keepdims=True)
    centred = x - mean
    spread = jnp.mean(centred * centred, axis=-1, keepdims=True)
    scale = lax.rsqrt(spread + norm_eps)
    return centred * scale, scale


def norm_back(grad, gain, hat, scale):
    inner = grad * gain
    first = jnp.mean(inner, axis=-1, keepdims=True)
    second = jnp.mean(inner * hat, axis=-1, keepdims=True)
    return scale * (inner - first - hat * second)


def gelu_both(h):
    expo = jnp.exp(-0.5 * h * h)
    t = 1.0 / (1.0 + (0.3275911 * math.sqrt(0.5)) * jnp.abs(h))
    poly = 0.5 * 1.061405429
    for coef in (-1.453152027, 1.421413741, -0.284496736, 0.254829592):
        poly = poly * t + 0.5 * coef
    tail = poly * t * expo
    cdf = jnp.where(h >= 0.0, 1.0 - tail, tail)
    return h * cdf, cdf + h * expo * (1.0 / math.sqrt(2.0 * math.pi))


def head_masks(value):
    lane = lax.broadcasted_iota(jnp.int32, (1, PAIR), 1)
    return [
        jnp.where(lane < HEAD, value, 0.0).astype(bf16),
        jnp.where(lane < HEAD, 0.0, value).astype(bf16),
    ]


def arrivals(count):
    low = count // 2 - 1
    order = list(range(count - 1, low, -1)) + list(range(low))
    return [order[i : i + 2] for i in range(0, count - 1, 2)]


def shard_sources(count, is_high, direct):
    rounds = arrivals(count)
    own = count // 2 - 1
    sources = [None] * count
    for index, pair in enumerate(rounds):
        for side, shard in enumerate(pair):
            sources[shard] = index + (0 if direct == (side == 0) else len(rounds))
    sources[own] = 2 * len(rounds) + (0 if direct else 1)
    return sources[::-1] if is_high else sources


class Weights:
    def __init__(self, role, arrays, mats, sems):
        self.role = role
        count = len(PLACES) // arrays[0].shape[0]
        per = arrays[0].shape[0]
        self.copies = []
        for is_high in (False, True):
            for direct in (False, True):
                sources = shard_sources(count, is_high, direct)
                self.copies.append(
                    [
                        pltpu.make_async_copy(
                            arrays[sources[index // per]].at[index % per],
                            mats[matrix].at[pl.ds(row * TILE, TILE), pl.ds(col * TILE, TILE)],
                            sems.at[index],
                        )
                        for index, (matrix, row, col) in enumerate(PLACES)
                    ]
                )

    def start(self, *matrices):
        for role, copies in enumerate(self.copies):

            @pl.when(self.role == role)
            def _(copies=copies):
                for matrix in matrices:
                    for place, copy in zip(PLACES, copies):
                        if place[0] == matrix:
                            copy.start()

    def wait(self, matrix):
        for place, copy in zip(PLACES, self.copies[0]):
            if place[0] == matrix:
                copy.wait()


def forward_kernel(tick, units, *rest):
    meta_ref = rest[5]

    @pl.when(meta_ref[1 + tick] < units)
    def _():
        forward_body(tick, *rest)


def forward_body(tick, unit, part_count, shard_count, first, handed, *refs):
    meta_ref, order_ref, vec_ref, fin_ref, cos_ref, sa_ref, sb_ref = refs[:7]
    if handed:
        recv_ref, *refs = refs[7:]
    else:
        refs = refs[7:]
    parts, refs = refs[:part_count], refs[part_count:]
    shards = refs[:shard_count]
    rest = refs[shard_count + (0 if first else 3) :]
    xb_ref, red_ref, kept_out, xo_out, lse_out = rest[:5]
    wqkv, wo, w1, w2, kept, xo, lse, looked, wsem, isem, osem = rest[5:]
    mats = (wqkv, wo, w1, w2)
    length = xb_ref.shape[0]
    slot = meta_ref[1 + tick]
    weights = Weights(meta_ref[0], shards, mats, wsem)
    width = looked.shape[1]

    def assemble():
        copies = [
            pltpu.make_async_copy(part.at[:, pl.ds(unit * length, length)], looked.at[k], isem.at[k])
            for k, part in enumerate(parts)
        ]
        for copy in copies:
            copy.start()
        for copy in copies:
            copy.wait()
        found = jnp.zeros((length, D), f32)
        for k in range(part_count):
            found = found + tn(looked[k], order_ref[k * width : (k + 1) * width, :])
        kept[:, COL_X : COL_X + D] = found.astype(bf16)

    weights.start(0)
    if handed:
        is_high = meta_ref[0] >= 2

        @pl.when(is_high)
        def _():
            copy = pltpu.make_async_copy(recv_ref, kept.at[:, pl.ds(COL_X, D)], isem.at[0])
            copy.start()
            copy.wait()

        pl.when(jnp.logical_not(is_high))(assemble)
    else:
        assemble()
    inputs = kept[:, COL_X : COL_X + D]
    stores = []

    def store(index, start, width):
        copy = pltpu.make_async_copy(
            kept.at[:, pl.ds(start, width)],
            kept_out.at[slot, :, pl.ds(start, width)],
            osem.at[index],
        )
        copy.start()
        stores.append(copy)

    hat, _ = normalized(inputs.astype(f32))
    kept[:, COL_A : COL_A + D] = (hat * vec_ref[:, V_G1 : V_G1 + D] + vec_ref[:, V_C1 : V_C1 + D]).astype(bf16)
    kept[:, COL_B : COL_B + D] = (hat * vec_ref[:, V_G2 : V_G2 + D] + vec_ref[:, V_C2 : V_C2 + D]).astype(bf16)
    weights.wait(0)
    weights.start(1, 2, 3)
    for part in range(3):
        at = part * D
        proj = nn(kept[:, COL_A : COL_A + D], wqkv[:, at : at + D])
        proj = proj + vec_ref[:, V_QKV + at : V_QKV + at + D]
        if part == 2:
            kept[:, COL_QKV + at : COL_QKV + at + D] = proj.astype(bf16)
        else:
            for p in range(D // PAIR):
                u = proj[:, p * PAIR : (p + 1) * PAIR]
                turned = (
                    u * cos_ref[...]
                    + pltpu.roll(u, PAIR - ROT // 2, 1) * sa_ref[...]
                    + pltpu.roll(u, ROT // 2, 1) * sb_ref[...]
                )
                kept[:, COL_QKV + at + p * PAIR : COL_QKV + at + (p + 1) * PAIR] = turned.astype(bf16)
    store(0, COL_QKV, 3 * D)
    store(1, COL_X, D)
    lse[HEADS:LSE_ROWS, :] = jnp.zeros((LSE_ROWS - HEADS, length), f32)

    scales = head_masks(1.0 / math.sqrt(HEAD))
    lane = lax.broadcasted_iota(jnp.int32, (1, PAIR), 1)
    k_at = lax.broadcasted_iota(jnp.int32, (QROWS, QROWS), 0)
    q_at = lax.broadcasted_iota(jnp.int32, (QROWS, QROWS), 1)

    def attend(p, carry):
        lanes = pl.multiple_of(p * PAIR, PAIR)
        for tile in range(length // QROWS):
            rows = pl.ds(tile * QROWS, QROWS)
            keys = (tile + 1) * QROWS
            q = kept[rows, pl.ds(COL_QKV + lanes, PAIR)]
            k = kept[pl.ds(0, keys), pl.ds(COL_QKV + D + lanes, PAIR)]
            v = kept[pl.ds(0, keys), pl.ds(COL_QKV + 2 * D + lanes, PAIR)]
            outs = []
            for side in range(2):
                s = nt(k, q * scales[side])
                near = jnp.where(k_at <= q_at, s[keys - QROWS :, :], -1e30)
                s = jnp.concatenate([s[: keys - QROWS, :], near], axis=0) if tile else near
                peak = jnp.max(s, axis=0, keepdims=True)
                expo = jnp.exp(s - peak)
                total = jnp.sum(expo, axis=0, keepdims=True)
                soft = (expo * (1.0 / total)).astype(bf16)
                outs.append(tn(soft, v))
                lse[pl.ds(2 * p + side, 1), rows] = peak + jnp.log(total)
            mixed = jnp.where(lane < HEAD, outs[0], outs[1])
            kept[rows, pl.ds(COL_O + lanes, PAIR)] = mixed.astype(bf16)
        return carry

    lax.fori_loop(0, HEADS // 2, attend, 0)
    weights.wait(1)
    out = kept[:, COL_X : COL_X + D].astype(f32) + (nn(kept[:, COL_O : COL_O + D], wo[...]) + vec_ref[:, V_O : V_O + D])
    store(2, COL_A, 3 * D)
    weights.wait(2)
    weights.wait(3)
    branch = jnp.zeros((length, D), f32) + vec_ref[:, V_B2 : V_B2 + D]
    for c in range(0, FF, CHUNK):
        h = nn(kept[:, COL_B : COL_B + D], w1[:, c : c + CHUNK]) + vec_ref[:, V_B1 + c : V_B1 + c + CHUNK]
        act, slope = gelu_both(h)
        kept[:, COL_H + c : COL_H + c + CHUNK] = act.astype(bf16)
        kept[:, COL_GP + c : COL_GP + c + CHUNK] = slope.astype(bf16)
        branch = branch + nn(kept[:, COL_H + c : COL_H + c + CHUNK], w2[c : c + CHUNK, :])
        store(5 + 2 * (c // CHUNK), COL_H + c, CHUNK)
        store(6 + 2 * (c // CHUNK), COL_GP + c, CHUNK)
    out = out + branch
    xo[...] = out
    xb_ref[...] = out.astype(bf16)
    tails = [
        pltpu.make_async_copy(xo, xo_out.at[slot], osem.at[3]),
        pltpu.make_async_copy(lse, lse_out.at[slot], osem.at[4]),
    ]
    for copy in tails:
        copy.start()
    hat, _ = normalized(out)
    final = (hat * fin_ref[:, :D] + fin_ref[:, D : 2 * D]).astype(bf16)
    red_ref[0:1, :] = jnp.sum(hat, axis=0, keepdims=True)
    red_ref[1:2, :] = jnp.sum(final.astype(f32), axis=0, keepdims=True)
    red_ref[2:8, :] = jnp.zeros((6, D), f32)
    for copy in stores + tails:
        copy.wait()


def forward(tick, meta, order, parts, unit, recv, vec, fin, tables, shards, state, slots):
    length = tables[0].shape[0]
    count = len(shards)
    first, handed = state is None, recv is not None
    whole = pl.BlockSpec(memory_space=pltpu.VMEM)
    anywhere = pl.BlockSpec(memory_space=pl.ANY)
    kept_shape = (
        jax.ShapeDtypeStruct((slots, length, KEPT), bf16),
        jax.ShapeDtypeStruct((slots, length, D), f32),
        jax.ShapeDtypeStruct((slots, LSE_ROWS, length), f32),
    )
    operands = [meta, order, vec, fin, *tables]
    if handed:
        operands.append(recv)
    operands += parts
    before = len(operands)
    operands = operands + [*shards] + ([] if first else list(state))
    return pl.pallas_call(
        functools.partial(forward_kernel, tick, slots, unit, len(parts), count, first, handed),
        out_shape=(
            jax.ShapeDtypeStruct((length, D), bf16),
            jax.ShapeDtypeStruct((8, D), f32),
            *kept_shape,
        ),
        in_specs=[pl.BlockSpec(memory_space=pltpu.SMEM)]
        + [whole] * 6
        + [anywhere] * (len(operands) - 7),
        out_specs=(whole, whole, anywhere, anywhere, anywhere),
        input_output_aliases={} if first else {before + count + i: 2 + i for i in range(3)},
        scratch_shapes=[
            pltpu.VMEM((D, 3 * D), bf16),
            pltpu.VMEM((D, D), bf16),
            pltpu.VMEM((D, FF), bf16),
            pltpu.VMEM((FF, D), bf16),
            pltpu.VMEM((length, KEPT), bf16),
            pltpu.VMEM((length, D), f32),
            pltpu.VMEM((LSE_ROWS, length), f32),
            pltpu.VMEM((len(parts), parts[0].shape[0], length), bf16),
            pltpu.SemaphoreType.DMA((len(PLACES),)),
            pltpu.SemaphoreType.DMA((len(parts),)),
            pltpu.SemaphoreType.DMA((5 + 2 * (FF // CHUNK),)),
        ],
        compiler_params=pltpu.CompilerParams(vmem_limit_bytes=VMEM_LIMIT),
        cost_estimate=pl.CostEstimate(flops=10 * 10**9, bytes_accessed=30 * 10**6, transcendentals=5 * 10**6),
        name="layer_forward",
    )(*operands)


def backward_kernel(tick, units, *rest):
    meta_ref = rest[4]

    @pl.when(meta_ref[1 + units + 2 + tick] < units)
    def _():
        backward_body(tick, units, *rest)


def backward_body(tick, units, shard_count, handed, back_in, back_out, *refs):
    meta_ref, flag_ref, order_ref, vec_ref, fin_ref, cos_ref, sa_ref, sb_ref = refs[:8]
    if handed:
        recv_ref, *refs = refs[8:]
    else:
        refs = refs[8:]
    shards = refs[:shard_count]
    kept_in, xo_in, lse_in = refs[shard_count : 3 + shard_count]
    rest = refs[3 + shard_count + back_in :]
    dx_ref, vg_ref, kept_out = rest[:3]
    backs, rest = rest[3 : 3 + back_out], rest[3 + back_out :]
    wqkv, wo, w1, w2, qkv, gp, x, xo, lse, grads, dmix, dq, dk, dv, turned, wsem, isem, osem, bsem = rest
    mats = (wqkv, wo, w1, w2)
    length = cos_ref.shape[0]
    slot = meta_ref[1 + units + 2 + tick]
    weights = Weights(meta_ref[0], shards, mats, wsem)
    loads = [
        pltpu.make_async_copy(xo_in.at[slot], xo, isem.at[0]),
        pltpu.make_async_copy(kept_in.at[slot, :, pl.ds(COL_GP, FF)], gp, isem.at[1]),
        pltpu.make_async_copy(kept_in.at[slot, :, pl.ds(COL_X, D)], x, isem.at[2]),
        pltpu.make_async_copy(kept_in.at[slot, :, pl.ds(COL_QKV, 3 * D)], qkv, isem.at[3]),
        pltpu.make_async_copy(lse_in.at[slot], lse, isem.at[4]),
    ]
    loads[0].start()
    weights.start(1)
    loads[3].start()
    loads[4].start()
    loads[0].wait()
    hat, scale = normalized(xo[...])
    headed = fin_ref[:, 2 * D : 3 * D] * fin_ref[:, :D]
    top = flag_ref[min(tick, units - 1)] * norm_back(1.0, headed, hat, scale)
    if handed:
        top = jnp.where(meta_ref[0] >= 2, top, recv_ref[...].astype(f32))
    xo[...] = top
    grads[:, COL_G : COL_G + D] = xo[...].astype(bf16)
    bias = jnp.sum(grads[:, COL_G : COL_G + D].astype(f32), axis=0, keepdims=True)
    vg_ref[:, V_O : V_O + D] = bias
    vg_ref[:, V_B2 : V_B2 + D] = bias

    weights.wait(1)
    dmix[...] = nt(grads[:, COL_G : COL_G + D], wo[...]).astype(bf16)
    loads[3].wait()
    loads[4].wait()
    weights.start(3)
    loads[1].start()
    weights.start(2)
    loads[2].start()
    weights.start(0)
    scales = head_masks(1.0 / math.sqrt(HEAD))
    ones = head_masks(1.0)
    k_at = lax.broadcasted_iota(jnp.int32, (QROWS, QROWS), 0)
    q_at = lax.broadcasted_iota(jnp.int32, (QROWS, QROWS), 1)

    def attend(p, carry):
        lanes = pl.multiple_of(p * PAIR, PAIR)
        for tile in range(length // QROWS):
            rows = pl.ds(tile * QROWS, QROWS)
            keys = (tile + 1) * QROWS
            q = qkv[rows, pl.ds(lanes, PAIR)]
            k = qkv[pl.ds(0, keys), pl.ds(D + lanes, PAIR)]
            v = qkv[pl.ds(0, keys), pl.ds(2 * D + lanes, PAIR)]
            dm = dmix[rows, pl.ds(lanes, PAIR)]
            dq_sum = dk_sum = dv_sum = None
            for side in range(2):
                qs = q * scales[side]
                ks = k * scales[side]
                dms = dm * ones[side]
                s = nt(k, qs)
                soft = jnp.exp(s - lse[pl.ds(2 * p + side, 1), rows])
                near = jnp.where(k_at <= q_at, soft[keys - QROWS :, :], 0.0)
                soft = jnp.concatenate([soft[: keys - QROWS, :], near], axis=0) if tile else near
                dsoft = nt(v, dms)
                centre = jnp.sum(soft * dsoft, axis=0, keepdims=True)
                ds = (soft * (dsoft - centre)).astype(bf16)
                one_dv = nn(soft.astype(bf16), dms)
                one_dk = nn(ds, qs)
                one_dq = tn(ds, ks)
                if side:
                    dq_sum, dk_sum, dv_sum = dq_sum + one_dq, dk_sum + one_dk, dv_sum + one_dv
                else:
                    dq_sum, dk_sum, dv_sum = one_dq, one_dk, one_dv
            dq[rows, :] = dq_sum
            if tile:
                old = pl.ds(0, tile * QROWS)
                new = pl.ds(tile * QROWS, QROWS)
                dk[old, :] = dk[old, :] + dk_sum[: tile * QROWS]
                dk[new, :] = dk_sum[tile * QROWS :]
                dv[old, :] = dv[old, :] + dv_sum[: tile * QROWS]
                dv[new, :] = dv_sum[tile * QROWS :]
            else:
                dk[rows, :] = dk_sum
                dv[rows, :] = dv_sum
        for part, ref in ((0, dq), (1, dk)):
            g = ref[...]
            turned = (
                g * cos_ref[...]
                - pltpu.roll(g, PAIR - ROT // 2, 1) * sa_ref[...]
                - pltpu.roll(g, ROT // 2, 1) * sb_ref[...]
            )
            grads[:, pl.ds(COL_DP + part * D + lanes, PAIR)] = turned.astype(bf16)
        grads[:, pl.ds(COL_DP + 2 * D + lanes, PAIR)] = dv[...].astype(bf16)
        return carry

    lax.fori_loop(0, HEADS // 2, attend, 0)
    stores = [
        pltpu.make_async_copy(
            grads.at[:, pl.ds(COL_DP, 3 * D)], kept_out.at[slot, :, pl.ds(COL_QKV, 3 * D)], osem.at[2]
        )
    ]
    stores[0].start()
    weights.wait(3)
    loads[1].wait()
    loads[2].wait()
    weights.wait(2)
    second = jnp.zeros((length, D), f32)
    for c in range(0, FF, CHUNK):
        act = nt(grads[:, COL_G : COL_G + D], w2[c : c + CHUNK, :])
        pre = (act * gp[:, c : c + CHUNK].astype(f32)).astype(bf16)
        grads[:, COL_DH + c : COL_DH + c + CHUNK] = pre
        vg_ref[:, V_B1 + c : V_B1 + c + CHUNK] = jnp.sum(pre.astype(f32), axis=0, keepdims=True)
        second = second + nt(pre, w1[:, c : c + CHUNK])
    hat, scale = normalized(x[...].astype(f32))
    vg_ref[:, V_G2 : V_G2 + D] = jnp.sum(second * hat, axis=0, keepdims=True)
    vg_ref[:, V_C2 : V_C2 + D] = jnp.sum(second, axis=0, keepdims=True)
    xo[...] = xo[...] + norm_back(second, vec_ref[:, V_G2 : V_G2 + D], hat, scale)
    stores += [
        pltpu.make_async_copy(
            grads.at[:, pl.ds(COL_G, D)], kept_out.at[slot, :, pl.ds(COL_X, D)], osem.at[0]
        ),
        pltpu.make_async_copy(
            grads.at[:, pl.ds(COL_DH, FF)], kept_out.at[slot, :, pl.ds(COL_GP, FF)], osem.at[1]
        ),
    ]
    stores[1].start()
    stores[2].start()

    vg_ref[:, V_QKV : V_QKV + 3 * D] = jnp.sum(
        grads[:, COL_DP : COL_DP + 3 * D].astype(f32), axis=0, keepdims=True
    )
    weights.wait(0)
    one = nt(grads[:, COL_DP : COL_DP + 3 * D], wqkv[...])
    hat, scale = normalized(x[...].astype(f32))
    vg_ref[:, V_G1 : V_G1 + D] = jnp.sum(one * hat, axis=0, keepdims=True)
    vg_ref[:, V_C1 : V_C1 + D] = jnp.sum(one, axis=0, keepdims=True)
    total = xo[...] + norm_back(one, vec_ref[:, V_G1 : V_G1 + D], hat, scale)
    dx_ref[...] = total.astype(bf16)
    if back_out:
        turned[...] = nt(order_ref[...], dx_ref[...]).astype(bf16)
        start = (tick - 2) * length if tick <= units else 0
        width = backs[0].shape[0]
        for k, back in enumerate(backs):
            copy = pltpu.make_async_copy(
                turned.at[pl.ds(k * width, width)], back.at[:, pl.ds(start, length)], bsem.at[k]
            )
            copy.start()
            stores.append(copy)
    for copy in stores:
        copy.wait()


def backward(tick, units, meta, flags, order, recv, vec, fin, tables, shards, state, backs):
    length = tables[0].shape[0]
    count = len(shards)
    handed = recv is not None
    chips = len(PLACES) // shards[0].shape[0]
    spans = 0 if tick < 2 else (units - 1 if tick <= units else 1)
    back_shapes = [jax.ShapeDtypeStruct((D // chips, spans * length), bf16)] * (chips if spans else 0)
    whole = pl.BlockSpec(memory_space=pltpu.VMEM)
    anywhere = pl.BlockSpec(memory_space=pl.ANY)
    small = pl.BlockSpec(memory_space=pltpu.SMEM)
    operands = [meta, flags, order, vec, fin, *tables]
    if handed:
        operands.append(recv)
    dense = len(operands)
    operands = operands + [*shards, *state, *backs]
    aliases = {dense + count: 2} | {dense + count + 3 + i: 3 + i for i in range(len(backs))}
    return pl.pallas_call(
        functools.partial(backward_kernel, tick, units, count, handed, len(backs), len(back_shapes)),
        out_shape=(
            jax.ShapeDtypeStruct((length, D), bf16),
            jax.ShapeDtypeStruct((1, V_END), f32),
            jax.ShapeDtypeStruct(state[0].shape, bf16),
            *back_shapes,
        ),
        in_specs=[small, small] + [whole] * (dense - 2) + [anywhere] * (len(operands) - dense),
        out_specs=(whole, whole, anywhere) + (anywhere,) * len(back_shapes),
        input_output_aliases=aliases,
        scratch_shapes=[
            pltpu.VMEM((D, 3 * D), bf16),
            pltpu.VMEM((D, D), bf16),
            pltpu.VMEM((D, FF), bf16),
            pltpu.VMEM((FF, D), bf16),
            pltpu.VMEM((length, 3 * D), bf16),
            pltpu.VMEM((length, FF), bf16),
            pltpu.VMEM((length, D), bf16),
            pltpu.VMEM((length, D), f32),
            pltpu.VMEM((LSE_ROWS, length), f32),
            pltpu.VMEM((length, GRADS), bf16),
            pltpu.VMEM((length, D), bf16),
            pltpu.VMEM((length, PAIR), f32),
            pltpu.VMEM((length, PAIR), f32),
            pltpu.VMEM((length, PAIR), f32),
            pltpu.VMEM((D, length), bf16),
            pltpu.SemaphoreType.DMA((len(PLACES),)),
            pltpu.SemaphoreType.DMA((5,)),
            pltpu.SemaphoreType.DMA((3,)),
            pltpu.SemaphoreType.DMA((chips,)),
        ],
        compiler_params=pltpu.CompilerParams(vmem_limit_bytes=VMEM_LIMIT),
        cost_estimate=pl.CostEstimate(flops=20 * 10**9, bytes_accessed=40 * 10**6, transcendentals=5 * 10**6),
        name="layer_backward",
    )(*operands)


def product_kernel(shards, start, tiles, x_ref, y_ref, *refs):
    sent_ref = refs[0] if len(refs) > 2 else None
    turned = refs[-1]
    units, rows, width = x_ref.shape
    step = pl.program_id(0)
    steps = pl.num_programs(0)
    before = tiles[start + jnp.maximum(step - 1, 0)]

    @pl.when(jnp.logical_or(step == 0, tiles[start + step] != before))
    def _():
        for unit in range(units):
            turned[:, unit * rows : (unit + 1) * rows] = jnp.transpose(x_ref[unit])

    found = nn(turned[...], y_ref[...].reshape(units * rows, -1))
    if sent_ref is None:
        out_ref = refs[0]
        for i in range(out_ref.shape[0]):
            out_ref[i] = found[:, i * TILE : (i + 1) * TILE].astype(bf16)
        return
    square_ref, *out_refs = refs[1:-1]

    @pl.when(step == 0)
    def _():
        square_ref[...] = jnp.zeros_like(square_ref)

    each = sent_ref.shape[0]
    blocks = []
    for i in range(each):
        whole = found[:, i * TILE : (i + 1) * TILE] + sent_ref[i].astype(f32)
        blocks.append(whole.astype(bf16))
        weight = tiles[start + 2 * steps + step * each + i].astype(f32)
        square_ref[...] += weight * jnp.sum(whole * whole, axis=0, keepdims=True)
    per = steps // shards
    for shard, out_ref in enumerate(out_refs):

        @pl.when(step // per == shard)
        def _(out_ref=out_ref):
            for i in range(each):
                out_ref[i] = blocks[i]


def product_tiles(count, each):
    total = len(PLACES) // count
    part = (total + 1) // 2
    rest = total - part
    group = max(count // 2, 1)
    left = [(0, 2, 4, 6)[m] + row for m, row, _ in PLACES]
    right = [((14, 28, 20, 28)[m] + col) // each for m, _, col in PLACES]
    found = []
    for is_high in range(2):
        for core in range(2):
            row = []
            for start in range(0, count, group):
                shards = [shard_order(count, is_high)[step] for step in range(start, start + group)]
                for half in (1 - core, core):
                    places = [k * total + half * rest + i for k in shards for i in range(part)]
                    row += [left[b] for b in places[::each]] + [right[b] for b in places[::each]]
                    row += [0 if half == 1 and i < part - rest else 1 for _ in shards for i in range(part)]
            found.append(row)
    return found


def shard_order(count, is_high):
    low = count // 2 - 1
    order = list(range(count - 1, low, -1)) + list(range(low + 1))
    return [count - 1 - k for k in order] if is_high else order


def products(shards, tiles, call, kept, units, each, sent=None):
    part = (len(PLACES) // (2 * shards) + 1) // 2
    steps = shards * part // each
    start = call * (2 * steps + shards * part)
    per = steps // shards
    length = kept.shape[1]
    block = pl.BlockSpec((each, TILE, TILE), lambda i, t: (i, 0, 0))
    if sent is None:
        out_shape, out_specs, more = jax.ShapeDtypeStruct((steps * each, TILE, TILE), bf16), block, []
    else:
        out_shape = (jax.ShapeDtypeStruct((1, TILE), f32),)
        out_shape += (jax.ShapeDtypeStruct((per * each, TILE, TILE), bf16),) * shards
        out_specs = (pl.BlockSpec((1, TILE), lambda i, t: (0, 0)),)
        for shard in range(shards):
            out_specs += (
                pl.BlockSpec(
                    (each, TILE, TILE),
                    lambda i, t, first=shard * per: (jnp.clip(i - first, 0, per - 1), 0, 0),
                ),
            )
        more = [sent]
    return pl.pallas_call(
        functools.partial(product_kernel, shards, start),
        out_shape=out_shape,
        grid_spec=pltpu.PrefetchScalarGridSpec(
            num_scalar_prefetch=1,
            grid=(steps,),
            in_specs=[
                pl.BlockSpec((units, length, TILE), lambda i, t: (0, 0, t[start + i])),
                pl.BlockSpec((units, length, each * TILE), lambda i, t: (0, 0, t[start + steps + i])),
            ]
            + [block] * len(more),
            out_specs=out_specs,
            scratch_shapes=[pltpu.VMEM((TILE, units * length), bf16)],
        ),
        compiler_params=pltpu.CompilerParams(vmem_limit_bytes=VMEM_LIMIT),
        cost_estimate=LIGHT,
        name="weight_products",
    )(tiles, kept, kept, *more)


def lookup_kernel(ids_ref, embedding_ref, first_ref, rest_ref, table, wide):
    step = pl.program_id(0)
    features = embedding_ref.shape[0]
    lanes = table.shape[1]
    tiles = embedding_ref.shape[1] // lanes
    tokens = wide.shape[0]

    def turn(i):
        tile = embedding_ref[:, pl.ds(pl.multiple_of(i * lanes, lanes), lanes)]
        table[pl.ds(pl.multiple_of((step * tiles + i) * lanes, lanes), lanes), :features] = jnp.transpose(tile)

    def several(i, carry):
        for j in range(8):
            turn(i * 8 + j)
        return carry

    lax.fori_loop(0, tiles // 8, several, 0)
    for i in range(tiles // 8 * 8, tiles):
        turn(i)

    @pl.when(step == pl.num_programs(0) - 1)
    def _():
        def fetch(i, carry):
            for j in range(16):
                wide[pl.ds(i * 16 + j, 1), :] = table[pl.ds(ids_ref[i * 16 + j], 1), :]
            return carry

        lax.fori_loop(0, tokens // 16, fetch, 0)
        start = 0
        for ref in (first_ref, rest_ref):

            def flat(i, carry, ref=ref, start=start):
                rows = wide[pl.ds(pl.multiple_of(start + i * lanes, lanes), lanes), :]
                ref[:, pl.ds(pl.multiple_of(i * lanes, lanes), lanes)] = jnp.transpose(rows)[:features].astype(bf16)
                return carry

            lax.fori_loop(0, ref.shape[1] // lanes, flat, 0)
            start += ref.shape[1]


def lookup(ids, embedding, first):
    features, vocab = embedding.shape
    tokens = ids.shape[0]
    lanes = 128
    steps = 3 if vocab % (3 * lanes) == 0 else 1
    whole = lambda i: (0, 0)
    return pl.pallas_call(
        lookup_kernel,
        out_shape=(
            jax.ShapeDtypeStruct((features, first), bf16),
            jax.ShapeDtypeStruct((features, tokens - first), bf16),
        ),
        grid=(steps,),
        in_specs=[
            pl.BlockSpec(memory_space=pltpu.SMEM),
            pl.BlockSpec((features, vocab // steps), lambda i: (0, i)),
        ],
        out_specs=(
            pl.BlockSpec((features, first), whole),
            pl.BlockSpec((features, tokens - first), whole),
        ),
        scratch_shapes=[pltpu.VMEM((vocab, lanes), f32), pltpu.VMEM((tokens, lanes), f32)],
        compiler_params=pltpu.CompilerParams(vmem_limit_bytes=VMEM_LIMIT),
        cost_estimate=LIGHT,
        name="table_lookup",
    )(ids, embedding)


def table_kernel(ids_ref, *refs):
    parts = refs[:-5]
    out_ref, square_ref, table, wide, total = refs[-5:]
    step = pl.program_id(0)
    features = out_ref.shape[0]
    tokens = wide.shape[0]
    vocab, lanes = table.shape
    tiles = out_ref.shape[1] // lanes

    @pl.when(step == 0)
    def _():
        def clear(i, carry):
            table[pl.ds(pl.multiple_of(i * 3 * lanes, lanes), 3 * lanes), :] = jnp.zeros((3 * lanes, lanes), f32)
            return carry

        lax.fori_loop(0, vocab // (3 * lanes), clear, 0)
        total[...] = jnp.zeros_like(total)
        if features < lanes:
            wide[:, features:] = jnp.zeros((tokens, lanes - features), f32)
        start = 0
        for part in parts:

            def upright(i, carry, part=part, start=start):
                tile = part[:, pl.ds(pl.multiple_of(i * lanes, lanes), lanes)].astype(f32)
                wide[pl.ds(pl.multiple_of(start + i * lanes, lanes), lanes), :features] = jnp.transpose(tile)
                return carry

            lax.fori_loop(0, part.shape[1] // lanes, upright, 0)
            start += part.shape[1]

        def add(i, carry):
            for j in range(16):
                row = pl.ds(ids_ref[i * 16 + j], 1)
                table[row, :] = table[row, :] + wide[pl.ds(i * 16 + j, 1), :]
            return carry

        lax.fori_loop(0, tokens // 16, add, 0)

    def turn(i):
        tile = table[pl.ds(pl.multiple_of((step * tiles + i) * lanes, lanes), lanes), :]
        total[...] += tile * tile
        out_ref[:, pl.ds(pl.multiple_of(i * lanes, lanes), lanes)] = jnp.transpose(tile)[:features]

    def several(i, carry):
        for j in range(8):
            turn(i * 8 + j)
        return carry

    lax.fori_loop(0, tiles // 8, several, 0)
    for i in range(tiles // 8 * 8, tiles):
        turn(i)

    @pl.when(step == pl.num_programs(0) - 1)
    def _():
        square_ref[...] = jnp.sum(total[...], axis=0, keepdims=True)


def table_gradient(ids, parts, vocab):
    tokens, features = ids.shape[0], parts[0].shape[0]
    lanes = 128
    steps = 3 if vocab % (3 * lanes) == 0 else 1
    return pl.pallas_call(
        table_kernel,
        out_shape=(jax.ShapeDtypeStruct((features, vocab), f32), jax.ShapeDtypeStruct((1, lanes), f32)),
        grid=(steps,),
        in_specs=[
            pl.BlockSpec(memory_space=pltpu.SMEM),
        ]
        + [pl.BlockSpec(part.shape, lambda i: (0, 0), pipeline_mode=pl.Buffered(1)) for part in parts],
        out_specs=(
            pl.BlockSpec((features, vocab // steps), lambda i: (0, i)),
            pl.BlockSpec((1, lanes), lambda i: (0, 0)),
        ),
        scratch_shapes=[
            pltpu.VMEM((vocab, lanes), f32),
            pltpu.VMEM((tokens, lanes), f32),
            pltpu.VMEM((lanes, lanes), f32),
        ],
        compiler_params=pltpu.CompilerParams(vmem_limit_bytes=VMEM_LIMIT),
        cost_estimate=LIGHT,
        name="table_gradient",
    )(ids, *parts)


def split(value):
    high = value.astype(bf16)
    return high, (value - high.astype(f32)).astype(bf16)


def shampoo_kernel(factor_ref, g_ref, w_ref, ls_ref, rs_ref, lr_ref, rr_ref, bg_ref, nw_ref, nl_ref, nr_ref):
    factor = factor_ref[0]
    level = (1.0 - stats_decay) * factor * factor
    for i in range(g_ref.shape[0]):
        g = g_ref[i]
        bg_ref[i] = g.astype(f32) * factor
        nl_ref[i] = stats_decay * ls_ref[i] + level * nt(g, g)
        nr_ref[i] = stats_decay * rs_ref[i] + level * tn(g, g)
        right_high, right_low = split(rr_ref[i])
        inner = nn(g, right_high) + nn(g, right_low)
        inner_high, inner_low = split(inner)
        left_high, left_low = split(lr_ref[i])
        direction = nn(left_high, inner_high) + (nn(left_high, inner_low) + nn(left_low, inner_high))
        nw_ref[i] = w_ref[i] - (shampoo_rate * factor) * direction


def shampoo(factor, grad, weights, left_stats, right_stats, left_root, right_root):
    count = grad.shape[0]
    each = max(i for i in (1, 2, 3) if count % i == 0)
    block = pl.BlockSpec((each, TILE, TILE), lambda i: (i, 0, 0))
    shape = jax.ShapeDtypeStruct((count, TILE, TILE), f32)
    return pl.pallas_call(
        shampoo_kernel,
        out_shape=(shape,) * 4,
        grid=(count // each,),
        in_specs=[pl.BlockSpec(memory_space=pltpu.SMEM)] + [block] * 6,
        out_specs=(block,) * 4,
        compiler_params=pltpu.CompilerParams(vmem_limit_bytes=VMEM_LIMIT),
        cost_estimate=LIGHT,
        name="shampoo",
    )(factor, grad, weights, left_stats, right_stats, left_root, right_root)


def rope_columns(length):
    half_rot = ROT // 2
    lanes = jnp.arange(PAIR) % HEAD
    index = jnp.where(lanes < half_rot, lanes, lanes - half_rot).astype(f32)
    inverse = rope_base ** (-2.0 * index / ROT)
    angles = jnp.arange(length)[:, None].astype(f32) * inverse[None, :]
    cosine = jnp.where(lanes < ROT, jnp.cos(angles), 1.0)
    sine = jnp.where(lanes < ROT, jnp.sin(angles), 0.0)
    first = jnp.where(lanes < half_rot, -sine, 0.0)
    second = jnp.where(lanes < half_rot, 0.0, sine)
    return cosine, first, second


def adam_step(weight, moment, second, grad, rate, decay):
    moment_new = beta_first * moment + (1.0 - beta_first) * grad
    second_new = beta_second * second + (1.0 - beta_second) * grad * grad
    corrected = moment_new / (1.0 - beta_first**STEP)
    scaled = jnp.sqrt(second_new / (1.0 - beta_second**STEP)) + adam_eps
    return (moment_new, second_new, weight - rate * (corrected / scaled + decay * weight))


def rounded(values):
    return lax.reduce_precision(values, 8, 7)


def chosen(flags, values):
    total = values[-1]
    for flag, value in zip(flags[:-1], values[:-1]):
        total = jnp.where(flag, value, total)
    return total


def ordered(section, mine, other, axis):
    return jnp.concatenate(
        [jnp.where(section == 0, mine, other), jnp.where(section == 0, other, mine)], axis=axis
    )


def swapped(value):
    return lax.ppermute(value, "section", [(0, 1), (1, 0)])


def local(
    tokens,
    margins,
    tie_flags,
    embedding,
    embed_moment,
    embed_second,
    layer_blocks,
    left_stats,
    right_stats,
    left_root,
    right_root,
    layer_vectors,
    vector_moment,
    vector_second,
    closing_vectors,
    final_moment,
    final_second,
):
    both = ("section", "dp")
    count = lax.axis_size("dp")
    section = lax.axis_index("section")
    place = lax.axis_index("dp")
    low, high = count // 2 - 1, count // 2
    is_high = place >= high
    order_low, order_high = shard_order(count, False), shard_order(count, True)
    length = tokens.shape[2]
    units = tokens.shape[0] * count
    own_blocks = layer_blocks.shape[1]
    own_vector = layer_vectors.shape[1]
    own_final = closing_vectors.shape[0]
    features, vocab = embedding.shape

    own_closing = rounded(closing_vectors)
    pack = jnp.concatenate(
        [
            tokens.reshape(-1).astype(f32),
            margins.astype(f32),
            tie_flags.astype(f32),
            rounded(layer_vectors[0]),
            own_closing,
        ]
    )
    passed = [pack] + [
        lax.ppermute(pack, "dp", [(i, (i + d) % count) for i in range(count)]) for d in range(1, count)
    ]
    packs = jnp.stack(passed)

    own, packs = lax.optimization_barrier((layer_blocks[0].astype(bf16), packs))
    rounds = arrivals(count)
    received = []
    for pair in rounds:
        route = []
        for side, shard in enumerate(pair):
            route.append((shard, side * count + low))
            route.append((count + count - 1 - shard, (1 - side) * count + high))
        received.append(lax.ppermute(own, both, route))

    packs = packs[(place - jnp.arange(count)) % count]
    at = tokens.size
    ids = packs[:, :at].astype(jnp.int32).reshape(2, units, length)
    pair_margins = packs[:, at : at + margins.size].reshape(-1)
    at = at + margins.size
    pair_ties = packs[:, at : at + margins.size].reshape(-1)
    at = at + margins.size
    other_packs = swapped(packs[:, at:])
    layer_packs = jnp.where((section == 1) == is_high, packs[:, at:], other_packs)
    vec = layer_packs[:, :own_vector].reshape(1, -1)
    fin = ordered(section, packs[:, at + own_vector :], other_packs[:, own_vector:], 0).reshape(1, -1)
    tables = rope_columns(length)

    ids_here = jnp.where(section == 0, ids, ids[::-1])
    looked = lookup(
        jnp.concatenate([ids_here[:, :1].reshape(-1), ids_here[:, 1:].reshape(-1)]), embedding, 2 * length
    )

    def joined(columns):
        half = columns.shape[1] // 2
        return ordered(section, columns[:, :half], swapped(columns[:, half:]), 0)

    def sent_on(columns):
        return [columns if k == low else lax.ppermute(columns, "dp", [(k, low)]) for k in range(count)]

    looked = [joined(columns) for columns in looked]
    first = sent_on(looked[0])
    slot_at = jnp.arange(D)
    chip, within = slot_at // (2 * features), slot_at % (2 * features)
    feature_at = within // features * (D // 2) + chip * features + within % features
    order = (feature_at[:, None] == jnp.arange(D)[None, :]).astype(bf16)
    part = (own_blocks + 1) // 2
    each = 2 if own_blocks % 4 == 0 else 1
    group = max(count // 2, 1)
    tiles = lax.dynamic_index_in_dim(
        jnp.array(product_tiles(count, each), jnp.int32), is_high * 2 + section, 0, False
    )

    first, later, received, vec, fin, tables, order, tiles = lax.optimization_barrier(
        (first, looked[1], received, vec, fin, tables, order, tiles)
    )
    relays = [
        lax.ppermute(
            array, both, [(low, count + low), (count + low, low), (high, count + high), (count + high, high)]
        )
        for array in [own, *received]
    ]
    later, relays[-1] = lax.optimization_barrier((later, relays[-1]))
    later = sent_on(later)
    shards = [*received, *relays[1:], own, relays[0]]
    role = is_high * 2 + ((section == 1) == is_high) * 1

    live_low, live_high = place == low, place == high
    early = [*range(units), units, units]
    late = [units, units, *range(units)]
    meta = jnp.where(live_high, jnp.array([0, *late, *early]), jnp.array([0, *early, *late]))
    meta = jnp.where(live_low | live_high, meta, units).at[0].set(role).astype(jnp.int32)
    state = None
    arrived = []
    sums = []
    for tick in range(units + 2):
        unit = min(tick, units - 1)
        result, tail, *state = forward(
            tick,
            meta,
            order,
            later if unit else first,
            max(unit - 1, 0),
            arrived[tick - 2] if tick >= 2 else None,
            vec,
            fin,
            tables,
            shards,
            state,
            units,
        )
        if tick < units:
            arrived.append(lax.ppermute(result, "dp", [(low, high)]))
        if tick >= 2:
            sums.append(tail[:2])
    sums = jnp.stack(sums)
    sum_hat, sum_final = sums[:, 0], sums[:, 1]
    final_gain, head = fin[0, :D], fin[0, 2 * D :]
    rewards = (jnp.sum(sum_final * head, axis=1) / length).reshape(-1, 2)
    pairs = units // 2
    gap = rewards[:, 0] - rewards[:, 1]
    half_margin = 0.5 * lax.dynamic_slice_in_dim(pair_margins, section * pairs, pairs, 0)
    tie = lax.dynamic_slice_in_dim(pair_ties, section * pairs, pairs, 0)
    pair_loss = (1.0 - tie) * jax.nn.softplus(half_margin - gap) + tie * 0.5 * (
        jax.nn.softplus(gap) + jax.nn.softplus(-gap)
    )
    gap_grad = -(1.0 - tie) * jax.nn.sigmoid(half_margin - gap) + tie * 0.5 * (
        jax.nn.sigmoid(gap) - jax.nn.sigmoid(-gap)
    )
    reward_grad = (jnp.stack([gap_grad, -gap_grad], axis=1) / length).reshape(-1)
    final_local = jnp.concatenate(
        [
            head * jnp.sum(reward_grad[:, None] * sum_hat, axis=0),
            head * (length * jnp.sum(reward_grad)),
            jnp.sum(reward_grad[:, None] * sum_final, axis=0),
        ]
    )

    def returned(parts):
        return [part if k == low else lax.ppermute(part, "dp", [(low, k)]) for k, part in enumerate(parts)]

    def own_features(parts):
        both_cores = chosen([place == k for k in range(count)], parts)
        mine, other = both_cores[:features], both_cores[features:]
        return [jnp.where(section == 0, mine, other), swapped(jnp.where(section == 0, other, mine))]

    arrived = []
    vector_sum = jnp.zeros((1, V_END), f32)
    backs = []
    token_grads = []
    for tick in range(units + 2):
        if tick == units + 1:
            token_grads.append(returned(backs))
            backs = []
        grad_in, vector_part, state[0], *backs = backward(
            tick,
            units,
            meta,
            reward_grad,
            order,
            arrived[tick - 2] if tick >= 2 else None,
            vec,
            fin,
            tables,
            shards,
            state,
            backs,
        )
        if tick < units:
            arrived.append(lax.ppermute(grad_in, "dp", [(high, low)]))
        vector_sum = vector_sum + jnp.where(meta[1 + units + 2 + tick] < units, vector_part, 0.0)
    token_grads.append(returned(backs))

    vector_pack = jnp.concatenate([vector_sum[0], jnp.where(live_high, final_local, 0.0)])
    vector_pack = vector_pack + swapped(vector_pack)

    def to_owner(value, step):
        route = [
            (core * count + source, core * count + target)
            for core in range(2)
            for source, target in ((low, order_low[step]), (high, order_high[step]))
        ]
        return lax.ppermute(value, both, route) if step < count - 1 else value

    live = live_low | live_high
    token_grads[0], tiles = lax.optimization_barrier((token_grads[0], tiles))
    kept = state[0]
    squares = jnp.where(live & (section == 0), jnp.sum(vector_pack * vector_pack), 0.0)
    ids_ordered = jnp.concatenate(
        [ids_here[0, :-1], ids_here[1, :-1], ids_here[0, -1:], ids_here[1, -1:]], axis=0
    ).reshape(-1)
    sent, pieces = [], []
    for index in range(count // group):
        sums = products(group, tiles, 2 * index, kept, units, each)
        if index == 0:
            token_grads[1], sums = lax.optimization_barrier((token_grads[1], sums))
        block_squares, *found = products(group, tiles, 2 * index + 1, kept, units, each, swapped(sums))
        squares = squares + jnp.where(live, jnp.sum(block_squares), 0.0)
        if index + 1 < count // group:
            tiles, found = lax.optimization_barrier((tiles, found))
            found = [to_owner(piece, index * group + i) for i, piece in enumerate(found)]
        pieces += found
    vectors = [to_owner(vector_pack, step) for step in range(count)]
    token_grads, pieces[-1] = lax.optimization_barrier((token_grads, pieces[-1]))
    table_grad, table_squares = table_gradient(
        ids_ordered, own_features(token_grads[0]) + own_features(token_grads[1]), vocab
    )

    squares = squares + jnp.sum(table_squares)
    squares, pieces[: count - group] = lax.optimization_barrier((squares, pieces[: count - group]))
    loss = jnp.where(place == high, jnp.sum(pair_loss), 0.0)
    square_total, loss_total = lax.psum((squares, loss), both)
    norm_value = jnp.sqrt(square_total)
    factor = clip_limit / jnp.maximum(norm_value, clip_limit)
    pieces[count - group :], factor = lax.optimization_barrier((pieces[count - group :], factor))
    pieces[count - group :] = [to_owner(pieces[step], step) for step in range(count - group, count)]
    embed_m, embed_v, embed_w = adam_step(
        embedding, embed_moment, embed_second, table_grad * factor, embed_rate, embed_decay
    )
    pieces, embed_w = lax.optimization_barrier((pieces, embed_w))
    from_low = [place == k for k in order_low]
    from_high = [place == k for k in order_high]
    piece_low, piece_high = chosen(from_low, pieces), chosen(from_high, pieces)
    mine = jnp.where(section == 0, piece_low, piece_high)
    other = swapped(jnp.where(section == 0, piece_high, piece_low))
    grad_blocks = jnp.concatenate(
        [jnp.where(section == 0, mine, other), jnp.where(section == 0, other, mine)[2 * part - own_blocks :]],
        axis=0,
    )
    vectors_high = chosen(from_high, vectors)
    owned_vector = lax.dynamic_slice_in_dim(
        jnp.where(section == 0, chosen(from_low, vectors), vectors_high), place * own_vector, own_vector, 0
    )[None]
    owned_final = lax.dynamic_slice_in_dim(
        vectors_high, V_END + (section * count + place) * own_final, own_final, 0
    )

    block_grad, new_blocks, new_left, new_right = (
        out[None]
        for out in shampoo(
            factor.reshape(1),
            grad_blocks,
            layer_blocks[0],
            left_stats[0],
            right_stats[0],
            left_root[0],
            right_root[0],
        )
    )
    vector_m, vector_v, vector_w = adam_step(
        layer_vectors, vector_moment, vector_second, owned_vector * factor, vector_rate, 0.0
    )
    final_m, final_v, final_w = adam_step(
        closing_vectors, final_moment, final_second, owned_final * factor, vector_rate, 0.0
    )
    return (
        loss_total.reshape(1),
        norm_value.reshape(1),
        block_grad,
        new_blocks,
        new_left,
        new_right,
        vector_m,
        vector_v,
        vector_w,
        final_m,
        final_v,
        final_w,
        embed_m,
        embed_v,
        embed_w,
    )


def solution(mesh):
    return jax.shard_map(
        local,
        mesh=mesh,
        in_specs=(
            P(("member", "dp"), None, None),
            P(("member", "dp")),
            P(("member", "dp")),
            P(("member", "section", "dp"), None),
            P(("member", "section", "dp"), None),
            P(("member", "section", "dp"), None),
            P(("member", "section"), "dp", None, None),
            P(("member", "section"), "dp", None, None),
            P(("member", "section"), "dp", None, None),
            P(("member", "section"), "dp", None, None),
            P(("member", "section"), "dp", None, None),
            P(("member", "section"), "dp"),
            P(("member", "section"), "dp"),
            P(("member", "section"), "dp"),
            P(("member", "section", "dp")),
            P(("member", "section", "dp")),
            P(("member", "section", "dp")),
        ),
        out_specs=(
            P("member"),
            P("member"),
            P(("member", "section"), "dp", None, None),
            P(("member", "section"), "dp", None, None),
            P(("member", "section"), "dp", None, None),
            P(("member", "section"), "dp", None, None),
            P(("member", "section"), "dp"),
            P(("member", "section"), "dp"),
            P(("member", "section"), "dp"),
            P(("member", "section", "dp")),
            P(("member", "section", "dp")),
            P(("member", "section", "dp")),
            P(("member", "section", "dp"), None),
            P(("member", "section", "dp"), None),
            P(("member", "section", "dp"), None),
        ),
        check_vma=False,
    )
```

```python
import functools
import math

import jax
import jax.numpy as jnp
from jax import lax
from jax.experimental import pallas as pl
from jax.experimental.pallas import tpu as pltpu
from jax.sharding import PartitionSpec as P

D = 768
HEADS = 12
HEAD = 64
ROT = 16
FF = 3072
STEP = 10
TILE = 384
PAIR = 2 * HEAD
QROWS = 256
CHUNK = 768
LSE_ROWS = 16

norm_eps = 1e-05
beta_first = 0.9
beta_second = 0.999
adam_eps = 1e-08
clip_limit = 1.0
embed_rate = 0.2
embed_decay = 0.01
vector_rate = 0.5
shampoo_rate = 0.1
stats_decay = 0.95
rope_base = 10000.0

f32 = jnp.float32
bf16 = jnp.bfloat16
VMEM_LIMIT = 60 * 2**20
LIGHT = pl.CostEstimate(flops=1, bytes_accessed=1, transcendentals=0)

COL_A, COL_O, COL_B, COL_H = 0, D, 2 * D, 3 * D
COL_QKV = 3 * D + FF
COL_GP = COL_QKV + 3 * D
COL_X = COL_GP + FF
KEPT = COL_X + D
COL_DP, COL_G, COL_DH = 0, 3 * D, 4 * D
GRADS = 4 * D + FF

V_G1, V_C1, V_G2, V_C2, V_QKV, V_O = 0, D, 2 * D, 3 * D, 4 * D, 7 * D
V_B1, V_B2, V_END = 8 * D, 8 * D + FF, 9 * D + FF


def block_places():
    places = []
    for matrix, (rows, cols) in enumerate(((D, 3 * D), (D, D), (D, FF), (FF, D))):
        for row in range(rows // TILE):
            for col in range(cols // TILE):
                places.append((matrix, row, col))
    return places


PLACES = block_places()


def nt(a, b):
    return lax.dot_general(a, b, (((1,), (1,)), ((), ())), preferred_element_type=f32)


def tn(a, b):
    return lax.dot_general(a, b, (((0,), (0,)), ((), ())), preferred_element_type=f32)


def nn(a, b):
    return lax.dot_general(a, b, (((1,), (0,)), ((), ())), preferred_element_type=f32)


def normalized(x):
    mean = jnp.mean(x, axis=-1, keepdims=True)
    centred = x - mean
    spread = jnp.mean(centred * centred, axis=-1, keepdims=True)
    scale = lax.rsqrt(spread + norm_eps)
    return centred * scale, scale


def norm_back(grad, gain, hat, scale):
    inner = grad * gain
    first = jnp.mean(inner, axis=-1, keepdims=True)
    second = jnp.mean(inner * hat, axis=-1, keepdims=True)
    return scale * (inner - first - hat * second)


def gelu_both(h):
    expo = jnp.exp(-0.5 * h * h)
    t = 1.0 / (1.0 + (0.3275911 * math.sqrt(0.5)) * jnp.abs(h))
    poly = 0.5 * 1.061405429
    for coef in (-1.453152027, 1.421413741, -0.284496736, 0.254829592):
        poly = poly * t + 0.5 * coef
    tail = poly * t * expo
    cdf = jnp.where(h >= 0.0, 1.0 - tail, tail)
    return h * cdf, cdf + h * expo * (1.0 / math.sqrt(2.0 * math.pi))


def head_masks(value):
    lane = lax.broadcasted_iota(jnp.int32, (1, PAIR), 1)
    return [
        jnp.where(lane < HEAD, value, 0.0).astype(bf16),
        jnp.where(lane < HEAD, 0.0, value).astype(bf16),
    ]


def arrivals(count):
    low = count // 2 - 1
    order = list(range(count - 1, low, -1)) + list(range(low))
    return [order[i : i + 2] for i in range(0, count - 1, 2)]


def shard_sources(count, is_high, direct):
    rounds = arrivals(count)
    own = count // 2 - 1
    sources = [None] * count
    for index, pair in enumerate(rounds):
        for side, shard in enumerate(pair):
            sources[shard] = index + (0 if direct == (side == 0) else len(rounds))
    sources[own] = 2 * len(rounds) + (0 if direct else 1)
    return sources[::-1] if is_high else sources


class Weights:
    def __init__(self, role, arrays, mats, sems):
        self.role = role
        count = len(PLACES) // arrays[0].shape[0]
        per = arrays[0].shape[0]
        self.copies = []
        for is_high in (False, True):
            for direct in (False, True):
                sources = shard_sources(count, is_high, direct)
                self.copies.append(
                    [
                        pltpu.make_async_copy(
                            arrays[sources[index // per]].at[index % per],
                            mats[matrix].at[pl.ds(row * TILE, TILE), pl.ds(col * TILE, TILE)],
                            sems.at[index],
                        )
                        for index, (matrix, row, col) in enumerate(PLACES)
                    ]
                )

    def start(self, *matrices):
        for role, copies in enumerate(self.copies):

            @pl.when(self.role == role)
            def _(copies=copies):
                for matrix in matrices:
                    for place, copy in zip(PLACES, copies):
                        if place[0] == matrix:
                            copy.start()

    def wait(self, matrix):
        for place, copy in zip(PLACES, self.copies[0]):
            if place[0] == matrix:
                copy.wait()


def forward_kernel(tick, units, *rest):
    meta_ref = rest[5]

    @pl.when(meta_ref[1 + tick] < units)
    def _():
        forward_body(tick, *rest)


def forward_body(tick, unit, part_count, shard_count, first, handed, *refs):
    meta_ref, order_ref, vec_ref, fin_ref, cos_ref, sa_ref, sb_ref = refs[:7]
    if handed:
        recv_ref, *refs = refs[7:]
    else:
        refs = refs[7:]
    parts, refs = refs[:part_count], refs[part_count:]
    shards = refs[:shard_count]
    rest = refs[shard_count + (0 if first else 3) :]
    xb_ref, red_ref, kept_out, xo_out, lse_out = rest[:5]
    wqkv, wo, w1, w2, kept, xo, lse, looked, wsem, isem, osem = rest[5:]
    mats = (wqkv, wo, w1, w2)
    length = xb_ref.shape[0]
    slot = meta_ref[1 + tick]
    weights = Weights(meta_ref[0], shards, mats, wsem)
    width = looked.shape[1]

    def assemble():
        copies = [
            pltpu.make_async_copy(part.at[:, pl.ds(unit * length, length)], looked.at[k], isem.at[k])
            for k, part in enumerate(parts)
        ]
        for copy in copies:
            copy.start()
        for copy in copies:
            copy.wait()
        found = jnp.zeros((length, D), f32)
        for k in range(part_count):
            found = found + tn(looked[k], order_ref[k * width : (k + 1) * width, :])
        kept[:, COL_X : COL_X + D] = found.astype(bf16)

    weights.start(0)
    if handed:
        is_high = meta_ref[0] >= 2

        @pl.when(is_high)
        def _():
            copy = pltpu.make_async_copy(recv_ref, kept.at[:, pl.ds(COL_X, D)], isem.at[0])
            copy.start()
            copy.wait()

        pl.when(jnp.logical_not(is_high))(assemble)
    else:
        assemble()
    inputs = kept[:, COL_X : COL_X + D]
    stores = []

    def store(index, start, width):
        copy = pltpu.make_async_copy(
            kept.at[:, pl.ds(start, width)],
            kept_out.at[slot, :, pl.ds(start, width)],
            osem.at[index],
        )
        copy.start()
        stores.append(copy)

    hat, _ = normalized(inputs.astype(f32))
    kept[:, COL_A : COL_A + D] = (hat * vec_ref[:, V_G1 : V_G1 + D] + vec_ref[:, V_C1 : V_C1 + D]).astype(bf16)
    kept[:, COL_B : COL_B + D] = (hat * vec_ref[:, V_G2 : V_G2 + D] + vec_ref[:, V_C2 : V_C2 + D]).astype(bf16)
    weights.wait(0)
    weights.start(1, 2, 3)
    for part in range(3):
        at = part * D
        proj = nn(kept[:, COL_A : COL_A + D], wqkv[:, at : at + D])
        proj = proj + vec_ref[:, V_QKV + at : V_QKV + at + D]
        if part == 2:
            kept[:, COL_QKV + at : COL_QKV + at + D] = proj.astype(bf16)
        else:
            for p in range(D // PAIR):
                u = proj[:, p * PAIR : (p + 1) * PAIR]
                turned = (
                    u * cos_ref[...]
                    + pltpu.roll(u, PAIR - ROT // 2, 1) * sa_ref[...]
                    + pltpu.roll(u, ROT // 2, 1) * sb_ref[...]
                )
                kept[:, COL_QKV + at + p * PAIR : COL_QKV + at + (p + 1) * PAIR] = turned.astype(bf16)
    store(0, COL_QKV, 3 * D)
    store(1, COL_X, D)
    lse[HEADS:LSE_ROWS, :] = jnp.zeros((LSE_ROWS - HEADS, length), f32)

    scales = head_masks(1.0 / math.sqrt(HEAD))
    lane = lax.broadcasted_iota(jnp.int32, (1, PAIR), 1)
    k_at = lax.broadcasted_iota(jnp.int32, (QROWS, QROWS), 0)
    q_at = lax.broadcasted_iota(jnp.int32, (QROWS, QROWS), 1)

    def attend(p, carry):
        lanes = pl.multiple_of(p * PAIR, PAIR)
        for tile in range(length // QROWS):
            rows = pl.ds(tile * QROWS, QROWS)
            keys = (tile + 1) * QROWS
            q = kept[rows, pl.ds(COL_QKV + lanes, PAIR)]
            k = kept[pl.ds(0, keys), pl.ds(COL_QKV + D + lanes, PAIR)]
            v = kept[pl.ds(0, keys), pl.ds(COL_QKV + 2 * D + lanes, PAIR)]
            outs = []
            for side in range(2):
                s = nt(k, q * scales[side])
                near = jnp.where(k_at <= q_at, s[keys - QROWS :, :], -1e30)
                s = jnp.concatenate([s[: keys - QROWS, :], near], axis=0) if tile else near
                peak = jnp.max(s, axis=0, keepdims=True)
                expo = jnp.exp(s - peak)
                total = jnp.sum(expo, axis=0, keepdims=True)
                soft = (expo * (1.0 / total)).astype(bf16)
                outs.append(tn(soft, v))
                lse[pl.ds(2 * p + side, 1), rows] = peak + jnp.log(total)
            mixed = jnp.where(lane < HEAD, outs[0], outs[1])
            kept[rows, pl.ds(COL_O + lanes, PAIR)] = mixed.astype(bf16)
        return carry

    lax.fori_loop(0, HEADS // 2, attend, 0)
    weights.wait(1)
    out = kept[:, COL_X : COL_X + D].astype(f32) + (nn(kept[:, COL_O : COL_O + D], wo[...]) + vec_ref[:, V_O : V_O + D])
    store(2, COL_A, 3 * D)
    weights.wait(2)
    weights.wait(3)
    branch = jnp.zeros((length, D), f32) + vec_ref[:, V_B2 : V_B2 + D]
    for c in range(0, FF, CHUNK):
        h = nn(kept[:, COL_B : COL_B + D], w1[:, c : c + CHUNK]) + vec_ref[:, V_B1 + c : V_B1 + c + CHUNK]
        act, slope = gelu_both(h)
        kept[:, COL_H + c : COL_H + c + CHUNK] = act.astype(bf16)
        kept[:, COL_GP + c : COL_GP + c + CHUNK] = slope.astype(bf16)
        branch = branch + nn(kept[:, COL_H + c : COL_H + c + CHUNK], w2[c : c + CHUNK, :])
        store(5 + 2 * (c // CHUNK), COL_H + c, CHUNK)
        store(6 + 2 * (c // CHUNK), COL_GP + c, CHUNK)
    out = out + branch
    xo[...] = out
    xb_ref[...] = out.astype(bf16)
    tails = [
        pltpu.make_async_copy(xo, xo_out.at[slot], osem.at[3]),
        pltpu.make_async_copy(lse, lse_out.at[slot], osem.at[4]),
    ]
    for copy in tails:
        copy.start()

    @pl.when(meta_ref[0] >= 2)
    def _():
        hat, _ = normalized(xo[...])
        final = (hat * fin_ref[:, :D] + fin_ref[:, D : 2 * D]).astype(bf16)
        red_ref[0:1, :] = jnp.sum(hat, axis=0, keepdims=True)
        red_ref[1:2, :] = jnp.sum(final.astype(f32), axis=0, keepdims=True)
        red_ref[2:8, :] = jnp.zeros((6, D), f32)

    for copy in stores + tails:
        copy.wait()


def forward(tick, meta, order, parts, unit, recv, vec, fin, tables, shards, state, slots):
    length = tables[0].shape[0]
    count = len(shards)
    first, handed = state is None, recv is not None
    whole = pl.BlockSpec(memory_space=pltpu.VMEM)
    anywhere = pl.BlockSpec(memory_space=pl.ANY)
    kept_shape = (
        jax.ShapeDtypeStruct((slots, length, KEPT), bf16),
        jax.ShapeDtypeStruct((slots, length, D), f32),
        jax.ShapeDtypeStruct((slots, LSE_ROWS, length), f32),
    )
    operands = [meta, order, vec, fin, *tables]
    if handed:
        operands.append(recv)
    operands += parts
    before = len(operands)
    operands = operands + [*shards] + ([] if first else list(state))
    return pl.pallas_call(
        functools.partial(forward_kernel, tick, slots, unit, len(parts), count, first, handed),
        out_shape=(
            jax.ShapeDtypeStruct((length, D), bf16),
            jax.ShapeDtypeStruct((8, D), f32),
            *kept_shape,
        ),
        in_specs=[pl.BlockSpec(memory_space=pltpu.SMEM)]
        + [whole] * 6
        + [anywhere] * (len(operands) - 7),
        out_specs=(whole, whole, anywhere, anywhere, anywhere),
        input_output_aliases={} if first else {before + count + i: 2 + i for i in range(3)},
        scratch_shapes=[
            pltpu.VMEM((D, 3 * D), bf16),
            pltpu.VMEM((D, D), bf16),
            pltpu.VMEM((D, FF), bf16),
            pltpu.VMEM((FF, D), bf16),
            pltpu.VMEM((length, KEPT), bf16),
            pltpu.VMEM((length, D), f32),
            pltpu.VMEM((LSE_ROWS, length), f32),
            pltpu.VMEM((len(parts), parts[0].shape[0], length), bf16),
            pltpu.SemaphoreType.DMA((len(PLACES),)),
            pltpu.SemaphoreType.DMA((len(parts),)),
            pltpu.SemaphoreType.DMA((5 + 2 * (FF // CHUNK),)),
        ],
        compiler_params=pltpu.CompilerParams(vmem_limit_bytes=VMEM_LIMIT),
        cost_estimate=pl.CostEstimate(flops=10 * 10**9, bytes_accessed=30 * 10**6, transcendentals=5 * 10**6),
        name="layer_forward",
    )(*operands)


def backward_kernel(tick, units, *rest):
    meta_ref = rest[4]

    @pl.when(meta_ref[1 + units + 2 + tick] < units)
    def _():
        backward_body(tick, units, *rest)


def backward_body(tick, units, shard_count, handed, back_in, back_out, *refs):
    meta_ref, flag_ref, order_ref, vec_ref, fin_ref, cos_ref, sa_ref, sb_ref = refs[:8]
    if handed:
        recv_ref, *refs = refs[8:]
    else:
        refs = refs[8:]
    shards = refs[:shard_count]
    kept_in, xo_in, lse_in = refs[shard_count : 3 + shard_count]
    rest = refs[3 + shard_count + back_in :]
    dx_ref, vg_ref, kept_out = rest[:3]
    backs, rest = rest[3 : 3 + back_out], rest[3 + back_out :]
    wqkv, wo, w1, w2, qkv, gp, x, xo, lse, grads, dmix, dq, dk, dv, turned, wsem, isem, osem, bsem = rest
    mats = (wqkv, wo, w1, w2)
    length = cos_ref.shape[0]
    slot = meta_ref[1 + units + 2 + tick]
    weights = Weights(meta_ref[0], shards, mats, wsem)
    loads = [
        pltpu.make_async_copy(xo_in.at[slot], xo, isem.at[0]),
        pltpu.make_async_copy(kept_in.at[slot, :, pl.ds(COL_GP, FF)], gp, isem.at[1]),
        pltpu.make_async_copy(kept_in.at[slot, :, pl.ds(COL_X, D)], x, isem.at[2]),
        pltpu.make_async_copy(kept_in.at[slot, :, pl.ds(COL_QKV, 3 * D)], qkv, isem.at[3]),
        pltpu.make_async_copy(lse_in.at[slot], lse, isem.at[4]),
    ]
    is_high = meta_ref[0] >= 2
    pl.when(is_high)(loads[0].start)
    weights.start(1)
    loads[3].start()
    loads[4].start()

    @pl.when(is_high)
    def _():
        loads[0].wait()
        hat, scale = normalized(xo[...])
        headed = fin_ref[:, 2 * D : 3 * D] * fin_ref[:, :D]
        xo[...] = flag_ref[min(tick, units - 1)] * norm_back(1.0, headed, hat, scale)

    if handed:

        @pl.when(jnp.logical_not(is_high))
        def _():
            xo[...] = recv_ref[...].astype(f32)

    grads[:, COL_G : COL_G + D] = xo[...].astype(bf16)
    bias = jnp.sum(grads[:, COL_G : COL_G + D].astype(f32), axis=0, keepdims=True)
    vg_ref[:, V_O : V_O + D] = bias
    vg_ref[:, V_B2 : V_B2 + D] = bias

    weights.wait(1)
    dmix[...] = nt(grads[:, COL_G : COL_G + D], wo[...]).astype(bf16)
    loads[3].wait()
    loads[4].wait()
    weights.start(3)
    loads[1].start()
    weights.start(2)
    loads[2].start()
    weights.start(0)
    scales = head_masks(1.0 / math.sqrt(HEAD))
    ones = head_masks(1.0)
    k_at = lax.broadcasted_iota(jnp.int32, (QROWS, QROWS), 0)
    q_at = lax.broadcasted_iota(jnp.int32, (QROWS, QROWS), 1)

    def attend(p, carry):
        lanes = pl.multiple_of(p * PAIR, PAIR)
        for tile in range(length // QROWS):
            rows = pl.ds(tile * QROWS, QROWS)
            keys = (tile + 1) * QROWS
            q = qkv[rows, pl.ds(lanes, PAIR)]
            k = qkv[pl.ds(0, keys), pl.ds(D + lanes, PAIR)]
            v = qkv[pl.ds(0, keys), pl.ds(2 * D + lanes, PAIR)]
            dm = dmix[rows, pl.ds(lanes, PAIR)]
            dq_sum = dk_sum = dv_sum = None
            for side in range(2):
                qs = q * scales[side]
                ks = k * scales[side]
                dms = dm * ones[side]
                s = nt(k, qs)
                soft = jnp.exp(s - lse[pl.ds(2 * p + side, 1), rows])
                near = jnp.where(k_at <= q_at, soft[keys - QROWS :, :], 0.0)
                soft = jnp.concatenate([soft[: keys - QROWS, :], near], axis=0) if tile else near
                dsoft = nt(v, dms)
                centre = jnp.sum(soft * dsoft, axis=0, keepdims=True)
                ds = (soft * (dsoft - centre)).astype(bf16)
                one_dv = nn(soft.astype(bf16), dms)
                one_dk = nn(ds, qs)
                one_dq = tn(ds, ks)
                if side:
                    dq_sum, dk_sum, dv_sum = dq_sum + one_dq, dk_sum + one_dk, dv_sum + one_dv
                else:
                    dq_sum, dk_sum, dv_sum = one_dq, one_dk, one_dv
            dq[rows, :] = dq_sum
            if tile:
                old = pl.ds(0, tile * QROWS)
                new = pl.ds(tile * QROWS, QROWS)
                dk[old, :] = dk[old, :] + dk_sum[: tile * QROWS]
                dk[new, :] = dk_sum[tile * QROWS :]
                dv[old, :] = dv[old, :] + dv_sum[: tile * QROWS]
                dv[new, :] = dv_sum[tile * QROWS :]
            else:
                dk[rows, :] = dk_sum
                dv[rows, :] = dv_sum
        for part, ref in ((0, dq), (1, dk)):
            g = ref[...]
            turned = (
                g * cos_ref[...]
                - pltpu.roll(g, PAIR - ROT // 2, 1) * sa_ref[...]
                - pltpu.roll(g, ROT // 2, 1) * sb_ref[...]
            )
            grads[:, pl.ds(COL_DP + part * D + lanes, PAIR)] = turned.astype(bf16)
        grads[:, pl.ds(COL_DP + 2 * D + lanes, PAIR)] = dv[...].astype(bf16)
        return carry

    lax.fori_loop(0, HEADS // 2, attend, 0)
    stores = [
        pltpu.make_async_copy(
            grads.at[:, pl.ds(COL_DP, 3 * D)], kept_out.at[slot, :, pl.ds(COL_QKV, 3 * D)], osem.at[2]
        )
    ]
    stores[0].start()
    weights.wait(3)
    loads[1].wait()
    loads[2].wait()
    weights.wait(2)
    second = jnp.zeros((length, D), f32)
    for c in range(0, FF, CHUNK):
        act = nt(grads[:, COL_G : COL_G + D], w2[c : c + CHUNK, :])
        pre = (act * gp[:, c : c + CHUNK].astype(f32)).astype(bf16)
        grads[:, COL_DH + c : COL_DH + c + CHUNK] = pre
        vg_ref[:, V_B1 + c : V_B1 + c + CHUNK] = jnp.sum(pre.astype(f32), axis=0, keepdims=True)
        second = second + nt(pre, w1[:, c : c + CHUNK])
    hat, scale = normalized(x[...].astype(f32))
    vg_ref[:, V_G2 : V_G2 + D] = jnp.sum(second * hat, axis=0, keepdims=True)
    vg_ref[:, V_C2 : V_C2 + D] = jnp.sum(second, axis=0, keepdims=True)
    xo[...] = xo[...] + norm_back(second, vec_ref[:, V_G2 : V_G2 + D], hat, scale)
    stores += [
        pltpu.make_async_copy(
            grads.at[:, pl.ds(COL_G, D)], kept_out.at[slot, :, pl.ds(COL_X, D)], osem.at[0]
        ),
        pltpu.make_async_copy(
            grads.at[:, pl.ds(COL_DH, FF)], kept_out.at[slot, :, pl.ds(COL_GP, FF)], osem.at[1]
        ),
    ]
    stores[1].start()
    stores[2].start()

    vg_ref[:, V_QKV : V_QKV + 3 * D] = jnp.sum(
        grads[:, COL_DP : COL_DP + 3 * D].astype(f32), axis=0, keepdims=True
    )
    weights.wait(0)
    one = nt(grads[:, COL_DP : COL_DP + 3 * D], wqkv[...])
    hat, scale = normalized(x[...].astype(f32))
    vg_ref[:, V_G1 : V_G1 + D] = jnp.sum(one * hat, axis=0, keepdims=True)
    vg_ref[:, V_C1 : V_C1 + D] = jnp.sum(one, axis=0, keepdims=True)
    total = xo[...] + norm_back(one, vec_ref[:, V_G1 : V_G1 + D], hat, scale)
    dx_ref[...] = total.astype(bf16)
    if back_out:

        @pl.when(jnp.logical_not(is_high))
        def _():
            turned[...] = nt(order_ref[...], dx_ref[...]).astype(bf16)
            start = (tick - 2) * length if tick <= units else 0
            width = backs[0].shape[0]
            copies = [
                pltpu.make_async_copy(
                    turned.at[pl.ds(k * width, width)], back.at[:, pl.ds(start, length)], bsem.at[k]
                )
                for k, back in enumerate(backs)
            ]
            for copy in copies:
                copy.start()
            for copy in copies:
                copy.wait()

    for copy in stores:
        copy.wait()


def backward(tick, units, meta, flags, order, recv, vec, fin, tables, shards, state, backs):
    length = tables[0].shape[0]
    count = len(shards)
    handed = recv is not None
    chips = len(PLACES) // shards[0].shape[0]
    spans = 0 if tick < 2 else (units - 1 if tick <= units else 1)
    back_shapes = [jax.ShapeDtypeStruct((D // chips, spans * length), bf16)] * (chips if spans else 0)
    whole = pl.BlockSpec(memory_space=pltpu.VMEM)
    anywhere = pl.BlockSpec(memory_space=pl.ANY)
    small = pl.BlockSpec(memory_space=pltpu.SMEM)
    operands = [meta, flags, order, vec, fin, *tables]
    if handed:
        operands.append(recv)
    dense = len(operands)
    operands = operands + [*shards, *state, *backs]
    aliases = {dense + count: 2} | {dense + count + 3 + i: 3 + i for i in range(len(backs))}
    return pl.pallas_call(
        functools.partial(backward_kernel, tick, units, count, handed, len(backs), len(back_shapes)),
        out_shape=(
            jax.ShapeDtypeStruct((length, D), bf16),
            jax.ShapeDtypeStruct((1, V_END), f32),
            jax.ShapeDtypeStruct(state[0].shape, bf16),
            *back_shapes,
        ),
        in_specs=[small, small] + [whole] * (dense - 2) + [anywhere] * (len(operands) - dense),
        out_specs=(whole, whole, anywhere) + (anywhere,) * len(back_shapes),
        input_output_aliases=aliases,
        scratch_shapes=[
            pltpu.VMEM((D, 3 * D), bf16),
            pltpu.VMEM((D, D), bf16),
            pltpu.VMEM((D, FF), bf16),
            pltpu.VMEM((FF, D), bf16),
            pltpu.VMEM((length, 3 * D), bf16),
            pltpu.VMEM((length, FF), bf16),
            pltpu.VMEM((length, D), bf16),
            pltpu.VMEM((length, D), f32),
            pltpu.VMEM((LSE_ROWS, length), f32),
            pltpu.VMEM((length, GRADS), bf16),
            pltpu.VMEM((length, D), bf16),
            pltpu.VMEM((length, PAIR), f32),
            pltpu.VMEM((length, PAIR), f32),
            pltpu.VMEM((length, PAIR), f32),
            pltpu.VMEM((D, length), bf16),
            pltpu.SemaphoreType.DMA((len(PLACES),)),
            pltpu.SemaphoreType.DMA((5,)),
            pltpu.SemaphoreType.DMA((3,)),
            pltpu.SemaphoreType.DMA((chips,)),
        ],
        compiler_params=pltpu.CompilerParams(vmem_limit_bytes=VMEM_LIMIT),
        cost_estimate=pl.CostEstimate(flops=20 * 10**9, bytes_accessed=40 * 10**6, transcendentals=5 * 10**6),
        name="layer_backward",
    )(*operands)


def product_kernel(shards, start, tiles, x_ref, y_ref, *refs):
    sent_ref = refs[0] if len(refs) > 2 else None
    turned = refs[-1]
    units, rows, width = x_ref.shape
    step = pl.program_id(0)
    steps = pl.num_programs(0)
    before = tiles[start + jnp.maximum(step - 1, 0)]

    @pl.when(jnp.logical_or(step == 0, tiles[start + step] != before))
    def _():
        for unit in range(units):
            turned[:, unit * rows : (unit + 1) * rows] = jnp.transpose(x_ref[unit])

    found = nn(turned[...], y_ref[...].reshape(units * rows, -1))
    if sent_ref is None:
        out_ref = refs[0]
        for i in range(out_ref.shape[0]):
            out_ref[i] = found[:, i * TILE : (i + 1) * TILE].astype(bf16)
        return
    square_ref, *out_refs = refs[1:-1]

    @pl.when(step == 0)
    def _():
        square_ref[...] = jnp.zeros_like(square_ref)

    each = sent_ref.shape[0]
    blocks = []
    for i in range(each):
        whole = found[:, i * TILE : (i + 1) * TILE] + sent_ref[i].astype(f32)
        blocks.append(whole.astype(bf16))
        counts = tiles[start + 2 * steps + step * each + i] > 0
        square_ref[...] += jnp.sum(jnp.where(counts, whole * whole, 0.0), axis=0, keepdims=True)
    per = steps // shards
    for shard, out_ref in enumerate(out_refs):

        @pl.when(step // per == shard)
        def _(out_ref=out_ref):
            for i in range(each):
                out_ref[i] = blocks[i]


def product_tiles(count, each):
    total = len(PLACES) // count
    part = (total + 1) // 2
    rest = total - part
    group = max(count // 2, 1)
    left = [(0, 2, 4, 6)[m] + row for m, row, _ in PLACES]
    right = [((14, 28, 20, 28)[m] + col) // each for m, _, col in PLACES]
    found = []
    for is_high in range(2):
        for core in range(2):
            row = []
            for start in range(0, count, group):
                shards = [shard_order(count, is_high)[step] for step in range(start, start + group)]
                for half in (1 - core, core):
                    places = [k * total + half * rest + i for k in shards for i in range(part)]
                    row += [left[b] for b in places[::each]] + [right[b] for b in places[::each]]
                    row += [0 if half == 1 and i < part - rest else 1 for _ in shards for i in range(part)]
            found.append(row)
    found.append([0] * len(found[0]))
    return found


def shard_order(count, is_high):
    low = count // 2 - 1
    order = list(range(count - 1, low, -1)) + list(range(low + 1))
    return [count - 1 - k for k in order] if is_high else order


def products(shards, tiles, call, kept, units, each, sent=None):
    part = (len(PLACES) // (2 * shards) + 1) // 2
    steps = shards * part // each
    start = call * (2 * steps + shards * part)
    per = steps // shards
    length = kept.shape[1]
    block = pl.BlockSpec((each, TILE, TILE), lambda i, t: (i, 0, 0))
    if sent is None:
        out_shape, out_specs, more = jax.ShapeDtypeStruct((steps * each, TILE, TILE), bf16), block, []
    else:
        out_shape = (jax.ShapeDtypeStruct((1, TILE), f32),)
        out_shape += (jax.ShapeDtypeStruct((per * each, TILE, TILE), bf16),) * shards
        out_specs = (pl.BlockSpec((1, TILE), lambda i, t: (0, 0)),)
        for shard in range(shards):
            out_specs += (
                pl.BlockSpec(
                    (each, TILE, TILE),
                    lambda i, t, first=shard * per: (jnp.clip(i - first, 0, per - 1), 0, 0),
                ),
            )
        more = [sent]
    return pl.pallas_call(
        functools.partial(product_kernel, shards, start),
        out_shape=out_shape,
        grid_spec=pltpu.PrefetchScalarGridSpec(
            num_scalar_prefetch=1,
            grid=(steps,),
            in_specs=[
                pl.BlockSpec((units, length, TILE), lambda i, t: (0, 0, t[start + i])),
                pl.BlockSpec((units, length, each * TILE), lambda i, t: (0, 0, t[start + steps + i])),
            ]
            + [block] * len(more),
            out_specs=out_specs,
            scratch_shapes=[pltpu.VMEM((TILE, units * length), bf16)],
        ),
        compiler_params=pltpu.CompilerParams(vmem_limit_bytes=VMEM_LIMIT),
        cost_estimate=LIGHT,
        name="weight_products",
    )(tiles, kept, kept, *more)


def lookup_kernel(ids_ref, embedding_ref, first_ref, rest_ref, table, wide):
    step = pl.program_id(0)
    features = embedding_ref.shape[0]
    lanes = table.shape[1]
    tiles = embedding_ref.shape[1] // lanes
    tokens = wide.shape[0]

    def turn(i):
        tile = embedding_ref[:, pl.ds(pl.multiple_of(i * lanes, lanes), lanes)]
        table[pl.ds(pl.multiple_of((step * tiles + i) * lanes, lanes), lanes), :features] = jnp.transpose(tile)

    def several(i, carry):
        for j in range(8):
            turn(i * 8 + j)
        return carry

    lax.fori_loop(0, tiles // 8, several, 0)
    for i in range(tiles // 8 * 8, tiles):
        turn(i)

    @pl.when(step == pl.num_programs(0) - 1)
    def _():
        def fetch(i, carry):
            for j in range(16):
                wide[pl.ds(i * 16 + j, 1), :] = table[pl.ds(ids_ref[i * 16 + j], 1), :]
            return carry

        lax.fori_loop(0, tokens // 16, fetch, 0)
        start = 0
        for ref in (first_ref, rest_ref):

            def flat(i, carry, ref=ref, start=start):
                rows = wide[pl.ds(pl.multiple_of(start + i * lanes, lanes), lanes), :]
                ref[:, pl.ds(pl.multiple_of(i * lanes, lanes), lanes)] = jnp.transpose(rows)[:features].astype(bf16)
                return carry

            lax.fori_loop(0, ref.shape[1] // lanes, flat, 0)
            start += ref.shape[1]


def lookup(ids, embedding, first):
    features, vocab = embedding.shape
    tokens = ids.shape[0]
    lanes = 128
    steps = 3 if vocab % (3 * lanes) == 0 else 1
    whole = lambda i: (0, 0)
    return pl.pallas_call(
        lookup_kernel,
        out_shape=(
            jax.ShapeDtypeStruct((features, first), bf16),
            jax.ShapeDtypeStruct((features, tokens - first), bf16),
        ),
        grid=(steps,),
        in_specs=[
            pl.BlockSpec(memory_space=pltpu.SMEM),
            pl.BlockSpec((features, vocab // steps), lambda i: (0, i)),
        ],
        out_specs=(
            pl.BlockSpec((features, first), whole),
            pl.BlockSpec((features, tokens - first), whole),
        ),
        scratch_shapes=[pltpu.VMEM((vocab, lanes), f32), pltpu.VMEM((tokens, lanes), f32)],
        compiler_params=pltpu.CompilerParams(vmem_limit_bytes=VMEM_LIMIT),
        cost_estimate=LIGHT,
        name="table_lookup",
    )(ids, embedding)


def table_kernel(ids_ref, *refs):
    *parts, vectors_ref, first_ref, second_ref = refs[:-5]
    out_ref, square_ref, table, wide, total = refs[-5:]
    step = pl.program_id(0)
    features = out_ref.shape[0]
    tokens = wide.shape[0]
    vocab, lanes = table.shape
    tiles = out_ref.shape[1] // lanes

    @pl.when(step == 0)
    def _():
        def clear(i, carry):
            table[pl.ds(pl.multiple_of(i * 3 * lanes, lanes), 3 * lanes), :] = jnp.zeros((3 * lanes, lanes), f32)
            return carry

        lax.fori_loop(0, vocab // (3 * lanes), clear, 0)
        total[...] = jnp.zeros_like(total)
        if features < lanes:
            wide[:, features:] = jnp.zeros((tokens, lanes - features), f32)
        start = 0
        for part in parts:

            def upright(i, carry, part=part, start=start):
                tile = part[:, pl.ds(pl.multiple_of(i * lanes, lanes), lanes)].astype(f32)
                wide[pl.ds(pl.multiple_of(start + i * lanes, lanes), lanes), :features] = jnp.transpose(tile)
                return carry

            lax.fori_loop(0, part.shape[1] // lanes, upright, 0)
            start += part.shape[1]

        def add(i, carry):
            for j in range(16):
                row = pl.ds(ids_ref[i * 16 + j], 1)
                table[row, :] = table[row, :] + wide[pl.ds(i * 16 + j, 1), :]
            return carry

        lax.fori_loop(0, tokens // 16, add, 0)

    def turn(i):
        tile = table[pl.ds(pl.multiple_of((step * tiles + i) * lanes, lanes), lanes), :]
        total[...] += tile * tile
        out_ref[:, pl.ds(pl.multiple_of(i * lanes, lanes), lanes)] = jnp.transpose(tile)[:features]

    def several(i, carry):
        for j in range(8):
            turn(i * 8 + j)
        return carry

    lax.fori_loop(0, tiles // 8, several, 0)
    for i in range(tiles // 8 * 8, tiles):
        turn(i)

    @pl.when(step == pl.num_programs(0) - 1)
    def _():
        lanes_sum = jnp.sum(total[...], axis=0, keepdims=True)
        others = jnp.sum(first_ref[...] + second_ref[...], axis=1, keepdims=True)
        vectors = vectors_ref[...]
        others = others + 0.5 * jnp.sum(vectors * vectors, axis=1, keepdims=True)
        square_ref[...] = jnp.sum(lanes_sum, axis=1, keepdims=True) + others


def table_gradient(ids, parts, vocab, vectors, first, second):
    tokens, features = ids.shape[0], parts[0].shape[0]
    lanes = 128
    steps = 3 if vocab % (3 * lanes) == 0 else 1
    return pl.pallas_call(
        table_kernel,
        out_shape=(jax.ShapeDtypeStruct((features, vocab), f32), jax.ShapeDtypeStruct((1, 1), f32)),
        grid=(steps,),
        in_specs=[
            pl.BlockSpec(memory_space=pltpu.SMEM),
        ]
        + [
            pl.BlockSpec(part.shape, lambda i: (0, 0), pipeline_mode=pl.Buffered(1))
            for part in (*parts, vectors, first, second)
        ],
        out_specs=(
            pl.BlockSpec((features, vocab // steps), lambda i: (0, i)),
            pl.BlockSpec((1, 1), lambda i: (0, 0)),
        ),
        scratch_shapes=[
            pltpu.VMEM((vocab, lanes), f32),
            pltpu.VMEM((tokens, lanes), f32),
            pltpu.VMEM((lanes, lanes), f32),
        ],
        compiler_params=pltpu.CompilerParams(vmem_limit_bytes=VMEM_LIMIT),
        cost_estimate=LIGHT,
        name="table_gradient",
    )(ids, *parts, vectors, first, second)


def split(value):
    high = value.astype(bf16)
    return high, (value - high.astype(f32)).astype(bf16)


def shampoo_kernel(factor_ref, g_ref, w_ref, ls_ref, rs_ref, lr_ref, rr_ref, bg_ref, nw_ref, nl_ref, nr_ref):
    factor = factor_ref[0]
    level = (1.0 - stats_decay) * factor * factor
    for i in range(g_ref.shape[0]):
        g = g_ref[i]
        bg_ref[i] = g.astype(f32) * factor
        nl_ref[i] = stats_decay * ls_ref[i] + level * nt(g, g)
        nr_ref[i] = stats_decay * rs_ref[i] + level * tn(g, g)
        right_high, right_low = split(rr_ref[i])
        inner = nn(g, right_high) + nn(g, right_low)
        inner_high, inner_low = split(inner)
        left_high, left_low = split(lr_ref[i])
        direction = nn(left_high, inner_high) + (nn(left_high, inner_low) + nn(left_low, inner_high))
        nw_ref[i] = w_ref[i] - (shampoo_rate * factor) * direction


def shampoo(factor, grad, weights, left_stats, right_stats, left_root, right_root):
    count = grad.shape[0]
    each = max(i for i in (1, 2, 3) if count % i == 0)
    block = pl.BlockSpec((each, TILE, TILE), lambda i: (i, 0, 0))
    shape = jax.ShapeDtypeStruct((count, TILE, TILE), f32)
    return pl.pallas_call(
        shampoo_kernel,
        out_shape=(shape,) * 4,
        grid=(count // each,),
        in_specs=[pl.BlockSpec(memory_space=pltpu.SMEM)] + [block] * 6,
        out_specs=(block,) * 4,
        compiler_params=pltpu.CompilerParams(vmem_limit_bytes=VMEM_LIMIT),
        cost_estimate=LIGHT,
        name="shampoo",
    )(factor, grad, weights, left_stats, right_stats, left_root, right_root)


def rope_columns(length):
    half_rot = ROT // 2
    lanes = jnp.arange(PAIR) % HEAD
    index = jnp.where(lanes < half_rot, lanes, lanes - half_rot).astype(f32)
    inverse = rope_base ** (-2.0 * index / ROT)
    angles = jnp.arange(length)[:, None].astype(f32) * inverse[None, :]
    cosine = jnp.where(lanes < ROT, jnp.cos(angles), 1.0)
    sine = jnp.where(lanes < ROT, jnp.sin(angles), 0.0)
    first = jnp.where(lanes < half_rot, -sine, 0.0)
    second = jnp.where(lanes < half_rot, 0.0, sine)
    return cosine, first, second


def adam_step(weight, moment, second, grad, rate, decay):
    moment_new = beta_first * moment + (1.0 - beta_first) * grad
    second_new = beta_second * second + (1.0 - beta_second) * grad * grad
    corrected = moment_new / (1.0 - beta_first**STEP)
    scaled = jnp.sqrt(second_new / (1.0 - beta_second**STEP)) + adam_eps
    return (moment_new, second_new, weight - rate * (corrected / scaled + decay * weight))


def rounded(values):
    return lax.reduce_precision(values, 8, 7)


def chosen(flags, values):
    total = values[-1]
    for flag, value in zip(flags[:-1], values[:-1]):
        total = jnp.where(flag, value, total)
    return total


def ordered(section, mine, other, axis):
    return jnp.concatenate(
        [jnp.where(section == 0, mine, other), jnp.where(section == 0, other, mine)], axis=axis
    )


def swapped(value):
    return lax.ppermute(value, "section", [(0, 1), (1, 0)])


def local(
    tokens,
    margins,
    tie_flags,
    embedding,
    embed_moment,
    embed_second,
    layer_blocks,
    left_stats,
    right_stats,
    left_root,
    right_root,
    layer_vectors,
    vector_moment,
    vector_second,
    closing_vectors,
    final_moment,
    final_second,
):
    both = ("section", "dp")
    count = lax.axis_size("dp")
    section = lax.axis_index("section")
    place = lax.axis_index("dp")
    low, high = count // 2 - 1, count // 2
    is_high = place >= high
    order_low, order_high = shard_order(count, False), shard_order(count, True)
    length = tokens.shape[2]
    units = tokens.shape[0] * count
    own_blocks = layer_blocks.shape[1]
    own_vector = layer_vectors.shape[1]
    own_final = closing_vectors.shape[0]
    features, vocab = embedding.shape

    own_closing = rounded(closing_vectors)
    pack = jnp.concatenate(
        [
            tokens.reshape(-1).astype(f32),
            margins.astype(f32),
            tie_flags.astype(f32),
            rounded(layer_vectors[0]),
            own_closing,
        ]
    )
    passed = [pack] + [
        lax.ppermute(pack, "dp", [(i, (i + d) % count) for i in range(count)]) for d in range(1, count)
    ]
    packs = jnp.stack(passed)

    own, packs = lax.optimization_barrier((layer_blocks[0].astype(bf16), packs))
    rounds = arrivals(count)
    received = []
    for pair in rounds:
        route = []
        for side, shard in enumerate(pair):
            route.append((shard, side * count + low))
            route.append((count + count - 1 - shard, (1 - side) * count + high))
        received.append(lax.ppermute(own, both, route))

    packs = packs[(place - jnp.arange(count)) % count]
    at = tokens.size
    ids = packs[:, :at].astype(jnp.int32).reshape(2, units, length)
    pair_margins = packs[:, at : at + margins.size].reshape(-1)
    at = at + margins.size
    pair_ties = packs[:, at : at + margins.size].reshape(-1)
    at = at + margins.size
    other_packs = swapped(packs[:, at:])
    layer_packs = jnp.where((section == 1) == is_high, packs[:, at:], other_packs)
    vec = layer_packs[:, :own_vector].reshape(1, -1)
    fin = ordered(section, packs[:, at + own_vector :], other_packs[:, own_vector:], 0).reshape(1, -1)
    tables = rope_columns(length)

    ids_here = jnp.where(section == 0, ids, ids[::-1])
    looked = lookup(
        jnp.concatenate([ids_here[:, :1].reshape(-1), ids_here[:, 1:].reshape(-1)]), embedding, 2 * length
    )

    def joined(columns):
        half = columns.shape[1] // 2
        return ordered(section, columns[:, :half], swapped(columns[:, half:]), 0)

    def sent_on(columns):
        return [columns if k == low else lax.ppermute(columns, "dp", [(k, low)]) for k in range(count)]

    looked = [joined(columns) for columns in looked]
    first = sent_on(looked[0])
    slot_at = jnp.arange(D)
    chip, within = slot_at // (2 * features), slot_at % (2 * features)
    feature_at = within // features * (D // 2) + chip * features + within % features
    order = (feature_at[:, None] == jnp.arange(D)[None, :]).astype(bf16)
    part = (own_blocks + 1) // 2
    each = 2 if own_blocks % 4 == 0 else 1
    group = max(count // 2, 1)
    tiles = lax.dynamic_index_in_dim(
        jnp.array(product_tiles(count, each), jnp.int32),
        jnp.where((place == low) | (place == high), is_high * 2 + section, 4),
        0,
        False,
    )

    first, later, received, vec, fin, tables, order, tiles = lax.optimization_barrier(
        (first, looked[1], received, vec, fin, tables, order, tiles)
    )
    relays = [
        lax.ppermute(
            array, both, [(low, count + low), (count + low, low), (high, count + high), (count + high, high)]
        )
        for array in [own, *received]
    ]
    later, relays[-1] = lax.optimization_barrier((later, relays[-1]))
    later = sent_on(later)
    shards = [*received, *relays[1:], own, relays[0]]
    role = is_high * 2 + ((section == 1) == is_high) * 1

    live_low, live_high = place == low, place == high
    early = [*range(units), units, units]
    late = [units, units, *range(units)]
    meta = jnp.where(live_high, jnp.array([0, *late, *early]), jnp.array([0, *early, *late]))
    meta = jnp.where(live_low | live_high, meta, units).at[0].set(role).astype(jnp.int32)
    state = None
    arrived = []
    sums = []
    for tick in range(units + 2):
        unit = min(tick, units - 1)
        result, tail, *state = forward(
            tick,
            meta,
            order,
            later if unit else first,
            max(unit - 1, 0),
            arrived[tick - 2] if tick >= 2 else None,
            vec,
            fin,
            tables,
            shards,
            state,
            units,
        )
        if tick < units:
            arrived.append(lax.ppermute(result, "dp", [(low, high)]))
        if tick >= 2:
            sums.append(tail[:2])
    sums = jnp.stack(sums)
    sum_hat, sum_final = sums[:, 0], sums[:, 1]
    final_gain, head = fin[0, :D], fin[0, 2 * D :]
    rewards = (jnp.sum(sum_final * head, axis=1) / length).reshape(-1, 2)
    pairs = units // 2
    gap = rewards[:, 0] - rewards[:, 1]
    half_margin = 0.5 * lax.dynamic_slice_in_dim(pair_margins, section * pairs, pairs, 0)
    tie = lax.dynamic_slice_in_dim(pair_ties, section * pairs, pairs, 0)
    pair_loss = (1.0 - tie) * jax.nn.softplus(half_margin - gap) + tie * 0.5 * (
        jax.nn.softplus(gap) + jax.nn.softplus(-gap)
    )
    gap_grad = -(1.0 - tie) * jax.nn.sigmoid(half_margin - gap) + tie * 0.5 * (
        jax.nn.sigmoid(gap) - jax.nn.sigmoid(-gap)
    )
    reward_grad = (jnp.stack([gap_grad, -gap_grad], axis=1) / length).reshape(-1)
    final_local = jnp.concatenate(
        [
            head * jnp.sum(reward_grad[:, None] * sum_hat, axis=0),
            head * (length * jnp.sum(reward_grad)),
            jnp.sum(reward_grad[:, None] * sum_final, axis=0),
        ]
    )

    def returned(parts):
        return [part if k == low else lax.ppermute(part, "dp", [(low, k)]) for k, part in enumerate(parts)]

    def own_features(parts):
        both_cores = chosen([place == k for k in range(count)], parts)
        mine, other = both_cores[:features], both_cores[features:]
        return [jnp.where(section == 0, mine, other), swapped(jnp.where(section == 0, other, mine))]

    arrived = []
    vector_sum = jnp.zeros((1, V_END), f32)
    backs = []
    token_grads = []
    for tick in range(units + 2):
        if tick == units + 1:
            token_grads.append(returned(backs))
            backs = []
        grad_in, vector_part, state[0], *backs = backward(
            tick,
            units,
            meta,
            reward_grad,
            order,
            arrived[tick - 2] if tick >= 2 else None,
            vec,
            fin,
            tables,
            shards,
            state,
            backs,
        )
        if tick < units:
            arrived.append(lax.ppermute(grad_in, "dp", [(high, low)]))
        vector_sum = vector_sum + jnp.where(meta[1 + units + 2 + tick] < units, vector_part, 0.0)
    token_grads.append(returned(backs))

    vector_pack = jnp.concatenate([vector_sum[0], jnp.where(live_high, final_local, 0.0)])
    vector_pack = vector_pack + swapped(vector_pack)

    def to_owner(value, step):
        route = [
            (core * count + source, core * count + target)
            for core in range(2)
            for source, target in ((low, order_low[step]), (high, order_high[step]))
        ]
        return lax.ppermute(value, both, route) if step < count - 1 else value

    token_grads[0], tiles = lax.optimization_barrier((token_grads[0], tiles))
    kept = state[0]
    block_squares = []
    ids_ordered = jnp.concatenate(
        [ids_here[0, :-1], ids_here[1, :-1], ids_here[0, -1:], ids_here[1, -1:]], axis=0
    ).reshape(-1)
    sent, pieces = [], []
    for index in range(count // group):
        sums = products(group, tiles, 2 * index, kept, units, each)
        if index == 0:
            token_grads[1], sums = lax.optimization_barrier((token_grads[1], sums))
            vectors = [to_owner(vector_pack, step) for step in range(count)]
            token_parts = own_features(token_grads[0]) + own_features(token_grads[1])
        else:
            vectors, token_parts, sums = lax.optimization_barrier((vectors, token_parts, sums))
        tiles, sums = lax.optimization_barrier((tiles, sums))
        sent.append(swapped(sums))
    for index in range(count // group):
        square, *found = products(group, tiles, 2 * index + 1, kept, units, each, sent[index])
        block_squares.append(square)
        tiles, found = lax.optimization_barrier((tiles, found))
        if index + 1 < count // group:
            found = [to_owner(piece, index * group + i) for i, piece in enumerate(found)]
        pieces += found
    token_parts, pieces[-1] = lax.optimization_barrier((token_parts, pieces[-1]))
    table_grad, squares = table_gradient(
        ids_ordered,
        token_parts,
        vocab,
        vector_pack[None],
        *block_squares,
    )

    squares, pieces[: count - group], vectors = lax.optimization_barrier((squares, pieces[: count - group], vectors))
    loss = jnp.where(place == high, jnp.sum(pair_loss), 0.0)
    square_total, loss_total = lax.psum((squares, loss), both)
    norm_value = jnp.sqrt(square_total[0, 0])
    factor = clip_limit / jnp.maximum(norm_value, clip_limit)
    pieces[count - group :], factor = lax.optimization_barrier((pieces[count - group :], factor))
    pieces[count - group :] = [to_owner(pieces[step], step) for step in range(count - group, count)]
    embed_m, embed_v, embed_w = adam_step(
        embedding, embed_moment, embed_second, table_grad * factor, embed_rate, embed_decay
    )
    pieces, embed_w = lax.optimization_barrier((pieces, embed_w))
    from_low = [place == k for k in order_low]
    from_high = [place == k for k in order_high]
    piece_low, piece_high = chosen(from_low, pieces), chosen(from_high, pieces)
    mine = jnp.where(section == 0, piece_low, piece_high)
    other = swapped(jnp.where(section == 0, piece_high, piece_low))
    grad_blocks = jnp.concatenate(
        [jnp.where(section == 0, mine, other), jnp.where(section == 0, other, mine)[2 * part - own_blocks :]],
        axis=0,
    )
    vectors_high = chosen(from_high, vectors)
    owned_vector = lax.dynamic_slice_in_dim(
        jnp.where(section == 0, chosen(from_low, vectors), vectors_high), place * own_vector, own_vector, 0
    )[None]
    owned_final = lax.dynamic_slice_in_dim(
        vectors_high, V_END + (section * count + place) * own_final, own_final, 0
    )

    block_grad, new_blocks, new_left, new_right = (
        out[None]
        for out in shampoo(
            factor.reshape(1),
            grad_blocks,
            layer_blocks[0],
            left_stats[0],
            right_stats[0],
            left_root[0],
            right_root[0],
        )
    )
    vector_m, vector_v, vector_w = adam_step(
        layer_vectors, vector_moment, vector_second, owned_vector * factor, vector_rate, 0.0
    )
    final_m, final_v, final_w = adam_step(
        closing_vectors, final_moment, final_second, owned_final * factor, vector_rate, 0.0
    )
    return (
        loss_total.reshape(1),
        norm_value.reshape(1),
        block_grad,
        new_blocks,
        new_left,
        new_right,
        vector_m,
        vector_v,
        vector_w,
        final_m,
        final_v,
        final_w,
        embed_m,
        embed_v,
        embed_w,
    )


def solution(mesh):
    return jax.shard_map(
        local,
        mesh=mesh,
        in_specs=(
            P(("member", "dp"), None, None),
            P(("member", "dp")),
            P(("member", "dp")),
            P(("member", "section", "dp"), None),
            P(("member", "section", "dp"), None),
            P(("member", "section", "dp"), None),
            P(("member", "section"), "dp", None, None),
            P(("member", "section"), "dp", None, None),
            P(("member", "section"), "dp", None, None),
            P(("member", "section"), "dp", None, None),
            P(("member", "section"), "dp", None, None),
            P(("member", "section"), "dp"),
            P(("member", "section"), "dp"),
            P(("member", "section"), "dp"),
            P(("member", "section", "dp")),
            P(("member", "section", "dp")),
            P(("member", "section", "dp")),
        ),
        out_specs=(
            P("member"),
            P("member"),
            P(("member", "section"), "dp", None, None),
            P(("member", "section"), "dp", None, None),
            P(("member", "section"), "dp", None, None),
            P(("member", "section"), "dp", None, None),
            P(("member", "section"), "dp"),
            P(("member", "section"), "dp"),
            P(("member", "section"), "dp"),
            P(("member", "section", "dp")),
            P(("member", "section", "dp")),
            P(("member", "section", "dp")),
            P(("member", "section", "dp"), None),
            P(("member", "section", "dp"), None),
            P(("member", "section", "dp"), None),
        ),
        check_vma=False,
    )
```
